256 devices in a mesh: nodes: 128 (over y, z, x), rep: 2 (over core).
Axes of the slice: x: 4, y: 4, z: 8, core: 2. Of those that a mesh axis runs over, the one named last changes fastest.
Arguments:
- features: bfloat16 [131072, 128], P('nodes'), may hold values from -6 to 6
- weight: bfloat16 [128, 256], replicated, may hold values from -0.5 to 0.5
- out_bias: float32 [256], replicated, may hold values from -3 to 3
- edge_tiles: bfloat16 [16384, 128, 128], P(('nodes', 'rep')), may hold values from -0.125 to 0.125
- block_row: int32 [16384], P(('nodes', 'rep')), may hold values from 0 to 1023, as said below
- tile_slot: int32 [16384], P(('nodes', 'rep')), may hold values from 0 to 255, as said below
- send_list: int32 [32768, 2], P(('nodes', 'rep')), may hold values from 0 to 7, as said below
- out_grad: bfloat16 [131072, 256], P('nodes'), may hold values from -6 to 6
Outputs:
- activations: bfloat16 [131072, 256], P('nodes', 'rep')
- feature_grad: float32 [131072, 128], P(('nodes', 'rep'))
- weight_grad: float32 [128, 256], P(None, 'rep')
- bias_grad: float32 [256], P('rep')
The draws below stay inside these ranges and needn't reach their ends.
Inputs may be any that keep to these rules, and one draw needn't show every extreme that they name: `block_row`: an adjacency block of the device at nodes index r lies in block rows r * 8 to r * 8 + 7. `tile_slot`: slot s * 2 + c names the c-th block that nodes index s sends to this device's nodes index, as send_list states. `send_list`: row (s * 2 + q) * 128 + r lists the local block numbers that nodes index s sends to nodes index r, both at rep index q; the 2 numbers of a row differ.
All inputs are finite; a program needn't handle non-finite values.
Results may differ from the reference program's by a relative error of at most 0.012.
Values may be sent and summed in bfloat16 or wider, within the bound.
No kernel may reach another device: no remote copies, remote signals or barrier semaphores. Data moves between devices by JAX's collectives and lax.ppermute only.
A program may use at most 128 MiB of HBM per device.

```python
import math
import jax
import jax.numpy as jnp
from jax import lax

BLK = 128
FIN = 128
FOUT = 256
NBD = 8
DEG = 16
CAP = 2
TPD = 64
TILES = 16384
NBLK = 1024
NODES = 131072
N_NODES = 128
N_REP = 2


def draw_block_row(key, part):
    key = jax.random.fold_in(key, 11)
    tile_index = jnp.arange(TPD * N_NODES * N_REP, dtype=jnp.int32)
    nodes_index = tile_index // (TPD * N_REP)
    offset = jax.random.randint(key, (TPD * N_NODES * N_REP,), 0, NBD, dtype=jnp.int32)
    return nodes_index * NBD + offset


def device_slots(key):
    first_key, perm_key = jax.random.split(key)
    owner_index = jax.random.randint(first_key, (), 0, N_NODES, dtype=jnp.int32)
    ordering = jax.random.permutation(perm_key, N_NODES * CAP).astype(jnp.int32)
    position = jnp.arange(TPD, dtype=jnp.int32)
    spread = ordering[position % (N_NODES * CAP)]
    return jnp.where(position < CAP, owner_index * CAP + position, spread)


def draw_tile_slot(key, part):
    key = jax.random.fold_in(key, 23)
    device_keys = jax.random.split(key, N_NODES * N_REP)
    return jax.vmap(device_slots)(device_keys).reshape(-1)


def draw_send_list(key, part):
    key = jax.random.fold_in(key, 37)
    base_key, jitter_key = jax.random.split(key)
    rows_total = N_NODES * N_REP * N_NODES
    spacing = NBD // CAP
    base_block = jax.random.randint(base_key, (rows_total, 1), 0, NBD, dtype=jnp.int32)
    jitter = jax.random.randint(jitter_key, (rows_total, CAP), 0, spacing, dtype=jnp.int32)
    stride = jnp.arange(CAP, dtype=jnp.int32)[None, :] * spacing
    return (base_block + stride + jitter) % NBD


def steps_of(rng, extent, shards, least, top_value):
    level, own = 1.0, jax.random.fold_in(rng, 6)
    for dim, shards_of in shards:
        heights = jnp.exp(jax.random.uniform(jax.random.fold_in(own, dim), (shards_of,), jnp.float32, least / len(shards), top_value / len(shards)))
        level = level * jnp.repeat(heights, extent[dim] // shards_of).reshape([-1 if axis == dim else 1 for axis in range(len(extent))])
    return level


def noise(rng, extent, deviation, most, shards=(), kind=jnp.bfloat16):
    result = deviation * jax.random.normal(rng, extent, jnp.float32)
    if shards:
        result = result * steps_of(rng, extent, shards, -0.22, 0.18)
    return jnp.clip(result, -most, most).astype(kind)


def setup_inputs(seed: int = 0) -> dict:
    key_of = jax.random.split(jax.random.key(seed), 9)
    return {
        "features": noise(key_of[0], (NODES, FIN), 1.0, 6.0, ((0, 128),)),
        "weight": noise(key_of[1], (FIN, FOUT), FIN ** -0.5, 0.5),
        "out_bias": noise(key_of[2], (FOUT,), 0.5, 3.0, (), jnp.float32),
        "edge_tiles": noise(key_of[3], (TILES, BLK, BLK), (DEG * BLK) ** -0.5, 0.125, ((0, 256),)),
        "block_row": draw_block_row(jax.random.fold_in(key_of[8], 71), 0),
        "tile_slot": draw_tile_slot(jax.random.fold_in(key_of[8], 71), 0),
        "send_list": draw_send_list(jax.random.fold_in(key_of[8], 71), 0),
        "out_grad": noise(key_of[7], (NODES, FOUT), 1.0, 6.0, ((0, 128),)),
    }


ROOT_TWO_PI = 0.7978845608028654
CUBIC_TERM = 0.044715

def gelu_value(values):
    inner_term = ROOT_TWO_PI * (values + CUBIC_TERM * values * values * values)
    return 0.5 * values * (1.0 + jnp.tanh(inner_term))

def gelu_slope(values):
    tangent = jnp.tanh(ROOT_TWO_PI * (values + CUBIC_TERM * values * values * values))
    outer_part = 0.5 * values * (1.0 - tangent * tangent) * ROOT_TWO_PI
    return 0.5 * (1.0 + tangent) + outer_part * (1.0 + 3.0 * CUBIC_TERM * values * values)

def column_blocks(tile_slot, send_list):
    tile_index = jnp.arange(TILES, dtype=jnp.int32)
    device = tile_index // TPD
    nodes_index = device // N_REP
    rep_index = device % N_REP
    source = tile_slot // CAP
    column = tile_slot % CAP
    list_row = (source * N_REP + rep_index) * N_NODES + nodes_index
    local_block = send_list[list_row, column]
    return (source * NBD + local_block).astype(jnp.int32)

def reference(features, weight, out_bias, edge_tiles, block_row, tile_slot, send_list, out_grad):
    columns = column_blocks(tile_slot, send_list)
    group_count = N_NODES * N_REP
    slot_count = N_NODES * CAP
    tile_groups = edge_tiles.reshape(group_count, TPD, BLK, BLK)
    row_groups = block_row.reshape(group_count, TPD)
    col_groups = columns.reshape(group_count, TPD)
    slot_groups = tile_slot.reshape(group_count, TPD)
    group_ids = jnp.arange(group_count, dtype=jnp.int32)
    feature_blocks = features.reshape(NBLK, BLK, FIN)

    def forward_step(running, inputs):
        tile_set, row_ids, col_ids = inputs
        picked = feature_blocks[col_ids].astype(jnp.float32)
        products = jnp.einsum('tij,tjf->tif', tile_set.astype(jnp.float32), picked, precision=lax.Precision.HIGHEST)
        return (running.at[row_ids].add(products), None)
    aggregate, _ = lax.scan(forward_step, jnp.zeros((NBLK, BLK, FIN), jnp.float32), (tile_groups, row_groups, col_groups))
    aggregate_bf = aggregate.reshape(NODES, FIN).astype(jnp.bfloat16)
    preact = jnp.dot(aggregate_bf, weight, preferred_element_type=jnp.float32) + out_bias
    activations = gelu_value(preact).astype(jnp.bfloat16)
    pre_grad = (out_grad.astype(jnp.float32) * gelu_slope(preact)).astype(jnp.bfloat16)
    agg_grad = jnp.dot(pre_grad, weight.T, preferred_element_type=jnp.float32).astype(jnp.bfloat16)
    grad_blocks = agg_grad.reshape(NBLK, BLK, FIN)

    def backward_step(running, inputs):
        tile_set, row_ids, slot_ids, group = inputs
        picked = grad_blocks[row_ids].astype(jnp.float32)
        products = jnp.einsum('tji,tjf->tif', tile_set.astype(jnp.float32), picked, precision=lax.Precision.HIGHEST)
        sums = jax.ops.segment_sum(products, slot_ids, num_segments=slot_count)
        rounded = lax.optimization_barrier(sums.astype(jnp.bfloat16)).astype(jnp.float32)
        nodes_index = group // N_REP
        rep_index = group % N_REP
        slot_index = jnp.arange(slot_count, dtype=jnp.int32)
        source = slot_index // CAP
        place = slot_index % CAP
        list_row = (source * N_REP + rep_index) * N_NODES + nodes_index
        targets = (source * NBD + send_list[list_row, place]).astype(jnp.int32)
        return (running.at[targets].add(rounded), None)
    gathered, _ = lax.scan(backward_step, jnp.zeros((NBLK, BLK, FIN), jnp.float32), (tile_groups, row_groups, slot_groups, group_ids))
    feature_grad = gathered.reshape(NODES, FIN)
    norm_scale = 1.0 / math.sqrt(NODES)
    weight_grad = jnp.dot(aggregate_bf.T, pre_grad, preferred_element_type=jnp.float32) * norm_scale
    bias_grad = lax.optimization_barrier(jnp.sum(pre_grad.astype(jnp.float32), axis=0)) * norm_scale
    return (activations, feature_grad, weight_grad, bias_grad)
```

```python
import functools
import math

import jax
import jax.numpy as jnp
from jax import lax
from jax.experimental import pallas as pl
from jax.experimental.pallas import tpu as pltpu
from jax.sharding import PartitionSpec as P

ROOT_TWO_PI = 0.7978845608028654
CUBIC_TERM = 0.044715

NY, NZ, NX = 4, 8, 4
BLK = 128
HALF = 64
NB = 8
CAP = 56
MSG = NB * HALF + 16
PART = NZ * MSG
LOCAL = NY * PART
FAR = CAP * HALF
TILES = 128
LOC0, REM0, CNT0, OVER = 128, 256, 440, 444
VMEM_LIMIT = 48 * 1024 * 1024


def gelu_value(values):
    inner_term = ROOT_TWO_PI * (values + CUBIC_TERM * values * values * values)
    return 0.5 * values * (1.0 + jnp.tanh(inner_term))


def gelu_slope(values):
    tangent = jnp.tanh(ROOT_TWO_PI * (values + CUBIC_TERM * values * values * values))
    outer_part = 0.5 * values * (1.0 - tangent * tangent) * ROOT_TWO_PI
    return 0.5 * (1.0 + tangent) + outer_part * (1.0 + 3.0 * CUBIC_TERM * values * values)


def general_shards(features, weight, out_bias, edge_tiles, block_row, tile_slot, send_list, out_grad):
    node_count = lax.axis_size("nodes")
    rep_count = lax.axis_size("rep")
    rep_position = lax.axis_index("rep")
    block_size = edge_tiles.shape[1]
    local_blocks = features.shape[0] // block_size
    width_in = features.shape[1]
    capacity = send_list.shape[1]
    half_out = weight.shape[1] // rep_count
    feature_blocks = features.reshape(local_blocks, block_size, width_in)
    outgoing = feature_blocks[send_list]
    incoming = lax.all_to_all(outgoing, "nodes", split_axis=0, concat_axis=0, tiled=True)
    incoming = incoming.reshape(node_count * capacity, block_size, width_in)
    picked = incoming[tile_slot]
    products = jnp.einsum("tij,tjf->tif", edge_tiles, picked, preferred_element_type=jnp.float32)
    local_rows = block_row - lax.axis_index("nodes") * local_blocks
    partial_value = jax.ops.segment_sum(products, local_rows, num_segments=local_blocks)
    partial_value = partial_value.reshape(local_blocks * block_size, width_in)
    aggregate_bf = lax.psum(partial_value, "rep").astype(jnp.bfloat16)
    preact = jnp.dot(aggregate_bf, weight, preferred_element_type=jnp.float32) + out_bias
    own_preact = lax.dynamic_slice_in_dim(preact, rep_position * half_out, half_out, 1)
    activations = gelu_value(own_preact).astype(jnp.bfloat16)
    pre_grad = (out_grad.astype(jnp.float32) * gelu_slope(preact)).astype(jnp.bfloat16)
    agg_grad = lax.dot_general(
        pre_grad, weight, (((1,), (1,)), ((), ())), preferred_element_type=jnp.float32
    ).astype(jnp.bfloat16)
    grad_rows = agg_grad.reshape(local_blocks, block_size, width_in)[local_rows]
    back_products = jnp.einsum(
        "tji,tjf->tif", edge_tiles, grad_rows, preferred_element_type=jnp.float32
    )
    slot_sums = jax.ops.segment_sum(back_products, tile_slot, num_segments=node_count * capacity)
    slot_sums = slot_sums.astype(jnp.bfloat16)
    returned = lax.all_to_all(
        slot_sums.reshape(node_count, capacity, block_size, width_in),
        "nodes",
        split_axis=0,
        concat_axis=0,
        tiled=True,
    )
    returned = returned.astype(jnp.float32)
    owner_sums = jax.ops.segment_sum(
        returned.reshape(node_count * capacity, block_size, width_in),
        send_list.reshape(-1),
        num_segments=local_blocks,
    )
    feature_grad = lax.psum_scatter(
        owner_sums.reshape(local_blocks * block_size, width_in).astype(jnp.bfloat16),
        "rep",
        scatter_dimension=0,
        tiled=True,
    ).astype(jnp.float32)
    own_grad = lax.dynamic_slice_in_dim(pre_grad, rep_position * half_out, half_out, 1)
    norm_scale = 1.0 / math.sqrt(features.shape[0] * node_count)
    weight_part = (
        lax.dot_general(
            aggregate_bf, own_grad, (((0,), (0,)), ((), ())), preferred_element_type=jnp.float32
        )
        * norm_scale
    )
    bias_part = jnp.sum(own_grad.astype(jnp.float32), axis=0) * norm_scale
    weight_grad, bias_grad = lax.psum((weight_part, bias_part), "nodes")
    return (activations, feature_grad, weight_grad, bias_grad)


def device_of(y, z, x, c):
    return ((y % NY * NZ + z % NZ) * NX + x % NX) * 2 + c


def moved(value, target):
    pairs = [
        (device_of(y, z, x, c), device_of(*target(y, z, x, c)))
        for y in range(NY)
        for z in range(NZ)
        for x in range(NX)
        for c in range(2)
    ]
    return lax.ppermute(value, ("nodes", "rep"), pairs)


def along_z(value, step):
    return moved(value, lambda y, z, x, c: (y, z + step, x, c))


def along_dense(value, step):
    return moved(value, lambda y, z, x, c: (y + step, z, x, c) if c == 0 else (y, z, x + step, c))


def along_sparse(value, step):
    return moved(value, lambda y, z, x, c: (y, z, x + step, c) if c == 0 else (y + step, z, x, c))


def to_other_core(value):
    return moved(value, lambda y, z, x, c: (y, z, x, 1 - c))


SMEM = pl.BlockSpec(memory_space=pltpu.SMEM)
VMEM = pl.BlockSpec(memory_space=pltpu.VMEM)
ANY = pl.BlockSpec(memory_space=pl.ANY)


def call(kernel, out_shape, in_specs, out_specs, scratch=(), flops=0, moved_bytes=0):
    return pl.pallas_call(
        kernel,
        out_shape=out_shape,
        in_specs=in_specs,
        out_specs=out_specs,
        scratch_shapes=list(scratch),
        compiler_params=pltpu.CompilerParams(vmem_limit_bytes=VMEM_LIMIT),
        cost_estimate=pl.CostEstimate(flops=flops, bytes_accessed=moved_bytes, transcendentals=0),
    )


def struct(shape, dtype):
    return jax.ShapeDtypeStruct(shape, dtype)


def message_kernel(core_ref, features_ref, own_ref, other_ref, out_ref):
    core = core_ref[0]
    for block in range(NB):
        turned = features_ref[block * BLK : (block + 1) * BLK, :].astype(jnp.float32).T
        half = jnp.where(core == 0, turned[:HALF], turned[HALF:])
        out_ref[block * HALF : (block + 1) * HALF, :] = half.astype(jnp.bfloat16)
    own, other = own_ref[1:3, :], other_ref[1:3, :]
    lists = jnp.concatenate(
        [
            jnp.where(core == 0, own, other),
            jnp.where(core == 0, other, own),
            jnp.zeros((12, BLK), jnp.int32),
        ],
        axis=0,
    )
    out_ref[NB * HALF :, :] = lists.astype(jnp.float32).astype(jnp.bfloat16)


def plan_kernel(code_ref, info_ref, first_ref, second_ref, third_ref, count_ref):
    requests = (first_ref, second_ref, third_ref)
    for k in range(8):
        count_ref[k] = 0

    def clear(i, carry):
        for ref in requests:
            ref[i] = 0
        return carry

    lax.fori_loop(0, 128, clear, 0)

    def clear_info(i, carry):
        info_ref[i] = 0
        return carry

    lax.fori_loop(0, 512, clear_info, 0)

    def place(t, carry):
        code = code_ref[t]
        other_key = code // 512
        key = code // 128 % 4
        slot = code % 128
        count_ref[4 + other_key] = count_ref[4 + other_key] + 1
        rank = count_ref[key]
        count_ref[key] = rank + 1

        @pl.when(key == 0)
        def _():
            info_ref[t] = slot
            info_ref[LOC0 + rank] = t

        @pl.when(jnp.logical_and(key > 0, rank < CAP))
        def _():
            info_ref[t] = 256 + (key - 1) * CAP + rank
            info_ref[REM0 + (key - 1) * CAP + rank] = t
            for k in (1, 2, 3):

                @pl.when(key == k)
                def _():
                    requests[k - 1][rank] = slot

        return carry

    lax.fori_loop(0, TILES, place, 0)
    over = 0
    info_ref[CNT0] = count_ref[0]
    for k in (1, 2, 3):
        kept = jnp.minimum(count_ref[k], CAP)
        info_ref[CNT0 + k] = kept
        requests[k - 1][64] = kept
        over += count_ref[k] - kept
        over += jnp.maximum(count_ref[4 + k] - CAP, 0)
    info_ref[OVER] = over


def local_row(slot, table_ref, k):
    row = slot // 4 * MSG + table_ref[slot * 4 + k] * HALF
    return pl.multiple_of(row, 16)


def pick_kernel(
    a_ref, b_ref, c_ref, d_ref, first_ref, second_ref, third_ref, table_ref, o1, o2, o3, held, sem
):
    copies = [
        pltpu.make_async_copy(ref, held.at[pl.ds(j * PART, PART)], sem.at[j])
        for j, ref in enumerate((a_ref, b_ref, c_ref, d_ref))
    ]
    for copy in copies:
        copy.start()
    for copy in copies:
        copy.wait()
    for k, (req, out) in enumerate(((first_ref, o1), (second_ref, o2), (third_ref, o3))):

        def body(i, carry, req=req, out=out, k=k):
            for u in range(8):
                p = i * 8 + u
                row = local_row(req[p], table_ref, k + 1)
                out[pl.ds(pl.multiple_of(p * HALF, HALF), HALF), :] = held[pl.ds(row, HALF), :]
            return carry

        lax.fori_loop(0, CAP // 8, body, 0)


def forward_kernel(
    a_ref, b_ref, c_ref, d_ref, r1, r2, r3, own_ref, other_ref, info_ref, rows_ref, table_ref,
    out_ref, held, tiles, acc, sem,
):
    copies = [
        pltpu.make_async_copy(ref, held.at[pl.ds(j * PART, PART)], sem.at[j])
        for j, ref in enumerate((a_ref, b_ref, c_ref, d_ref))
    ]
    copies += [
        pltpu.make_async_copy(ref, held.at[pl.ds(LOCAL + j * FAR, FAR)], sem.at[4 + j])
        for j, ref in enumerate((r1, r2, r3))
    ]
    copies += [
        pltpu.make_async_copy(ref, tiles.at[pl.ds(j * 64, 64)], sem.at[7 + j])
        for j, ref in enumerate((own_ref, other_ref))
    ]
    for copy in copies:
        copy.start()
    acc[...] = jnp.zeros_like(acc)
    for copy in copies:
        copy.wait()

    def body(i, carry):
        done = []
        for u in range(8):
            t = i * 8 + u
            place = info_ref[t]
            near = jnp.minimum(place, 127)
            row = jnp.where(
                place < 256, local_row(near, table_ref, 0), LOCAL + (place - 256) * HALF
            )
            block = held[pl.ds(pl.multiple_of(row, 16), HALF), :]
            done.append(
                lax.dot_general(
                    block, tiles[t], (((1,), (1,)), ((), ())), preferred_element_type=jnp.float32
                )
            )
        for u in range(8):
            at = pl.ds(pl.multiple_of(rows_ref[i * 8 + u] * HALF, HALF), HALF)
            acc[at, :] += done[u]
        return carry

    lax.fori_loop(0, TILES // 8, body, 0)
    out_ref[...] = acc[...].astype(jnp.bfloat16)


def middle_kernel(
    core_ref, info_ref, rows_ref, own_agg, other_agg, weight_ref, bias_ref, grad_ref, own_ref,
    other_ref, act_ref, sums_ref, turned_ref, o1, o2, o3, tiles, sem,
):
    copies = [
        pltpu.make_async_copy(ref, tiles.at[pl.ds(j * 64, 64)], sem.at[j])
        for j, ref in enumerate((own_ref, other_ref))
    ]
    for copy in copies:
        copy.start()
    core = core_ref[0]
    sums_ref[...] = jnp.zeros_like(sums_ref)
    weight_half = weight_ref[pl.ds(pl.multiple_of(core * HALF, HALF), HALF), :]

    def block_step(b, carry):
        at = pl.ds(pl.multiple_of(b * HALF, HALF), HALF)
        own, other = own_agg[at, :], other_agg[at, :]
        low = jnp.where(core == 0, own, other)
        high = jnp.where(core == 0, other, own)
        agg = jnp.concatenate([low, high], axis=0)
        preact = lax.dot_general(
            agg, weight_ref[...], (((0,), (0,)), ((), ())), preferred_element_type=jnp.float32
        )
        preact = preact + bias_ref[...]
        tangent = jnp.tanh(ROOT_TWO_PI * (preact + CUBIC_TERM * preact * preact * preact))
        nodes = pl.ds(pl.multiple_of(b * BLK, BLK), BLK)
        value = 0.5 * preact * (1.0 + tangent)
        act_ref[nodes, :] = jnp.where(core == 0, value[:, :BLK], value[:, BLK:]).astype(jnp.bfloat16)
        outer = 0.5 * preact * (1.0 - tangent * tangent) * ROOT_TWO_PI
        slope = 0.5 * (1.0 + tangent) + outer * (1.0 + 3.0 * CUBIC_TERM * preact * preact)
        pre = (grad_ref[nodes, :].astype(jnp.float32) * slope).astype(jnp.bfloat16)
        turned_ref[at, :] = lax.dot_general(
            weight_half, pre, (((1,), (1,)), ((), ())), preferred_element_type=jnp.float32
        ).astype(jnp.bfloat16)
        mine = jnp.where(core == 0, pre[:, :BLK], pre[:, BLK:])
        sums_ref[:BLK, :] += lax.dot_general(
            agg, mine, (((1,), (0,)), ((), ())), preferred_element_type=jnp.float32
        )
        sums_ref[BLK : BLK + 1, :] += jnp.sum(mine.astype(jnp.float32), axis=0, keepdims=True)
        return carry

    lax.fori_loop(0, NB, block_step, 0)
    over = info_ref[OVER].astype(jnp.float32)
    sums_ref[BLK + 1 : BLK + 2, :] = jnp.full((1, BLK), over, jnp.float32)
    for copy in copies:
        copy.wait()
    for k, out in enumerate((o1, o2, o3)):

        def body(i, carry, out=out, k=k):
            for u in range(8):
                p = i * 8 + u
                t = info_ref[REM0 + k * CAP + p]
                left = turned_ref[pl.ds(pl.multiple_of(rows_ref[t] * HALF, HALF), HALF), :]
                out[pl.ds(pl.multiple_of(p * HALF, HALF), HALF), :] = jnp.dot(
                    left, tiles[t], preferred_element_type=jnp.float32
                ).astype(jnp.bfloat16)
            return carry

        lax.fori_loop(0, (info_ref[CNT0 + 1 + k] + 7) // 8, body, 0)


def owner_kernel(
    info_ref, rows_ref, table_ref, first_ref, second_ref, third_ref, turned_ref, own_ref, other_ref,
    r1, r2, r3, o0, o1, o2, o3, tiles, total, sem,
):
    copies = [
        pltpu.make_async_copy(ref, tiles.at[pl.ds(j * 64, 64)], sem.at[j])
        for j, ref in enumerate((own_ref, other_ref))
    ]
    for copy in copies:
        copy.start()
    total[...] = jnp.zeros_like(total)
    for copy in copies:
        copy.wait()
    spare = 256 * HALF

    def total_row(slot, k, used):
        row = (slot // 4 * NB + table_ref[slot * 4 + k]) * HALF
        return pl.ds(pl.multiple_of(jnp.where(used, row, spare), HALF), HALF)

    count = info_ref[CNT0]

    def near(i, carry):
        done = []
        for u in range(8):
            t = info_ref[LOC0 + jnp.minimum(i * 8 + u, TILES - 1)]
            left = turned_ref[pl.ds(pl.multiple_of(rows_ref[t] * HALF, HALF), HALF), :]
            done.append(jnp.dot(left, tiles[t], preferred_element_type=jnp.float32))
        for u in range(8):
            p = i * 8 + u
            t = info_ref[LOC0 + jnp.minimum(p, TILES - 1)]
            slot = jnp.minimum(info_ref[t], 127)
            total[total_row(slot, 0, p < count), :] += done[u]
        return carry

    lax.fori_loop(0, (count + 7) // 8, near, 0)
    for k, (req, got) in enumerate(((first_ref, r1), (second_ref, r2), (third_ref, r3))):
        kept = req[64]

        def far(i, carry, req=req, got=got, k=k, kept=kept):
            for u in range(8):
                p = i * 8 + u
                at = total_row(req[p], k + 1, p < kept)
                total[at, :] += got[pl.ds(pl.multiple_of(p * HALF, HALF), HALF), :].astype(
                    jnp.float32
                )
            return carry

        lax.fori_loop(0, (kept + 7) // 8, far, 0)
    for j, out in enumerate((o0, o1, o2, o3)):
        out[...] = total[j * 64 * HALF : (j + 1) * 64 * HALF, :].astype(jnp.bfloat16)


def split_sum_kernel(a_ref, b_ref, c_ref, d_ref, *outs):
    rows = NB * HALF
    for m in range(NZ):
        at = slice(m * rows, (m + 1) * rows)
        value = a_ref[at, :].astype(jnp.float32) + b_ref[at, :].astype(jnp.float32)
        value = value + (c_ref[at, :].astype(jnp.float32) + d_ref[at, :].astype(jnp.float32))
        outs[m][...] = value.astype(jnp.bfloat16)


def last_sum_kernel(core_ref, *refs):
    parts, (keep_ref, send_ref) = refs[:NZ], refs[NZ:]
    core = core_ref[0]
    value = parts[0][...].astype(jnp.float32)
    for ref in parts[1:]:
        value = value + ref[...].astype(jnp.float32)
    half = NB * HALF // 2
    keep_ref[...] = jnp.where(core == 0, value[:half], value[half:])
    send_ref[...] = jnp.where(core == 0, value[half:], value[:half])


def turn_kernel(core_ref, keep_ref, got_ref, out_ref):
    core = core_ref[0]
    for b in range(NB // 2):
        at = slice(b * HALF, (b + 1) * HALF)
        own, other = keep_ref[at, :], got_ref[at, :]
        both = jnp.concatenate(
            [jnp.where(core == 0, own, other), jnp.where(core == 0, other, own)], axis=0
        )
        out_ref[b * BLK : (b + 1) * BLK, :] = both.T


def shards(features, weight, out_bias, edge_tiles, block_row, tile_slot, send_list, out_grad):
    bf16, f32, i32 = jnp.bfloat16, jnp.float32, jnp.int32
    node = lax.axis_index("nodes")
    core = lax.axis_index("rep")
    y, z, x = node // (NZ * NX), node // NX % NZ, node % NX
    core_array = jnp.reshape(core, (1,)).astype(i32)

    local_rows = block_row - node * NB
    packed = jnp.pad(tile_slot * NB + local_rows, (0, BLK - 64))
    own_meta = jnp.concatenate([packed[None, :], send_list.T], axis=0)
    other_meta = to_other_core(own_meta)
    other_tiles = to_other_core(edge_tiles)

    message = call(
        message_kernel, struct((MSG, BLK), bf16), [SMEM, VMEM, VMEM, VMEM], VMEM, moved_bytes=500000
    )(core_array, features, own_meta, other_meta)
    column = jnp.concatenate([message] + [along_z(message, -m) for m in range(1, NZ)], axis=0)

    both = jnp.concatenate([own_meta[0, :64], other_meta[0, :64]])
    rows = both % NB
    slot = both // NB
    source, which = slot // 2, slot % 2
    step_y = (source // (NZ * NX) - y) % NY
    step_z = (source // NX - z) % NZ
    step_x = (source - x) % NX
    dense = jnp.where(core == 0, step_y, step_x)
    sparse = jnp.where(core == 0, step_x, step_y)
    holder = jnp.where(jnp.arange(TILES) < 64, core, 1 - core)
    code = (dense * 4 + sparse) * 128 + (dense * NZ + step_z) * 4 + holder * 2 + which
    info, *requests = call(
        plan_kernel,
        [struct((512,), i32)] + [struct((128,), i32)] * 3,
        [SMEM],
        [SMEM] * 4,
        [pltpu.SMEM((8,), i32)],
        moved_bytes=100000,
    )(code.astype(i32))
    requests = [along_sparse(requests[k - 1], k) for k in (1, 2, 3)]

    parts = [column] + [along_dense(column, -j) for j in range(1, 4)]

    steps = jnp.arange(4)
    asker = jnp.where(
        core == 0,
        node - x + (x - steps) % NX,
        node - y * (NZ * NX) + (y - steps) % NY * (NZ * NX),
    )
    lists = jnp.stack([part.reshape(NZ, MSG, BLK)[:, NB * HALF : NB * HALF + 4] for part in parts])
    chosen = (jnp.arange(BLK)[:, None] == asker[None, :]).astype(bf16)
    table = jnp.dot(lists.reshape(4 * NZ * 4, BLK), chosen, preferred_element_type=f32)
    table = table.astype(i32).reshape(-1)

    picked = call(
        pick_kernel,
        [struct((FAR, BLK), bf16)] * 3,
        [ANY] * 4 + [SMEM] * 4,
        [VMEM] * 3,
        [pltpu.VMEM((LOCAL, BLK), bf16), pltpu.SemaphoreType.DMA((4,))],
        moved_bytes=7000000,
    )(*parts, *requests, table)
    far = [along_sparse(picked[k - 1], -k) for k in (1, 2, 3)]

    agg_half = call(
        forward_kernel,
        struct((NB * HALF, BLK), bf16),
        [ANY] * 9 + [SMEM] * 3,
        VMEM,
        [
            pltpu.VMEM((LOCAL + 3 * FAR, BLK), bf16),
            pltpu.VMEM((TILES, BLK, BLK), bf16),
            pltpu.VMEM((NB * HALF, BLK), f32),
            pltpu.SemaphoreType.DMA((9,)),
        ],
        flops=2 * TILES * HALF * BLK * BLK,
        moved_bytes=11000000,
    )(*parts, *far, edge_tiles, other_tiles, info, rows, table)
    other_half = to_other_core(agg_half)

    activations, sums, turned, *back = call(
        middle_kernel,
        [
            struct((NB * BLK, BLK), bf16),
            struct((136, BLK), f32),
            struct((NB * HALF, BLK), bf16),
        ]
        + [struct((FAR, BLK), bf16)] * 3,
        [SMEM] * 3 + [VMEM] * 5 + [ANY] * 2,
        [VMEM] * 6,
        [pltpu.VMEM((TILES, BLK, BLK), bf16), pltpu.SemaphoreType.DMA((2,))],
        flops=2 * TILES * HALF * BLK * BLK,
        moved_bytes=8000000,
    )(
        core_array, info, rows, agg_half, other_half, weight, out_bias[None, :], out_grad,
        edge_tiles, other_tiles,
    )
    back = [along_sparse(back[k - 1], k) for k in (1, 2, 3)]

    for axis, size in ((0, NZ), (1, NY), (2, NX)):
        step = 1
        while step < size:
            sums = sums + moved(
                sums,
                lambda y, z, x, c, axis=axis, step=step: (
                    y ^ step if axis == 1 else y,
                    z ^ step if axis == 0 else z,
                    x ^ step if axis == 2 else x,
                    c,
                ),
            )
            step *= 2

    owned = call(
        owner_kernel,
        [struct((64 * HALF, BLK), bf16)] * 4,
        [SMEM] * 6 + [VMEM] + [ANY] * 2 + [VMEM] * 3,
        [VMEM] * 4,
        [
            pltpu.VMEM((TILES, BLK, BLK), bf16),
            pltpu.VMEM((257 * HALF, BLK), f32),
            pltpu.SemaphoreType.DMA((2,)),
        ],
        flops=2 * 32 * HALF * BLK * BLK,
        moved_bytes=11000000,
    )(info, rows, table, *requests, turned, edge_tiles, other_tiles, *back)
    owned = [owned[0]] + [along_dense(owned[j], j) for j in range(1, 4)]
    pieces = call(
        split_sum_kernel,
        [struct((NB * HALF, BLK), bf16)] * NZ,
        [VMEM] * 4,
        [VMEM] * NZ,
        moved_bytes=5000000,
    )(*owned)
    pieces = [pieces[0]] + [along_z(pieces[m], m) for m in range(1, NZ)]
    keep, send = call(
        last_sum_kernel,
        [struct((NB * HALF // 2, BLK), f32)] * 2,
        [SMEM] + [VMEM] * NZ,
        [VMEM] * 2,
        moved_bytes=1500000,
    )(core_array, *pieces)
    feature_grad = call(
        turn_kernel, struct((NB // 2 * BLK, BLK), f32), [SMEM, VMEM, VMEM], VMEM, moved_bytes=500000
    )(core_array, keep, to_other_core(send))

    norm_scale = 1.0 / math.sqrt(features.shape[0] * NY * NZ * NX)
    fast = (activations, feature_grad, sums[:BLK] * norm_scale, sums[BLK] * norm_scale)
    return lax.cond(
        sums[BLK + 1, 0] > 0.5,
        lambda: general_shards(
            features, weight, out_bias, edge_tiles, block_row, tile_slot, send_list, out_grad
        ),
        lambda: fast,
    )


def solution(mesh):
    placed = (
        P("nodes", None),
        P(),
        P(),
        P(("nodes", "rep"), None, None),
        P(("nodes", "rep")),
        P(("nodes", "rep")),
        P(("nodes", "rep"), None),
        P("nodes", None),
    )
    return jax.shard_map(
        shards,
        mesh=mesh,
        in_specs=placed,
        out_specs=(P("nodes", "rep"), P(("nodes", "rep"), None), P(None, "rep"), P("rep")),
        check_vma=False,
    )
```

```python
import functools
import math

import jax
import jax.numpy as jnp
from jax import lax
from jax.experimental import pallas as pl
from jax.experimental.pallas import tpu as pltpu
from jax.sharding import PartitionSpec as P

ROOT_TWO_PI = 0.7978845608028654
CUBIC_TERM = 0.044715

NY, NZ, NX = 4, 8, 4
BLK = 128
HALF = 64
NB = 8
CAP = 56
ROWS = NB * HALF
MSG = ROWS + 16
PART = NZ * MSG
LOCAL = NY * PART
FAR = CAP * HALF
TILES = 128
LOC0, REM0, CNT0, OVER, ROW0 = 128, 256, 440, 444, 512
INFO = 640
SUMS = BLK + 16
SEND = 64 * HALF


def gelu_value(values):
    inner_term = ROOT_TWO_PI * (values + CUBIC_TERM * values * values * values)
    return 0.5 * values * (1.0 + jnp.tanh(inner_term))


def gelu_slope(values):
    tangent = jnp.tanh(ROOT_TWO_PI * (values + CUBIC_TERM * values * values * values))
    outer_part = 0.5 * values * (1.0 - tangent * tangent) * ROOT_TWO_PI
    return 0.5 * (1.0 + tangent) + outer_part * (1.0 + 3.0 * CUBIC_TERM * values * values)


def general_shards(features, weight, out_bias, edge_tiles, block_row, tile_slot, send_list, out_grad):
    node_count = lax.axis_size("nodes")
    rep_count = lax.axis_size("rep")
    rep_position = lax.axis_index("rep")
    block_size = edge_tiles.shape[1]
    local_blocks = features.shape[0] // block_size
    width_in = features.shape[1]
    capacity = send_list.shape[1]
    half_out = weight.shape[1] // rep_count
    feature_blocks = features.reshape(local_blocks, block_size, width_in)
    outgoing = feature_blocks[send_list]
    incoming = lax.all_to_all(outgoing, "nodes", split_axis=0, concat_axis=0, tiled=True)
    incoming = incoming.reshape(node_count * capacity, block_size, width_in)
    picked = incoming[tile_slot]
    products = jnp.einsum("tij,tjf->tif", edge_tiles, picked, preferred_element_type=jnp.float32)
    local_rows = block_row - lax.axis_index("nodes") * local_blocks
    partial_value = jax.ops.segment_sum(products, local_rows, num_segments=local_blocks)
    partial_value = partial_value.reshape(local_blocks * block_size, width_in)
    aggregate_bf = lax.psum(partial_value, "rep").astype(jnp.bfloat16)
    preact = jnp.dot(aggregate_bf, weight, preferred_element_type=jnp.float32) + out_bias
    own_preact = lax.dynamic_slice_in_dim(preact, rep_position * half_out, half_out, 1)
    activations = gelu_value(own_preact).astype(jnp.bfloat16)
    pre_grad = (out_grad.astype(jnp.float32) * gelu_slope(preact)).astype(jnp.bfloat16)
    agg_grad = lax.dot_general(
        pre_grad, weight, (((1,), (1,)), ((), ())), preferred_element_type=jnp.float32
    ).astype(jnp.bfloat16)
    grad_rows = agg_grad.reshape(local_blocks, block_size, width_in)[local_rows]
    back_products = jnp.einsum(
        "tji,tjf->tif", edge_tiles, grad_rows, preferred_element_type=jnp.float32
    )
    slot_sums = jax.ops.segment_sum(back_products, tile_slot, num_segments=node_count * capacity)
    slot_sums = slot_sums.astype(jnp.bfloat16)
    returned = lax.all_to_all(
        slot_sums.reshape(node_count, capacity, block_size, width_in),
        "nodes",
        split_axis=0,
        concat_axis=0,
        tiled=True,
    )
    returned = returned.astype(jnp.float32)
    owner_sums = jax.ops.segment_sum(
        returned.reshape(node_count * capacity, block_size, width_in),
        send_list.reshape(-1),
        num_segments=local_blocks,
    )
    feature_grad = lax.psum_scatter(
        owner_sums.reshape(local_blocks * block_size, width_in).astype(jnp.bfloat16),
        "rep",
        scatter_dimension=0,
        tiled=True,
    ).astype(jnp.float32)
    own_grad = lax.dynamic_slice_in_dim(pre_grad, rep_position * half_out, half_out, 1)
    norm_scale = 1.0 / math.sqrt(features.shape[0] * node_count)
    weight_part = (
        lax.dot_general(
            aggregate_bf, own_grad, (((0,), (0,)), ((), ())), preferred_element_type=jnp.float32
        )
        * norm_scale
    )
    bias_part = jnp.sum(own_grad.astype(jnp.float32), axis=0) * norm_scale
    weight_grad, bias_grad = lax.psum((weight_part, bias_part), "nodes")
    return (activations, feature_grad, weight_grad, bias_grad)


def device_of(y, z, x, c):
    return ((y % NY * NZ + z % NZ) * NX + x % NX) * 2 + c


def moved(value, target):
    pairs = [
        (device_of(y, z, x, c), device_of(*target(y, z, x, c)))
        for y in range(NY)
        for z in range(NZ)
        for x in range(NX)
        for c in range(2)
    ]
    return lax.ppermute(value, ("nodes", "rep"), pairs)


def along_z(value, step):
    return moved(value, lambda y, z, x, c: (y, z + step if c == 0 else z - step, x, c))


def along_dense(value, step):
    return moved(value, lambda y, z, x, c: (y + step, z, x, c) if c == 0 else (y, z, x + step, c))


def along_sparse(value, step):
    return moved(value, lambda y, z, x, c: (y, z, x + step, c) if c == 0 else (y + step, z, x, c))


def to_other_core(value):
    return moved(value, lambda y, z, x, c: (y, z, x, 1 - c))


SMEM = pl.BlockSpec(memory_space=pltpu.SMEM)
VMEM = pl.BlockSpec(memory_space=pltpu.VMEM)
ANY = pl.BlockSpec(memory_space=pl.ANY)


def call(kernel, out_shape, in_specs, out_specs, scratch=(), flops=0, moved_bytes=0, vmem=12):
    return pl.pallas_call(
        kernel,
        out_shape=out_shape,
        in_specs=in_specs,
        out_specs=out_specs,
        scratch_shapes=list(scratch),
        compiler_params=pltpu.CompilerParams(vmem_limit_bytes=vmem << 20),
        cost_estimate=pl.CostEstimate(flops=flops, bytes_accessed=moved_bytes, transcendentals=0),
    )


def struct(shape, dtype):
    return jax.ShapeDtypeStruct(shape, dtype)


def message_kernel(core_ref, features_ref, own_ref, other_ref, out_ref, half_ref):
    core = core_ref[0]
    for block in range(NB):
        turned = features_ref[block * BLK : (block + 1) * BLK, :].astype(jnp.float32).T
        mine = jnp.where(core == 0, turned[:HALF], turned[HALF:]).astype(jnp.bfloat16)
        rest = jnp.where(core == 0, turned[HALF:], turned[:HALF]).astype(jnp.bfloat16)
        out_ref[block * HALF : (block + 1) * HALF, :] = mine
        half_ref[block * HALF : (block + 1) * HALF, :] = mine
        out_ref[MSG + block * HALF : MSG + (block + 1) * HALF, :] = rest
    own, other = own_ref[1:3, :], other_ref[1:3, :]
    lists = jnp.concatenate(
        [
            jnp.where(core == 0, own, other),
            jnp.where(core == 0, other, own),
            jnp.zeros((12, BLK), jnp.int32),
        ],
        axis=0,
    )
    lists = lists.astype(jnp.float32).astype(jnp.bfloat16)
    out_ref[ROWS:MSG, :] = lists
    half_ref[ROWS:MSG, :] = lists


def plan_kernel(code_ref, rows_ref, info_ref, first_ref, second_ref, third_ref, count_ref):
    requests = (first_ref, second_ref, third_ref)
    for k in range(8):
        count_ref[k] = 0

    def clear(i, carry):
        for ref in requests:
            ref[i] = 0
        info_ref[i] = 0
        info_ref[LOC0 + i] = 0
        info_ref[REM0 + i] = 0
        info_ref[REM0 + 128 + i] = 0
        info_ref[ROW0 + i] = rows_ref[i]
        return carry

    lax.fori_loop(0, 128, clear, 0)

    def place(t, carry):
        code = code_ref[t]
        other_key = code // 512
        key = code // 128 % 4
        slot = code % 128
        count_ref[4 + other_key] = count_ref[4 + other_key] + 1
        rank = count_ref[key]
        count_ref[key] = rank + 1

        @pl.when(key == 0)
        def _():
            info_ref[rank] = slot
            info_ref[LOC0 + rank] = t

        @pl.when(jnp.logical_and(key > 0, rank < CAP))
        def _():
            info_ref[REM0 + (key - 1) * CAP + rank] = t
            for k in (1, 2, 3):

                @pl.when(key == k)
                def _():
                    requests[k - 1][rank] = slot

        return carry

    lax.fori_loop(0, TILES, place, 0)
    over = 0
    info_ref[CNT0] = count_ref[0]
    for k in (1, 2, 3):
        kept = jnp.minimum(count_ref[k], CAP)
        info_ref[CNT0 + k] = kept
        requests[k - 1][64] = kept
        over += count_ref[k] - kept
        over += jnp.maximum(count_ref[4 + k] - CAP, 0)
    info_ref[OVER] = over


def start_all(pairs, sem):
    copies = [pltpu.make_async_copy(src, dst, sem.at[n]) for n, (src, dst) in enumerate(pairs)]
    for copy in copies:
        copy.start()
    return copies


def wait_all(copies):
    for copy in copies:
        copy.wait()


def half_rows(index):
    return pl.ds(pl.multiple_of(index * HALF, HALF), HALF)


def local_block(parts, slot, table, k):
    at = pl.ds(pl.multiple_of(slot // 4 % NZ * MSG + table[slot * 4 + k] * HALF, 16), HALF)
    part = slot // (4 * NZ)
    low = jnp.where(part == 0, parts[0][at, :], parts[1][at, :])
    high = jnp.where(part == 2, parts[2][at, :], parts[3][at, :])
    return jnp.where(part < 2, low, high)


def pick_kernel(
    a_ref, b_ref, c_ref, d_ref, first_ref, second_ref, third_ref, table_ref, o1, o2, o3,
    q1, q2, q3, table, sem,
):
    parts = (a_ref, b_ref, c_ref, d_ref)
    wait_all(
        start_all([(first_ref, q1), (second_ref, q2), (third_ref, q3), (table_ref, table)], sem)
    )
    for k, (req, out) in enumerate(((q1, o1), (q2, o2), (q3, o3))):

        def body(i, carry, req=req, out=out, k=k):
            for u in range(8):
                p = i * 8 + u
                out[half_rows(p), :] = local_block(parts, req[p], table, k + 1)
            return carry

        lax.fori_loop(0, CAP // 8, body, 0)


def near_kernel(
    a_ref, b_ref, c_ref, d_ref, tiles, info_ref, table_ref, out_ref, acc, info, table, sem
):
    parts = (a_ref, b_ref, c_ref, d_ref)
    copies = start_all([(info_ref, info), (table_ref, table)], sem)
    acc[...] = jnp.zeros_like(acc)
    wait_all(copies)
    count = info[CNT0]

    def body(i, carry):
        done = []
        for u in range(8):
            p = i * 8 + u
            block = local_block(parts, info[p], table, 0)
            done.append(
                lax.dot_general(
                    block, tiles[info[LOC0 + p]], (((1,), (1,)), ((), ())),
                    preferred_element_type=jnp.float32,
                )
            )
        for u in range(8):
            p = i * 8 + u
            row = jnp.where(p < count, info[ROW0 + info[LOC0 + p]], NB)
            acc[half_rows(row), :] += done[u]
        return carry

    lax.fori_loop(0, (count + 7) // 8, body, 0)
    out_ref[...] = acc[:ROWS, :]


def far_kernel(near_ref, r1, r2, r3, tiles, info_ref, out_ref, acc, info, sem):
    copies = start_all([(info_ref, info)], sem)
    acc[:ROWS, :] = near_ref[...]
    acc[ROWS:, :] = jnp.zeros((HALF, BLK), jnp.float32)
    wait_all(copies)
    for k, got in enumerate((r1, r2, r3)):
        count = info[CNT0 + 1 + k]

        def body(i, carry, k=k, got=got, count=count):
            done = []
            for u in range(8):
                p = i * 8 + u
                done.append(
                    lax.dot_general(
                        got[half_rows(p), :], tiles[info[REM0 + k * CAP + p]],
                        (((1,), (1,)), ((), ())), preferred_element_type=jnp.float32,
                    )
                )
            for u in range(8):
                p = i * 8 + u
                row = jnp.where(p < count, info[ROW0 + info[REM0 + k * CAP + p]], NB)
                acc[half_rows(row), :] += done[u]
            return carry

        lax.fori_loop(0, (count + 7) // 8, body, 0)
    out_ref[...] = acc[:ROWS, :].astype(jnp.bfloat16)


def products(step, tiles, turned_ref, info, out):
    first = REM0 + (step - 1) * CAP

    def body(i, carry):
        for u in range(8):
            p = i * 8 + u
            t = info[first + p]
            left = turned_ref[half_rows(info[ROW0 + t]), :]
            out[half_rows(p), :] = jnp.dot(
                left, tiles[t], preferred_element_type=jnp.float32
            ).astype(jnp.bfloat16)
        return carry

    lax.fori_loop(0, (info[CNT0 + step] + 7) // 8, body, 0)


def middle_kernel(
    core_ref, own_agg, other_agg, weight_ref, bias_ref, grad_ref, tiles, info_ref,
    act_ref, sums_ref, turned_ref, out, info, sem,
):
    copies = start_all([(info_ref, info)], sem)
    core = core_ref[0]
    sums_ref[...] = jnp.zeros_like(sums_ref)
    weight_half = weight_ref[half_rows(core), :]

    def block_step(b, carry):
        own, other = own_agg[half_rows(b), :], other_agg[half_rows(b), :]
        low = jnp.where(core == 0, own, other)
        high = jnp.where(core == 0, other, own)
        agg = jnp.concatenate([low, high], axis=0)
        preact = lax.dot_general(
            agg, weight_ref[...], (((0,), (0,)), ((), ())), preferred_element_type=jnp.float32
        )
        preact = preact + bias_ref[...]
        tangent = jnp.tanh(ROOT_TWO_PI * (preact + CUBIC_TERM * preact * preact * preact))
        nodes = pl.ds(pl.multiple_of(b * BLK, BLK), BLK)
        value = 0.5 * preact * (1.0 + tangent)
        act_ref[nodes, :] = jnp.where(core == 0, value[:, :BLK], value[:, BLK:]).astype(jnp.bfloat16)
        outer = 0.5 * preact * (1.0 - tangent * tangent) * ROOT_TWO_PI
        slope = 0.5 * (1.0 + tangent) + outer * (1.0 + 3.0 * CUBIC_TERM * preact * preact)
        pre = (grad_ref[nodes, :].astype(jnp.float32) * slope).astype(jnp.bfloat16)
        turned_ref[half_rows(b), :] = lax.dot_general(
            weight_half, pre, (((1,), (1,)), ((), ())), preferred_element_type=jnp.float32
        ).astype(jnp.bfloat16)
        mine = jnp.where(core == 0, pre[:, :BLK], pre[:, BLK:])
        sums_ref[:BLK, :] += lax.dot_general(
            agg, mine, (((1,), (0,)), ((), ())), preferred_element_type=jnp.float32
        )
        sums_ref[BLK : BLK + 1, :] += jnp.sum(mine.astype(jnp.float32), axis=0, keepdims=True)
        return carry

    lax.fori_loop(0, NB, block_step, 0, unroll=2)
    wait_all(copies)
    over = info[OVER].astype(jnp.float32)
    sums_ref[BLK + 1 : BLK + 2, :] = jnp.full((1, BLK), over, jnp.float32)
    products(2, tiles, turned_ref, info, out)


def side_kernel(tiles, turned_ref, info_ref, o1, o3, info, sem):
    wait_all(start_all([(info_ref, info)], sem))
    products(1, tiles, turned_ref, info, o1)
    products(3, tiles, turned_ref, info, o3)


NORM = 1.0 / math.sqrt(NY * NZ * NX * NB * BLK)


def two_parts(value):
    upper = value.astype(jnp.bfloat16)
    return upper, (value - upper.astype(jnp.float32)).astype(jnp.bfloat16)


def owner_kernel(
    info_ref, table_ref, first_ref, second_ref, third_ref, turned_ref, tiles,
    r1, r2, r3, sums_ref, o0, o1, o2, o3, total, info, table, q1, q2, q3, sem,
):
    copies = start_all(
        [(info_ref, info), (table_ref, table), (first_ref, q1), (second_ref, q2), (third_ref, q3)],
        sem,
    )
    total[...] = jnp.zeros_like(total)
    wait_all(copies)

    def total_rows(slot, k, used):
        return half_rows(jnp.where(used, slot // 4 * NB + table[slot * 4 + k], 256))

    count = info[CNT0]

    def near(i, carry):
        done = []
        for u in range(8):
            t = info[LOC0 + i * 8 + u]
            left = turned_ref[half_rows(info[ROW0 + t]), :]
            done.append(jnp.dot(left, tiles[t], preferred_element_type=jnp.float32))
        for u in range(8):
            p = i * 8 + u
            total[total_rows(info[p], 0, p < count), :] += done[u]
        return carry

    lax.fori_loop(0, (count + 7) // 8, near, 0)
    for k, (req, got) in enumerate(((q1, r1), (q2, r2), (q3, r3))):
        kept = req[64]

        def far(i, carry, req=req, got=got, k=k, kept=kept):
            for u in range(8):
                p = i * 8 + u
                at = total_rows(req[p], k + 1, p < kept)
                total[at, :] += got[half_rows(p), :].astype(jnp.float32)
            return carry

        lax.fori_loop(0, (kept + 7) // 8, far, 0)
    upper, lower = two_parts(sums_ref[...])
    for j, out in enumerate((o0, o1, o2, o3)):
        out[:SEND, :] = total[j * SEND : (j + 1) * SEND, :].astype(jnp.bfloat16)
        if j > 0:
            out[SEND : SEND + SUMS, :] = upper
            out[SEND + SUMS :, :] = lower


def split_sum_kernel(
    odd_ref, a_ref, b_ref, c_ref, d_ref, sums_ref, keep_ref, far_ref, mine_ref, swap_ref, passed_ref
):
    def sent(ref):
        upper, lower = ref[SEND : SEND + SUMS, :], ref[SEND + SUMS :, :]
        return upper.astype(jnp.float32) + lower.astype(jnp.float32)

    upper, lower = two_parts(sums_ref[...])
    own = upper.astype(jnp.float32) + lower.astype(jnp.float32)
    one, two, three = sent(b_ref), sent(c_ref), sent(d_ref)
    odd = odd_ref[0] == 1
    passed_ref[...] = (own + jnp.where(odd, three, one)) + (two + jnp.where(odd, one, three))
    for m in range(NZ):
        at = slice(m * ROWS, (m + 1) * ROWS)
        value = a_ref[at, :].astype(jnp.float32) + b_ref[at, :].astype(jnp.float32)
        value = value + (c_ref[at, :].astype(jnp.float32) + d_ref[at, :].astype(jnp.float32))
        value = value.astype(jnp.bfloat16)
        if m == 0:
            keep_ref[...] = value
        elif m < 4:
            mine_ref[(m - 1) * ROWS : m * ROWS, :] = value
        elif m == 4:
            far_ref[...] = value
        else:
            swap_ref[(m - 5) * ROWS : (m - 4) * ROWS, :] = value


def last_sum_kernel(
    core_ref, sums_ref, keep_ref, far_ref, a_ref, b_ref, c_ref, hold_ref, send_ref, passed_ref
):
    passed_ref[...] = sums_ref[...]
    core = core_ref[0]
    half = ROWS // 2

    def total(first):
        at = slice(first, first + half)
        value = a_ref[at, :].astype(jnp.float32) + b_ref[at, :].astype(jnp.float32)
        value = value + c_ref[at, :].astype(jnp.float32)
        if first < ROWS:
            value = value + keep_ref[at, :].astype(jnp.float32) + far_ref[at, :].astype(jnp.float32)
        return value

    for n in range(2):
        low, high = total(n * ROWS), total(n * ROWS + half)
        at = slice(n * half, (n + 1) * half)
        hold_ref[at, :] = jnp.where(core == 0, low, high)
        send_ref[at, :] = jnp.where(core == 0, high, low)


def turn_kernel(core_ref, hold_ref, got_ref, sums_ref, out_ref, weight_ref, bias_ref):
    core = core_ref[0]
    half = ROWS // 2
    for b in range(NB // 2):
        first = slice(b * HALF, (b + 1) * HALF)
        second = slice(half + b * HALF, half + (b + 1) * HALF)
        own = hold_ref[first, :] + got_ref[second, :]
        other = hold_ref[second, :] + got_ref[first, :]
        both = jnp.concatenate(
            [jnp.where(core == 0, own, other), jnp.where(core == 0, other, own)], axis=0
        )
        out_ref[b * BLK : (b + 1) * BLK, :] = both.T
    weight_ref[...] = sums_ref[:BLK, :] * NORM
    bias_ref[...] = sums_ref[BLK : BLK + 1, :] * NORM


def butterfly(value, target, size):
    step = 1
    while step < size:
        value = value + moved(value, functools.partial(target, step))
        step *= 2
    return value


def shards(features, weight, out_bias, edge_tiles, block_row, tile_slot, send_list, out_grad):
    bf16, f32, i32 = jnp.bfloat16, jnp.float32, jnp.int32
    node = lax.axis_index("nodes")
    core = lax.axis_index("rep")
    y, z, x = node // (NZ * NX), node // NX % NZ, node % NX
    core_array = jnp.reshape(core, (1,)).astype(i32)
    dma = pltpu.SemaphoreType.DMA

    local_rows = block_row - node * NB
    packed = jnp.pad(tile_slot * NB + local_rows, (0, BLK - 64))
    own_meta = jnp.concatenate([packed[None, :], send_list.T], axis=0)
    other_meta = to_other_core(own_meta)
    tiles = jnp.concatenate([edge_tiles, to_other_core(edge_tiles)], axis=0)

    message, half_message = call(
        message_kernel,
        [struct((MSG + ROWS, BLK), bf16), struct((MSG, BLK), bf16)],
        [SMEM, VMEM, VMEM, VMEM],
        [VMEM] * 2,
        moved_bytes=500000,
    )(core_array, features, own_meta, other_meta)
    first, second = along_z(message, 1), along_z(message, 2)
    first, second = lax.optimization_barrier((first, second))
    across, third = along_z(second[:MSG], 2), along_z(second, 1)
    swapped = to_other_core(jnp.concatenate([first[ROWS:], second[ROWS:]], axis=0))
    swapped = [swapped[:MSG], swapped[MSG:], to_other_core(third[ROWS:])]
    column = [half_message, first[:MSG], second[:MSG], third[:MSG], across]
    for piece in swapped:
        column += [piece[MSG - ROWS :], piece[: MSG - ROWS]]
    column = jnp.concatenate(column, axis=0)

    both = jnp.concatenate([own_meta[0, :64], other_meta[0, :64]])
    rows = both % NB
    slot = both // NB
    source, which = slot // 2, slot % 2
    step_y = (source // (NZ * NX) - y) % NY
    step_z = (source // NX - z) % NZ
    step_x = (source - x) % NX
    dense = jnp.where(core == 0, step_y, step_x)
    sparse = jnp.where(core == 0, step_x, step_y)
    step_z = jnp.where(core == 0, (NZ - step_z) % NZ, step_z)
    step_z = jnp.where(step_z <= 4, step_z, 12 - step_z)
    holder = jnp.where(jnp.arange(TILES) < 64, core, 1 - core)
    code = (dense * 4 + sparse) * 128 + (dense * NZ + step_z) * 4 + holder * 2 + which
    info, *requests = call(
        plan_kernel,
        [struct((INFO,), i32)] + [struct((128,), i32)] * 3,
        [SMEM] * 2,
        [SMEM] * 4,
        [pltpu.SMEM((8,), i32)],
        moved_bytes=100000,
    )(code.astype(i32), rows)
    requests = [along_sparse(requests[k - 1], k) for k in (1, 2, 3)]

    column, *requests = lax.optimization_barrier((column, *requests))
    parts = [column] + [along_dense(column, -j) for j in range(1, 4)]

    away = jnp.arange(4)
    asker = jnp.where(
        core == 0,
        node - x + (x - away) % NX,
        node - y * (NZ * NX) + (y - away) % NY * (NZ * NX),
    )
    lists = jnp.stack([part.reshape(NZ, MSG, BLK)[:, ROWS : ROWS + 4] for part in parts])
    chosen = (jnp.arange(BLK)[:, None] == asker[None, :]).astype(bf16)
    table = jnp.dot(lists.reshape(4 * NZ * 4, BLK), chosen, preferred_element_type=f32)
    table = table.astype(i32).reshape(-1)

    picked = call(
        pick_kernel,
        [struct((FAR, BLK), bf16)] * 3,
        [VMEM] * 4 + [ANY] * 4,
        [VMEM] * 3,
        [pltpu.SMEM((128,), i32)] * 3 + [pltpu.SMEM((512,), i32), dma((4,))],
        moved_bytes=7000000,
    )(*parts, *requests, table)
    far = [along_sparse(picked[k - 1], -k) for k in (1, 2, 3)]

    near = call(
        near_kernel,
        struct((ROWS, BLK), f32),
        [VMEM] * 5 + [ANY] * 2,
        VMEM,
        [
            pltpu.VMEM((ROWS + HALF, BLK), f32),
            pltpu.SMEM((INFO,), i32),
            pltpu.SMEM((512,), i32),
            dma((2,)),
        ],
        flops=2 * 32 * HALF * BLK * BLK,
        moved_bytes=11000000,
    )(*parts, tiles, info, table)
    agg_half = call(
        far_kernel,
        struct((ROWS, BLK), bf16),
        [VMEM] * 5 + [ANY],
        VMEM,
        [pltpu.VMEM((ROWS + HALF, BLK), f32), pltpu.SMEM((INFO,), i32), dma((1,))],
        flops=2 * 96 * HALF * BLK * BLK,
        moved_bytes=7000000,
    )(near, *far, tiles, info)
    other_half = to_other_core(agg_half)

    activations, sums, turned, second_back = call(
        middle_kernel,
        [
            struct((NB * BLK, BLK), bf16),
            struct((SUMS, BLK), f32),
            struct((ROWS, BLK), bf16),
            struct((FAR, BLK), bf16),
        ],
        [SMEM] + [VMEM] * 6 + [ANY],
        [VMEM] * 4,
        [pltpu.SMEM((INFO,), i32), dma((1,))],
        flops=2 * TILES * HALF * BLK * BLK,
        moved_bytes=8000000,
    )(
        core_array, agg_half, other_half, weight, out_bias[None, :], out_grad, tiles, info
    )
    first_back, third_back = call(
        side_kernel,
        [struct((FAR, BLK), bf16)] * 2,
        [VMEM] * 2 + [ANY],
        [VMEM] * 2,
        [pltpu.SMEM((INFO,), i32), dma((1,))],
        flops=2 * 64 * HALF * BLK * BLK,
        moved_bytes=4000000,
    )(tiles, turned, info)
    second_back = along_sparse(second_back, 2)
    back = [along_sparse(first_back, 1), second_back, along_sparse(third_back, 3)]

    sums = butterfly(sums, lambda step, y, z, x, c: (y, z ^ step, x, c), NZ)
    owned = call(
        owner_kernel,
        [struct((SEND, BLK), bf16)] + [struct((SEND + 2 * SUMS, BLK), bf16)] * 3,
        [ANY] * 5 + [VMEM] * 6,
        [VMEM] * 4,
        [
            pltpu.VMEM((257 * HALF, BLK), f32),
            pltpu.SMEM((INFO,), i32),
            pltpu.SMEM((512,), i32),
        ]
        + [pltpu.SMEM((128,), i32)] * 3
        + [dma((5,))],
        flops=2 * 32 * HALF * BLK * BLK,
        moved_bytes=11000000,
        vmem=21,
    )(info, table, *requests, turned, tiles, *back, sums)
    owned = [owned[0]] + [along_dense(owned[j], j) for j in range(1, 4)]
    keep, opposite, mine, swap, sums = call(
        split_sum_kernel,
        [struct((ROWS, BLK), bf16)] * 2
        + [struct((3 * ROWS, BLK), bf16)] * 2
        + [struct((SUMS, BLK), f32)],
        [SMEM] + [VMEM] * 5,
        [VMEM] * 5,
        moved_bytes=5000000,
    )(jnp.reshape(jnp.where(core == 0, y, x) % 2, (1,)).astype(i32), *owned, sums)
    opposite = along_z(opposite, 4)
    swap = to_other_core(swap)
    pieces = [
        jnp.concatenate([mine[s * ROWS : (s + 1) * ROWS], swap[s * ROWS : (s + 1) * ROWS]], axis=0)
        for s in range(3)
    ]
    pieces = [along_z(pieces[s - 1], -s) for s in (3, 2, 1)][::-1]
    sums = butterfly(sums, lambda step, y, z, x, c: (y, z, x ^ step, c) if c == 0 else (y ^ step, z, x, c), NX)

    hold, send, sums = call(
        last_sum_kernel,
        [struct((ROWS, BLK), f32)] * 2 + [struct((SUMS, BLK), f32)],
        [SMEM] + [VMEM] * 6,
        [VMEM] * 3,
        moved_bytes=1500000,
    )(core_array, sums, keep, opposite, *pieces)
    feature_grad, weight_grad, bias_grad = call(
        turn_kernel,
        [struct((NB // 2 * BLK, BLK), f32), struct((BLK, BLK), f32), struct((1, BLK), f32)],
        [SMEM] + [VMEM] * 3,
        [VMEM] * 3,
        moved_bytes=1000000,
    )(core_array, hold, to_other_core(send), sums)

    def again(state):
        return (jnp.float32(0.0),) + general_shards(
            features, weight, out_bias, edge_tiles, block_row, tile_slot, send_list, out_grad
        )

    state = (sums[BLK + 1, 0], activations, feature_grad, weight_grad, bias_grad.reshape(-1))
    return lax.while_loop(lambda state: state[0] > 0.5, again, state)[1:]


def solution(mesh):
    placed = (
        P("nodes", None),
        P(),
        P(),
        P(("nodes", "rep"), None, None),
        P(("nodes", "rep")),
        P(("nodes", "rep")),
        P(("nodes", "rep"), None),
        P("nodes", None),
    )
    return jax.shard_map(
        shards,
        mesh=mesh,
        in_specs=placed,
        out_specs=(P("nodes", "rep"), P(("nodes", "rep"), None), P(None, "rep"), P("rep")),
        check_vma=False,
    )
```

```python
import functools
import math

import jax
import jax.numpy as jnp
from jax import lax
from jax.experimental import pallas as pl
from jax.experimental.pallas import tpu as pltpu
from jax.sharding import PartitionSpec as P

ROOT_TWO_PI = 0.7978845608028654
CUBIC_TERM = 0.044715

NY, NZ, NX = 4, 8, 4
BLK = 128
HALF = 64
NB = 8
CAP = 56
ROWS = NB * HALF
MSG = ROWS + 16
PART = NZ * MSG
LOCAL = NY * PART
TILES = 128
LOC0, REM0, CNT0, OVER, ROW0 = 128, 256, 440, 444, 512
INFO = 640
SUMS = BLK + 16
SEND = 64 * HALF


def gelu_value(values):
    inner_term = ROOT_TWO_PI * (values + CUBIC_TERM * values * values * values)
    return 0.5 * values * (1.0 + jnp.tanh(inner_term))


def gelu_slope(values):
    tangent = jnp.tanh(ROOT_TWO_PI * (values + CUBIC_TERM * values * values * values))
    outer_part = 0.5 * values * (1.0 - tangent * tangent) * ROOT_TWO_PI
    return 0.5 * (1.0 + tangent) + outer_part * (1.0 + 3.0 * CUBIC_TERM * values * values)


def general_shards(features, weight, out_bias, edge_tiles, block_row, tile_slot, send_list, out_grad):
    node_count = lax.axis_size("nodes")
    rep_count = lax.axis_size("rep")
    rep_position = lax.axis_index("rep")
    block_size = edge_tiles.shape[1]
    local_blocks = features.shape[0] // block_size
    width_in = features.shape[1]
    capacity = send_list.shape[1]
    half_out = weight.shape[1] // rep_count
    feature_blocks = features.reshape(local_blocks, block_size, width_in)
    outgoing = feature_blocks[send_list]
    incoming = lax.all_to_all(outgoing, "nodes", split_axis=0, concat_axis=0, tiled=True)
    incoming = incoming.reshape(node_count * capacity, block_size, width_in)
    picked = incoming[tile_slot]
    products = jnp.einsum("tij,tjf->tif", edge_tiles, picked, preferred_element_type=jnp.float32)
    local_rows = block_row - lax.axis_index("nodes") * local_blocks
    partial_value = jax.ops.segment_sum(products, local_rows, num_segments=local_blocks)
    partial_value = partial_value.reshape(local_blocks * block_size, width_in)
    aggregate_bf = lax.psum(partial_value, "rep").astype(jnp.bfloat16)
    preact = jnp.dot(aggregate_bf, weight, preferred_element_type=jnp.float32) + out_bias
    own_preact = lax.dynamic_slice_in_dim(preact, rep_position * half_out, half_out, 1)
    activations = gelu_value(own_preact).astype(jnp.bfloat16)
    pre_grad = (out_grad.astype(jnp.float32) * gelu_slope(preact)).astype(jnp.bfloat16)
    agg_grad = lax.dot_general(
        pre_grad, weight, (((1,), (1,)), ((), ())), preferred_element_type=jnp.float32
    ).astype(jnp.bfloat16)
    grad_rows = agg_grad.reshape(local_blocks, block_size, width_in)[local_rows]
    back_products = jnp.einsum(
        "tji,tjf->tif", edge_tiles, grad_rows, preferred_element_type=jnp.float32
    )
    slot_sums = jax.ops.segment_sum(back_products, tile_slot, num_segments=node_count * capacity)
    slot_sums = slot_sums.astype(jnp.bfloat16)
    returned = lax.all_to_all(
        slot_sums.reshape(node_count, capacity, block_size, width_in),
        "nodes",
        split_axis=0,
        concat_axis=0,
        tiled=True,
    )
    returned = returned.astype(jnp.float32)
    owner_sums = jax.ops.segment_sum(
        returned.reshape(node_count * capacity, block_size, width_in),
        send_list.reshape(-1),
        num_segments=local_blocks,
    )
    feature_grad = lax.psum_scatter(
        owner_sums.reshape(local_blocks * block_size, width_in).astype(jnp.bfloat16),
        "rep",
        scatter_dimension=0,
        tiled=True,
    ).astype(jnp.float32)
    own_grad = lax.dynamic_slice_in_dim(pre_grad, rep_position * half_out, half_out, 1)
    norm_scale = 1.0 / math.sqrt(features.shape[0] * node_count)
    weight_part = lax.dot_general(
        aggregate_bf, own_grad, (((0,), (0,)), ((), ())), preferred_element_type=jnp.float32
    )
    bias_part = jnp.sum(own_grad.astype(jnp.float32), axis=0)
    weight_sum, bias_sum = lax.psum((weight_part, bias_part), "nodes")
    return (activations, feature_grad, weight_sum * norm_scale, bias_sum * norm_scale)


def device_of(y, z, x, c):
    return ((y % NY * NZ + z % NZ) * NX + x % NX) * 2 + c


def moved(value, target):
    pairs = [
        (device_of(y, z, x, c), device_of(*target(y, z, x, c)))
        for y in range(NY)
        for z in range(NZ)
        for x in range(NX)
        for c in range(2)
    ]
    return lax.ppermute(value, ("nodes", "rep"), pairs)


def along_z(value, step):
    return moved(value, lambda y, z, x, c: (y, z + step if c == 0 else z - step, x, c))


def along_dense(value, step):
    return moved(value, lambda y, z, x, c: (y + step, z, x, c) if c == 0 else (y, z, x + step, c))


def along_sparse(value, step):
    return moved(value, lambda y, z, x, c: (y, z, x + step, c) if c == 0 else (y + step, z, x, c))


def to_other_core(value):
    return moved(value, lambda y, z, x, c: (y, z, x, 1 - c))


SMEM = pl.BlockSpec(memory_space=pltpu.SMEM)
VMEM = pl.BlockSpec(memory_space=pltpu.VMEM)
ANY = pl.BlockSpec(memory_space=pl.ANY)


def call(kernel, out_shape, in_specs, out_specs, scratch=(), flops=0, moved_bytes=0, vmem=12):
    return pl.pallas_call(
        kernel,
        out_shape=out_shape,
        in_specs=in_specs,
        out_specs=out_specs,
        scratch_shapes=list(scratch),
        compiler_params=pltpu.CompilerParams(vmem_limit_bytes=vmem << 20),
        cost_estimate=pl.CostEstimate(flops=flops, bytes_accessed=moved_bytes, transcendentals=0),
    )


def struct(shape, dtype):
    return jax.ShapeDtypeStruct(shape, dtype)


def message_kernel(core_ref, features_ref, own_ref, other_ref, out_ref, half_ref):
    core = core_ref[0]
    for block in range(NB):
        turned = features_ref[block * BLK : (block + 1) * BLK, :].astype(jnp.float32).T
        mine = jnp.where(core == 0, turned[:HALF], turned[HALF:]).astype(jnp.bfloat16)
        rest = jnp.where(core == 0, turned[HALF:], turned[:HALF]).astype(jnp.bfloat16)
        out_ref[block * HALF : (block + 1) * HALF, :] = mine
        half_ref[block * HALF : (block + 1) * HALF, :] = mine
        out_ref[MSG + block * HALF : MSG + (block + 1) * HALF, :] = rest
    own, other = own_ref[1:3, :], other_ref[1:3, :]
    lists = jnp.concatenate(
        [
            jnp.where(core == 0, own, other),
            jnp.where(core == 0, other, own),
            jnp.zeros((12, BLK), jnp.int32),
        ],
        axis=0,
    )
    lists = lists.astype(jnp.float32).astype(jnp.bfloat16)
    out_ref[ROWS:MSG, :] = lists
    half_ref[ROWS:MSG, :] = lists


def plan_kernel(code_ref, rows_ref, info_ref, first_ref, second_ref, third_ref, count_ref):
    requests = (first_ref, second_ref, third_ref)
    for k in range(8):
        count_ref[k] = 0

    def clear(i, carry):
        for ref in requests:
            ref[i] = 0
        info_ref[i] = 0
        info_ref[LOC0 + i] = 0
        info_ref[REM0 + i] = 0
        info_ref[REM0 + 128 + i] = 0
        info_ref[ROW0 + i] = rows_ref[i]
        return carry

    lax.fori_loop(0, 128, clear, 0)

    def place(t, carry):
        code = code_ref[t]
        other_key = code // 512
        key = code // 128 % 4
        slot = code % 128
        count_ref[4 + other_key] = count_ref[4 + other_key] + 1
        rank = count_ref[key]
        count_ref[key] = rank + 1

        @pl.when(key == 0)
        def _():
            info_ref[rank] = slot
            info_ref[LOC0 + rank] = t

        @pl.when(jnp.logical_and(key > 0, rank < CAP))
        def _():
            info_ref[REM0 + (key - 1) * CAP + rank] = t
            for k in (1, 2, 3):

                @pl.when(key == k)
                def _():
                    requests[k - 1][rank] = slot + 128 * rows_ref[t]

        return carry

    lax.fori_loop(0, TILES, place, 0)
    over = 0
    info_ref[CNT0] = count_ref[0]
    for k in (1, 2, 3):
        kept = jnp.minimum(count_ref[k], CAP)
        info_ref[CNT0 + k] = kept
        requests[k - 1][64] = kept
        over += count_ref[k] - kept
        over += jnp.maximum(count_ref[4 + k] - CAP, 0)
    info_ref[OVER] = over


def start_all(pairs, sem):
    copies = [pltpu.make_async_copy(src, dst, sem.at[n]) for n, (src, dst) in enumerate(pairs)]
    for copy in copies:
        copy.start()
    return copies


def wait_all(copies):
    for copy in copies:
        copy.wait()


def half_rows(index):
    return pl.ds(pl.multiple_of(index * HALF, HALF), HALF)


def local_block(parts, slot, table, k):
    at = pl.ds(pl.multiple_of(slot // 4 % NZ * MSG + table[slot * 4 + k] * HALF, 16), HALF)
    part = slot // (4 * NZ)
    low = jnp.where(part == 0, parts[0][at, :], parts[1][at, :])
    high = jnp.where(part == 2, parts[2][at, :], parts[3][at, :])
    return jnp.where(part < 2, low, high)


def pick_kernel(own_ref, other_ref, info_ref, o1, o2, o3, info, sem):
    wait_all(start_all([(info_ref, info)], sem))
    for k, out in ((2, o2), (1, o1), (3, o3)):

        def body(i, carry, k=k, out=out):
            for u in range(8):
                p = i * 8 + u
                out[p] = chip_tile(own_ref, other_ref, info[REM0 + (k - 1) * CAP + p])
            return carry

        lax.fori_loop(0, (info[CNT0 + k] + 7) // 8, body, 0)


def chip_tile(own_ref, other_ref, t):
    return jnp.where(t < 64, own_ref[jnp.minimum(t, 63)], other_ref[jnp.maximum(t - 64, 0)])


def each_tile(own_ref, other_ref, moved_tiles, requests, info, act):
    count = info[CNT0]

    def near(i, carry):
        group = []
        for u in range(8):
            p = i * 8 + u
            t = info[LOC0 + p]
            group.append((p < count, info[p], info[ROW0 + t], chip_tile(own_ref, other_ref, t)))
        act(0, group)
        return carry

    lax.fori_loop(0, (count + 7) // 8, near, 0)
    for k, (tiles, request) in enumerate(zip(moved_tiles, requests), start=1):
        kept = request[64]

        def far(i, carry, k=k, tiles=tiles, request=request, kept=kept):
            group = []
            for u in range(8):
                p = i * 8 + u
                group.append((p < kept, request[p] % 128, request[p] // 128, tiles[p]))
            act(k, group)
            return carry

        lax.fori_loop(0, (kept + 7) // 8, far, 0)


def forward_kernel(
    a_ref, b_ref, c_ref, d_ref, own_ref, other_ref, g1, g2, g3, info_ref, table_ref, first_ref,
    second_ref, third_ref, p0, p1, p2, p3, acc, info, table, q1, q2, q3, sem,
):
    parts = (a_ref, b_ref, c_ref, d_ref)
    copies = start_all(
        [(info_ref, info), (table_ref, table), (first_ref, q1), (second_ref, q2), (third_ref, q3)],
        sem,
    )
    acc[...] = jnp.zeros_like(acc)
    wait_all(copies)

    def act(k, group):
        done = [
            lax.dot_general(
                local_block(parts, slot, table, k), tile, (((1,), (1,)), ((), ())),
                preferred_element_type=jnp.float32,
            )
            for _, slot, _, tile in group
        ]
        for value, (used, _, row, _) in zip(done, group):
            acc[half_rows(k * (NB + 1) + jnp.where(used, row, NB)), :] += value

    each_tile(own_ref, other_ref, (g1, g2, g3), (q1, q2, q3), info, act)
    for k, out in enumerate((p0, p1, p2, p3)):
        first = k * (NB + 1) * HALF
        out[...] = acc[first : first + ROWS, :].astype(out.dtype)


def middle_kernel(
    core_ref, own_agg, other_agg, weight_ref, bias_ref, grad_ref, info_ref,
    act_ref, turned_ref, sums_ref, info, sem,
):
    copies = start_all([(info_ref, info)], sem)
    core = core_ref[0]
    sums_ref[...] = jnp.zeros_like(sums_ref)
    weight_half = weight_ref[half_rows(core), :]

    def block_step(b, carry):
        own, other = own_agg[half_rows(b), :], other_agg[half_rows(b), :]
        low = jnp.where(core == 0, own, other)
        high = jnp.where(core == 0, other, own)
        agg = jnp.concatenate([low, high], axis=0)
        preact = lax.dot_general(
            agg, weight_ref[...], (((0,), (0,)), ((), ())), preferred_element_type=jnp.float32
        )
        preact = preact + bias_ref[...]
        tangent = jnp.tanh(ROOT_TWO_PI * (preact + CUBIC_TERM * preact * preact * preact))
        nodes = pl.ds(pl.multiple_of(b * BLK, BLK), BLK)
        value = 0.5 * preact * (1.0 + tangent)
        act_ref[nodes, :] = jnp.where(core == 0, value[:, :BLK], value[:, BLK:]).astype(jnp.bfloat16)
        outer = 0.5 * preact * (1.0 - tangent * tangent) * ROOT_TWO_PI
        slope = 0.5 * (1.0 + tangent) + outer * (1.0 + 3.0 * CUBIC_TERM * preact * preact)
        pre = (grad_ref[nodes, :].astype(jnp.float32) * slope).astype(jnp.bfloat16)
        turned_ref[half_rows(b), :] = lax.dot_general(
            weight_half, pre, (((1,), (1,)), ((), ())), preferred_element_type=jnp.float32
        ).astype(jnp.bfloat16)
        mine = jnp.where(core == 0, pre[:, :BLK], pre[:, BLK:])
        sums_ref[:BLK, :] += lax.dot_general(
            agg, mine, (((1,), (0,)), ((), ())), preferred_element_type=jnp.float32
        )
        sums_ref[BLK : BLK + 1, :] += jnp.sum(mine.astype(jnp.float32), axis=0, keepdims=True)
        return carry

    lax.fori_loop(0, NB, block_step, 0, unroll=2)
    wait_all(copies)
    over = info[OVER].astype(jnp.float32)
    sums_ref[BLK + 1 : BLK + 2, :] = jnp.full((1, BLK), over, jnp.float32)
    upper, lower = two_parts(sums_ref[...])
    turned_ref[ROWS : ROWS + SUMS, :] = upper
    turned_ref[ROWS + SUMS :, :] = lower


NORM = 1.0 / math.sqrt(NY * NZ * NX * NB * BLK)


def two_parts(value):
    upper = value.astype(jnp.bfloat16)
    return upper, (value - upper.astype(jnp.float32)).astype(jnp.bfloat16)


def whole(ref):
    upper, lower = ref[ROWS : ROWS + SUMS, :], ref[ROWS + SUMS :, :]
    return upper.astype(jnp.float32) + lower.astype(jnp.float32)


def back_kernel(
    odd_ref, info_ref, table_ref, first_ref, second_ref, third_ref, own_ref, other_ref, g1, g2, g3,
    t0, t1, t2, t3, o0, o1, o2, o3, sums_ref, total, info, table, q1, q2, q3, sem,
):
    copies = start_all(
        [(info_ref, info), (table_ref, table), (first_ref, q1), (second_ref, q2), (third_ref, q3)],
        sem,
    )
    total[...] = jnp.zeros_like(total)
    turned = (t0, t1, t2, t3)
    odd = odd_ref[0] == 1
    one, two, three = whole(t1), whole(t2), whole(t3)
    sums_ref[...] = (whole(t0) + jnp.where(odd, one, three)) + (two + jnp.where(odd, three, one))
    wait_all(copies)

    def act(k, group):
        done = [
            jnp.dot(turned[k][half_rows(row), :], tile, preferred_element_type=jnp.float32)
            for _, _, row, tile in group
        ]
        for value, (used, slot, _, _) in zip(done, group):
            index = jnp.where(used, slot // 4 * NB + table[slot * 4 + k], 256)
            total[half_rows(index), :] += value

    each_tile(own_ref, other_ref, (g1, g2, g3), (q1, q2, q3), info, act)
    for j, out in enumerate((o0, o1, o2, o3)):
        out[...] = total[j * SEND : (j + 1) * SEND, :].astype(jnp.bfloat16)


def split_sum_kernel(
    a_ref, b_ref, c_ref, d_ref, sums_ref, keep_ref, far_ref, mine_ref, swap_ref, passed_ref
):
    passed_ref[...] = sums_ref[...]
    for m in range(NZ):
        at = slice(m * ROWS, (m + 1) * ROWS)
        value = a_ref[at, :].astype(jnp.float32) + b_ref[at, :].astype(jnp.float32)
        value = value + (c_ref[at, :].astype(jnp.float32) + d_ref[at, :].astype(jnp.float32))
        value = value.astype(jnp.bfloat16)
        if m == 0:
            keep_ref[...] = value
        elif m < 4:
            mine_ref[(m - 1) * ROWS : m * ROWS, :] = value
        elif m == 4:
            far_ref[...] = value
        else:
            swap_ref[(m - 5) * ROWS : (m - 4) * ROWS, :] = value


def last_sum_kernel(
    core_ref, sums_ref, keep_ref, far_ref, a_ref, b_ref, c_ref, hold_ref, send_ref, passed_ref
):
    passed_ref[...] = sums_ref[...]
    core = core_ref[0]
    half = ROWS // 2

    def total(first):
        at = slice(first, first + half)
        value = a_ref[at, :].astype(jnp.float32) + b_ref[at, :].astype(jnp.float32)
        value = value + c_ref[at, :].astype(jnp.float32)
        if first < ROWS:
            value = value + keep_ref[at, :].astype(jnp.float32) + far_ref[at, :].astype(jnp.float32)
        return value

    for n in range(2):
        low, high = total(n * ROWS), total(n * ROWS + half)
        at = slice(n * half, (n + 1) * half)
        hold_ref[at, :] = jnp.where(core == 0, low, high)
        send_ref[at, :] = jnp.where(core == 0, high, low)


def turn_kernel(core_ref, hold_ref, got_ref, sums_ref, out_ref, weight_ref, bias_ref):
    core = core_ref[0]
    half = ROWS // 2
    for b in range(NB // 2):
        first = slice(b * HALF, (b + 1) * HALF)
        second = slice(half + b * HALF, half + (b + 1) * HALF)
        own = hold_ref[first, :] + got_ref[second, :]
        other = hold_ref[second, :] + got_ref[first, :]
        both = jnp.concatenate(
            [jnp.where(core == 0, own, other), jnp.where(core == 0, other, own)], axis=0
        )
        out_ref[b * BLK : (b + 1) * BLK, :] = both.T
    weight_ref[...] = sums_ref[:BLK, :] * NORM
    bias_ref[...] = sums_ref[BLK : BLK + 1, :] * NORM


def butterfly(value, target, size):
    step = 1
    while step < size:
        value = value + moved(value, functools.partial(target, step))
        step *= 2
    return value


def shards(features, weight, out_bias, edge_tiles, block_row, tile_slot, send_list, out_grad):
    bf16, f32, i32 = jnp.bfloat16, jnp.float32, jnp.int32
    node = lax.axis_index("nodes")
    core = lax.axis_index("rep")
    y, z, x = node // (NZ * NX), node // NX % NZ, node % NX
    core_array = jnp.reshape(core, (1,)).astype(i32)
    dma = pltpu.SemaphoreType.DMA

    local_rows = block_row - node * NB
    packed = jnp.pad(tile_slot * NB + local_rows, (0, BLK - 64))
    own_meta = jnp.concatenate([packed[None, :], send_list.T], axis=0)
    other_meta = to_other_core(own_meta)
    other_tiles = to_other_core(edge_tiles)

    message, half_message = call(
        message_kernel,
        [struct((MSG + ROWS, BLK), bf16), struct((MSG, BLK), bf16)],
        [SMEM, VMEM, VMEM, VMEM],
        [VMEM] * 2,
        moved_bytes=500000,
    )(core_array, features, own_meta, other_meta)
    first, second = along_z(message, 1), along_z(message, 2)
    first, second = lax.optimization_barrier((first, second))
    across, third = along_z(second[:MSG], 2), along_z(second, 1)
    swapped = to_other_core(jnp.concatenate([first[ROWS:], second[ROWS:]], axis=0))
    swapped = [swapped[:MSG], swapped[MSG:], to_other_core(third[ROWS:])]
    column = [half_message, first[:MSG], second[:MSG], third[:MSG], across]
    for piece in swapped:
        column += [piece[MSG - ROWS :], piece[: MSG - ROWS]]
    column = jnp.concatenate(column, axis=0)

    both = jnp.concatenate([own_meta[0, :64], other_meta[0, :64]])
    rows = both % NB
    slot = both // NB
    source, which = slot // 2, slot % 2
    step_y = (source // (NZ * NX) - y) % NY
    step_z = (source // NX - z) % NZ
    step_x = (source - x) % NX
    dense = jnp.where(core == 0, step_y, step_x)
    sparse = jnp.where(core == 0, step_x, step_y)
    step_z = jnp.where(core == 0, (NZ - step_z) % NZ, step_z)
    step_z = jnp.where(step_z <= 4, step_z, 12 - step_z)
    holder = jnp.where(jnp.arange(TILES) < 64, core, 1 - core)
    code = (dense * 4 + sparse) * 128 + (dense * NZ + step_z) * 4 + holder * 2 + which
    info, *requests = call(
        plan_kernel,
        [struct((INFO,), i32)] + [struct((128,), i32)] * 3,
        [SMEM] * 2,
        [SMEM] * 4,
        [pltpu.SMEM((8,), i32)],
        moved_bytes=100000,
    )(code.astype(i32), rows)
    requests = [along_sparse(requests[k - 1], k) for k in (1, 2, 3)]

    picked = call(
        pick_kernel,
        [struct((CAP, BLK, BLK), bf16)] * 3,
        [VMEM] * 2 + [ANY],
        [VMEM] * 3,
        [pltpu.SMEM((INFO,), i32), dma((1,))],
        moved_bytes=7000000,
    )(edge_tiles, other_tiles, info)
    moved_tiles = [along_sparse(picked[k - 1], k) for k in (1, 2, 3)]

    column, *requests = lax.optimization_barrier((column, *requests))
    parts = [column] + [along_dense(column, -j) for j in range(1, 4)]

    away = jnp.arange(4)
    asker = jnp.where(
        core == 0,
        node - x + (x - away) % NX,
        node - y * (NZ * NX) + (y - away) % NY * (NZ * NX),
    )
    lists = jnp.stack([part.reshape(NZ, MSG, BLK)[:, ROWS : ROWS + 4] for part in parts])
    chosen = (jnp.arange(BLK)[:, None] == asker[None, :]).astype(bf16)
    table = jnp.dot(lists.reshape(4 * NZ * 4, BLK), chosen, preferred_element_type=f32)
    table = table.astype(i32).reshape(-1)

    request_scratch = [pltpu.SMEM((INFO,), i32), pltpu.SMEM((512,), i32)]
    request_scratch += [pltpu.SMEM((128,), i32)] * 3 + [dma((5,))]
    partial = call(
        forward_kernel,
        [struct((ROWS, BLK), f32)] + [struct((ROWS, BLK), bf16)] * 3,
        [VMEM] * 9 + [ANY] * 5,
        [VMEM] * 4,
        [pltpu.VMEM((4 * (ROWS + HALF), BLK), f32)] + request_scratch,
        flops=2 * TILES * HALF * BLK * BLK,
        moved_bytes=14000000,
        vmem=20,
    )(*parts, edge_tiles, other_tiles, *moved_tiles, info, table, *requests)
    returned = [along_sparse(partial[k], -k) for k in (1, 2, 3)]
    agg_half = partial[0] + returned[0].astype(f32) + returned[1].astype(f32)
    agg_half = (agg_half + returned[2].astype(f32)).astype(bf16)
    other_half = to_other_core(agg_half)

    activations, turned, _ = call(
        middle_kernel,
        [
            struct((NB * BLK, BLK), bf16),
            struct((ROWS + 2 * SUMS, BLK), bf16),
            struct((SUMS, BLK), f32),
        ],
        [SMEM] + [VMEM] * 5 + [ANY],
        [VMEM] * 3,
        [pltpu.SMEM((INFO,), i32), dma((1,))],
        flops=8 * NB * BLK * BLK * BLK,
        moved_bytes=2000000,
    )(core_array, agg_half, other_half, weight, out_bias[None, :], out_grad, info)
    turned = [turned] + [along_sparse(turned, k) for k in (1, 2, 3)]

    *owned, sums = call(
        back_kernel,
        [struct((SEND, BLK), bf16)] * 4 + [struct((SUMS, BLK), f32)],
        [SMEM] + [ANY] * 5 + [VMEM] * 9,
        [VMEM] * 5,
        [pltpu.VMEM((257 * HALF, BLK), f32)] + request_scratch,
        flops=2 * TILES * HALF * BLK * BLK,
        moved_bytes=14000000,
        vmem=28,
    )(
        jnp.reshape(jnp.where(core == 0, x, y) % 2, (1,)).astype(i32), info, table, *requests,
        edge_tiles, other_tiles, *moved_tiles, *turned,
    )
    sums = butterfly(sums, lambda step, y, z, x, c: (y, z ^ step, x, c), NZ)
    owned = [owned[0]] + [along_dense(owned[j], j) for j in range(1, 4)]
    keep, opposite, mine, swap, sums = call(
        split_sum_kernel,
        [struct((ROWS, BLK), bf16)] * 2
        + [struct((3 * ROWS, BLK), bf16)] * 2
        + [struct((SUMS, BLK), f32)],
        [VMEM] * 5,
        [VMEM] * 5,
        moved_bytes=5000000,
    )(*owned, sums)
    opposite = along_z(opposite, 4)
    swap = to_other_core(swap)
    pieces = [
        jnp.concatenate([mine[s * ROWS : (s + 1) * ROWS], swap[s * ROWS : (s + 1) * ROWS]], axis=0)
        for s in range(3)
    ]
    pieces = [along_z(pieces[s - 1], -s) for s in (3, 2, 1)][::-1]
    sums = butterfly(
        sums, lambda step, y, z, x, c: (y ^ step, z, x, c) if c == 0 else (y, z, x ^ step, c), NY
    )

    hold, send, sums = call(
        last_sum_kernel,
        [struct((ROWS, BLK), f32)] * 2 + [struct((SUMS, BLK), f32)],
        [SMEM] + [VMEM] * 6,
        [VMEM] * 3,
        moved_bytes=1500000,
    )(core_array, sums, keep, opposite, *pieces)
    feature_grad, weight_grad, bias_grad = call(
        turn_kernel,
        [struct((NB // 2 * BLK, BLK), f32), struct((BLK, BLK), f32), struct((1, BLK), f32)],
        [SMEM] + [VMEM] * 3,
        [VMEM] * 3,
        moved_bytes=1000000,
    )(core_array, hold, to_other_core(send), sums)

    def again(state):
        return (jnp.float32(0.0),) + general_shards(
            features, weight, out_bias, edge_tiles, block_row, tile_slot, send_list, out_grad
        )

    state = (sums[BLK + 1, 0], activations, feature_grad, weight_grad, bias_grad.reshape(-1))
    return lax.while_loop(lambda state: state[0] > 0.5, again, state)[1:]


def solution(mesh):
    placed = (
        P("nodes", None),
        P(),
        P(),
        P(("nodes", "rep"), None, None),
        P(("nodes", "rep")),
        P(("nodes", "rep")),
        P(("nodes", "rep"), None),
        P("nodes", None),
    )
    return jax.shard_map(
        shards,
        mesh=mesh,
        in_specs=placed,
        out_specs=(P("nodes", "rep"), P(("nodes", "rep"), None), P(None, "rep"), P("rep")),
        check_vma=False,
    )
```

```python
import functools
import math

import jax
import jax.numpy as jnp
from jax import lax
from jax.experimental import pallas as pl
from jax.experimental.pallas import tpu as pltpu
from jax.sharding import PartitionSpec as P

ROOT_TWO_PI = 0.7978845608028654
CUBIC_TERM = 0.044715

NY, NZ, NX = 4, 8, 4
BLK = 128
HALF = 64
NB = 8
CAP = 56
ROWS = NB * HALF
MSG = ROWS + 16
PART = NZ * MSG
LOCAL = NY * PART
TILES = 128
LOC0, REM0, CNT0, OVER, ROW0 = 128, 256, 440, 444, 512
INFO = 640
SUMS = BLK + 16
EARLY, LATE = (3, 4, 7), (0, 1, 2, 5, 6)


def gelu_value(values):
    inner_term = ROOT_TWO_PI * (values + CUBIC_TERM * values * values * values)
    return 0.5 * values * (1.0 + jnp.tanh(inner_term))


def gelu_slope(values):
    tangent = jnp.tanh(ROOT_TWO_PI * (values + CUBIC_TERM * values * values * values))
    outer_part = 0.5 * values * (1.0 - tangent * tangent) * ROOT_TWO_PI
    return 0.5 * (1.0 + tangent) + outer_part * (1.0 + 3.0 * CUBIC_TERM * values * values)


def general_shards(features, weight, out_bias, edge_tiles, block_row, tile_slot, send_list, out_grad):
    node_count = lax.axis_size("nodes")
    rep_count = lax.axis_size("rep")
    rep_position = lax.axis_index("rep")
    block_size = edge_tiles.shape[1]
    local_blocks = features.shape[0] // block_size
    width_in = features.shape[1]
    capacity = send_list.shape[1]
    half_out = weight.shape[1] // rep_count
    feature_blocks = features.reshape(local_blocks, block_size, width_in)
    outgoing = feature_blocks[send_list]
    incoming = lax.all_to_all(outgoing, "nodes", split_axis=0, concat_axis=0, tiled=True)
    incoming = incoming.reshape(node_count * capacity, block_size, width_in)
    picked = incoming[tile_slot]
    products = jnp.einsum("tij,tjf->tif", edge_tiles, picked, preferred_element_type=jnp.float32)
    local_rows = block_row - lax.axis_index("nodes") * local_blocks
    partial_value = jax.ops.segment_sum(products, local_rows, num_segments=local_blocks)
    partial_value = partial_value.reshape(local_blocks * block_size, width_in)
    aggregate_bf = lax.psum(partial_value, "rep").astype(jnp.bfloat16)
    preact = jnp.dot(aggregate_bf, weight, preferred_element_type=jnp.float32) + out_bias
    own_preact = lax.dynamic_slice_in_dim(preact, rep_position * half_out, half_out, 1)
    activations = gelu_value(own_preact).astype(jnp.bfloat16)
    pre_grad = (out_grad.astype(jnp.float32) * gelu_slope(preact)).astype(jnp.bfloat16)
    agg_grad = lax.dot_general(
        pre_grad, weight, (((1,), (1,)), ((), ())), preferred_element_type=jnp.float32
    ).astype(jnp.bfloat16)
    grad_rows = agg_grad.reshape(local_blocks, block_size, width_in)[local_rows]
    back_products = jnp.einsum(
        "tji,tjf->tif", edge_tiles, grad_rows, preferred_element_type=jnp.float32
    )
    slot_sums = jax.ops.segment_sum(back_products, tile_slot, num_segments=node_count * capacity)
    slot_sums = slot_sums.astype(jnp.bfloat16)
    returned = lax.all_to_all(
        slot_sums.reshape(node_count, capacity, block_size, width_in),
        "nodes",
        split_axis=0,
        concat_axis=0,
        tiled=True,
    )
    returned = returned.astype(jnp.float32)
    owner_sums = jax.ops.segment_sum(
        returned.reshape(node_count * capacity, block_size, width_in),
        send_list.reshape(-1),
        num_segments=local_blocks,
    )
    feature_grad = lax.psum_scatter(
        owner_sums.reshape(local_blocks * block_size, width_in).astype(jnp.bfloat16),
        "rep",
        scatter_dimension=0,
        tiled=True,
    ).astype(jnp.float32)
    own_grad = lax.dynamic_slice_in_dim(pre_grad, rep_position * half_out, half_out, 1)
    norm_scale = 1.0 / math.sqrt(features.shape[0] * node_count)
    weight_part = lax.dot_general(
        aggregate_bf, own_grad, (((0,), (0,)), ((), ())), preferred_element_type=jnp.float32
    )
    bias_part = jnp.sum(own_grad.astype(jnp.float32), axis=0)
    weight_sum, bias_sum = lax.psum((weight_part, bias_part), "nodes")
    return (activations, feature_grad, weight_sum * norm_scale, bias_sum * norm_scale)


def device_of(y, z, x, c):
    return ((y % NY * NZ + z % NZ) * NX + x % NX) * 2 + c


def moved(value, target):
    pairs = [
        (device_of(y, z, x, c), device_of(*target(y, z, x, c)))
        for y in range(NY)
        for z in range(NZ)
        for x in range(NX)
        for c in range(2)
    ]
    return lax.ppermute(value, ("nodes", "rep"), pairs)


def along_z(value, step):
    return moved(value, lambda y, z, x, c: (y, z + step if c == 0 else z - step, x, c))


def along_dense(value, step):
    return moved(value, lambda y, z, x, c: (y + step, z, x, c) if c == 0 else (y, z, x + step, c))


def along_sparse(value, step):
    return moved(value, lambda y, z, x, c: (y, z, x + step, c) if c == 0 else (y + step, z, x, c))


def to_other_core(value):
    return moved(value, lambda y, z, x, c: (y, z, x, 1 - c))


SMEM = pl.BlockSpec(memory_space=pltpu.SMEM)
VMEM = pl.BlockSpec(memory_space=pltpu.VMEM)
ANY = pl.BlockSpec(memory_space=pl.ANY)


def call(kernel, out_shape, in_specs, out_specs, scratch=(), flops=0, moved_bytes=0, vmem=12):
    return pl.pallas_call(
        kernel,
        out_shape=out_shape,
        in_specs=in_specs,
        out_specs=out_specs,
        scratch_shapes=list(scratch),
        compiler_params=pltpu.CompilerParams(vmem_limit_bytes=vmem << 20),
        cost_estimate=pl.CostEstimate(flops=flops, bytes_accessed=moved_bytes, transcendentals=0),
    )


def struct(shape, dtype):
    return jax.ShapeDtypeStruct(shape, dtype)


def message_kernel(core_ref, features_ref, own_ref, other_ref, out_ref, half_ref):
    core = core_ref[0]
    for block in range(NB):
        turned = features_ref[block * BLK : (block + 1) * BLK, :].astype(jnp.float32).T
        mine = jnp.where(core == 0, turned[:HALF], turned[HALF:]).astype(jnp.bfloat16)
        rest = jnp.where(core == 0, turned[HALF:], turned[:HALF]).astype(jnp.bfloat16)
        out_ref[block * HALF : (block + 1) * HALF, :] = mine
        half_ref[block * HALF : (block + 1) * HALF, :] = mine
        out_ref[MSG + block * HALF : MSG + (block + 1) * HALF, :] = rest
    own, other = own_ref[1:3, :], other_ref[1:3, :]
    lists = jnp.concatenate(
        [
            jnp.where(core == 0, own, other),
            jnp.where(core == 0, other, own),
            jnp.zeros((12, BLK), jnp.int32),
        ],
        axis=0,
    )
    lists = lists.astype(jnp.float32).astype(jnp.bfloat16)
    out_ref[ROWS:MSG, :] = lists
    half_ref[ROWS:MSG, :] = lists


def plan_kernel(code_ref, rows_ref, info_ref, first_ref, second_ref, third_ref, count_ref):
    requests = (first_ref, second_ref, third_ref)
    for k in range(8):
        count_ref[k] = 0

    def clear(i, carry):
        for ref in requests:
            ref[i] = 0
        info_ref[i] = 0
        info_ref[LOC0 + i] = 0
        info_ref[REM0 + i] = 0
        info_ref[REM0 + 128 + i] = 0
        info_ref[ROW0 + i] = rows_ref[i]
        return carry

    lax.fori_loop(0, 128, clear, 0)

    def place(t, carry):
        code = code_ref[t]
        other_key = code >> 9
        key = (code >> 7) & 3
        slot = code & 127
        count_ref[4 + other_key] = count_ref[4 + other_key] + 1
        rank = count_ref[key]
        count_ref[key] = rank + 1

        @pl.when(key == 0)
        def _():
            info_ref[rank] = slot
            info_ref[LOC0 + rank] = t

        @pl.when(jnp.logical_and(key > 0, rank < CAP))
        def _():
            info_ref[REM0 + (key - 1) * CAP + rank] = t
            for k in (1, 2, 3):

                @pl.when(key == k)
                def _():
                    requests[k - 1][rank] = slot + 128 * rows_ref[t]

        return carry

    lax.fori_loop(0, TILES, place, 0)
    over = 0
    info_ref[CNT0] = count_ref[0]
    for k in (1, 2, 3):
        kept = jnp.minimum(count_ref[k], CAP)
        info_ref[CNT0 + k] = kept
        requests[k - 1][64] = kept
        over += count_ref[k] - kept
        over += jnp.maximum(count_ref[4 + k] - CAP, 0)
    info_ref[OVER] = over


def start_all(pairs, sem):
    copies = [pltpu.make_async_copy(src, dst, sem.at[n]) for n, (src, dst) in enumerate(pairs)]
    for copy in copies:
        copy.start()
    return copies


def wait_all(copies):
    for copy in copies:
        copy.wait()


def half_rows(index):
    return pl.ds(pl.multiple_of(index * HALF, HALF), HALF)


def local_block(parts, slot, table, k):
    row = ((slot >> 2) & (NZ - 1)) * MSG + (table[(slot << 2) + k] << 6)
    at = pl.ds(pl.multiple_of(row, 16), HALF)
    part = slot >> 5
    low = jnp.where(part == 0, parts[0][at, :], parts[1][at, :])
    high = jnp.where(part == 2, parts[2][at, :], parts[3][at, :])
    return jnp.where(part < 2, low, high)


def pick_kernel(own_ref, other_ref, info_ref, o1, o2, o3, info, sem):
    wait_all(start_all([(info_ref, info)], sem))
    for k, out in ((2, o2), (1, o1), (3, o3)):

        def body(i, carry, k=k, out=out):
            for u in range(8):
                p = i * 8 + u
                out[p] = chip_tile(own_ref, other_ref, info[REM0 + (k - 1) * CAP + p])
            return carry

        lax.fori_loop(0, (info[CNT0 + k] + 7) >> 3, body, 0)


def chip_tile(own_ref, other_ref, t):
    return jnp.where(t < 64, own_ref[jnp.minimum(t, 63)], other_ref[jnp.maximum(t - 64, 0)])


def each_tile(own_ref, other_ref, moved_tiles, requests, info, act):
    count = info[CNT0]

    def near(i, carry):
        group = []
        for u in range(8):
            p = i * 8 + u
            t = info[LOC0 + p]
            group.append((p < count, info[p], info[ROW0 + t], chip_tile(own_ref, other_ref, t)))
        act(0, group)
        return carry

    lax.fori_loop(0, (count + 7) >> 3, near, 0)
    for k, (tiles, request) in enumerate(zip(moved_tiles, requests), start=1):
        kept = request[64]

        def far(i, carry, k=k, tiles=tiles, request=request, kept=kept):
            group = []
            for u in range(8):
                p = i * 8 + u
                group.append((p < kept, request[p] & 127, request[p] >> 7, tiles[p]))
            act(k, group)
            return carry

        lax.fori_loop(0, (kept + 7) >> 3, far, 0)


def forward_kernel(
    a_ref, b_ref, c_ref, d_ref, own_ref, other_ref, g1, g2, g3, info_ref, table_ref, first_ref,
    second_ref, third_ref, p0, p1, p2, p3, acc, info, table, q1, q2, q3, sem,
):
    parts = (a_ref, b_ref, c_ref, d_ref)
    copies = start_all(
        [(info_ref, info), (table_ref, table), (first_ref, q1), (second_ref, q2), (third_ref, q3)],
        sem,
    )
    acc[...] = jnp.zeros_like(acc)
    wait_all(copies)

    def act(k, group):
        done = [
            lax.dot_general(
                local_block(parts, slot, table, k), tile, (((1,), (1,)), ((), ())),
                preferred_element_type=jnp.float32,
            )
            for _, slot, _, tile in group
        ]
        for value, (used, _, row, _) in zip(done, group):
            acc[half_rows(k * (NB + 1) + jnp.where(used, row, NB)), :] += value

    each_tile(own_ref, other_ref, (g1, g2, g3), (q1, q2, q3), info, act)
    for k, out in enumerate((p0, p1, p2, p3)):
        first = k * (NB + 1) * HALF
        out[...] = acc[first : first + ROWS, :].astype(out.dtype)


def middle_kernel(
    core_ref, own_agg, other_agg, weight_ref, bias_ref, grad_ref, info_ref,
    act_ref, turned_ref, sums_ref, info, sem,
):
    copies = start_all([(info_ref, info)], sem)
    core = core_ref[0]
    sums_ref[...] = jnp.zeros_like(sums_ref)
    weight_half = weight_ref[half_rows(core), :]

    def block_step(b, carry):
        own, other = own_agg[half_rows(b), :], other_agg[half_rows(b), :]
        low = jnp.where(core == 0, own, other)
        high = jnp.where(core == 0, other, own)
        agg = jnp.concatenate([low, high], axis=0)
        preact = lax.dot_general(
            agg, weight_ref[...], (((0,), (0,)), ((), ())), preferred_element_type=jnp.float32
        )
        preact = preact + bias_ref[...]
        tangent = jnp.tanh(ROOT_TWO_PI * (preact + CUBIC_TERM * preact * preact * preact))
        nodes = pl.ds(pl.multiple_of(b * BLK, BLK), BLK)
        value = 0.5 * preact * (1.0 + tangent)
        act_ref[nodes, :] = jnp.where(core == 0, value[:, :BLK], value[:, BLK:]).astype(jnp.bfloat16)
        outer = 0.5 * preact * (1.0 - tangent * tangent) * ROOT_TWO_PI
        slope = 0.5 * (1.0 + tangent) + outer * (1.0 + 3.0 * CUBIC_TERM * preact * preact)
        pre = (grad_ref[nodes, :].astype(jnp.float32) * slope).astype(jnp.bfloat16)
        turned_ref[half_rows(b), :] = lax.dot_general(
            weight_half, pre, (((1,), (1,)), ((), ())), preferred_element_type=jnp.float32
        ).astype(jnp.bfloat16)
        mine = jnp.where(core == 0, pre[:, :BLK], pre[:, BLK:])
        sums_ref[:BLK, :] += lax.dot_general(
            agg, mine, (((1,), (0,)), ((), ())), preferred_element_type=jnp.float32
        )
        sums_ref[BLK : BLK + 1, :] += jnp.sum(mine.astype(jnp.float32), axis=0, keepdims=True)
        return carry

    lax.fori_loop(0, NB, block_step, 0, unroll=2)
    wait_all(copies)
    over = info[OVER].astype(jnp.float32)
    sums_ref[BLK + 1 : BLK + 2, :] = jnp.full((1, BLK), over, jnp.float32)
    upper, lower = two_parts(sums_ref[...])
    turned_ref[ROWS : ROWS + SUMS, :] = upper
    turned_ref[ROWS + SUMS :, :] = lower


NORM = 1.0 / math.sqrt(NY * NZ * NX * NB * BLK)


def two_parts(value):
    upper = value.astype(jnp.bfloat16)
    return upper, (value - upper.astype(jnp.float32)).astype(jnp.bfloat16)


def whole(ref):
    upper, lower = ref[ROWS : ROWS + SUMS, :], ref[ROWS + SUMS :, :]
    return upper.astype(jnp.float32) + lower.astype(jnp.float32)


def back_kernel(
    odd_ref, info_ref, table_ref, first_ref, second_ref, third_ref, own_ref, other_ref, g1, g2, g3,
    t0, t1, t2, t3, a0, a1, a2, a3, b0, b1, b2, b3, sums_ref, total, info, table, q1, q2, q3, sem,
):
    copies = start_all(
        [(info_ref, info), (table_ref, table), (first_ref, q1), (second_ref, q2), (third_ref, q3)],
        sem,
    )
    total[...] = jnp.zeros_like(total)
    turned = (t0, t1, t2, t3)
    odd = odd_ref[0] == 1
    one, two, three = whole(t1), whole(t2), whole(t3)
    sums_ref[...] = (whole(t0) + jnp.where(odd, one, three)) + (two + jnp.where(odd, three, one))
    wait_all(copies)

    def act(k, group):
        done = [
            jnp.dot(turned[k][half_rows(row), :], tile, preferred_element_type=jnp.float32)
            for _, _, row, tile in group
        ]
        for value, (used, slot, _, _) in zip(done, group):
            index = jnp.where(used, ((slot >> 2) << 3) + table[(slot << 2) + k], 256)
            total[half_rows(index), :] += value

    each_tile(own_ref, other_ref, (g1, g2, g3), (q1, q2, q3), info, act)
    for outs, places in (((a0, a1, a2, a3), EARLY), ((b0, b1, b2, b3), LATE)):
        for j, out in enumerate(outs):
            for n, m in enumerate(places):
                first = (j * NZ + m) * ROWS
                out[n * ROWS : (n + 1) * ROWS, :] = total[first : first + ROWS, :].astype(
                    jnp.bfloat16
                )


def four_sum(refs, n):
    a, b, c, d = (ref[n * ROWS : (n + 1) * ROWS, :].astype(jnp.float32) for ref in refs)
    return ((a + b) + (c + d)).astype(jnp.bfloat16)


def early_sum_kernel(a_ref, b_ref, c_ref, d_ref, mine_ref, far_ref, swap_ref):
    for n, out in enumerate((mine_ref, far_ref, swap_ref)):
        out[...] = four_sum((a_ref, b_ref, c_ref, d_ref), n)


def late_sum_kernel(
    a_ref, b_ref, c_ref, d_ref, sums_ref, keep_ref, mine_ref, swap_ref, passed_ref
):
    passed_ref[...] = sums_ref[...]
    refs = (a_ref, b_ref, c_ref, d_ref)
    keep_ref[...] = four_sum(refs, 0)
    for n in range(2):
        at = slice(n * ROWS, (n + 1) * ROWS)
        mine_ref[at, :] = four_sum(refs, 1 + n)
        swap_ref[at, :] = four_sum(refs, 3 + n)


def last_sum_kernel(
    core_ref, sums_ref, keep_ref, far_ref, a_ref, b_ref, c_ref, hold_ref, send_ref, passed_ref
):
    passed_ref[...] = sums_ref[...]
    core = core_ref[0]
    half = ROWS // 2

    def total(first):
        at = slice(first, first + half)
        value = a_ref[at, :].astype(jnp.float32) + b_ref[at, :].astype(jnp.float32)
        value = value + c_ref[at, :].astype(jnp.float32)
        if first < ROWS:
            value = value + keep_ref[at, :].astype(jnp.float32) + far_ref[at, :].astype(jnp.float32)
        return value

    for n in range(2):
        low, high = total(n * ROWS), total(n * ROWS + half)
        at = slice(n * half, (n + 1) * half)
        hold_ref[at, :] = jnp.where(core == 0, low, high)
        send_ref[at, :] = jnp.where(core == 0, high, low)


def turn_kernel(core_ref, hold_ref, got_ref, sums_ref, out_ref, weight_ref, bias_ref):
    core = core_ref[0]
    half = ROWS // 2
    for b in range(NB // 2):
        first = slice(b * HALF, (b + 1) * HALF)
        second = slice(half + b * HALF, half + (b + 1) * HALF)
        own = hold_ref[first, :] + got_ref[second, :]
        other = hold_ref[second, :] + got_ref[first, :]
        both = jnp.concatenate(
            [jnp.where(core == 0, own, other), jnp.where(core == 0, other, own)], axis=0
        )
        out_ref[b * BLK : (b + 1) * BLK, :] = both.T
    weight_ref[...] = sums_ref[:BLK, :] * NORM
    bias_ref[...] = sums_ref[BLK : BLK + 1, :] * NORM


def butterfly(value, target, size):
    step = 1
    while step < size:
        value = value + moved(value, functools.partial(target, step))
        step *= 2
    return value


def shards(features, weight, out_bias, edge_tiles, block_row, tile_slot, send_list, out_grad):
    bf16, f32, i32 = jnp.bfloat16, jnp.float32, jnp.int32
    node = lax.axis_index("nodes")
    core = lax.axis_index("rep")
    y, z, x = node // (NZ * NX), node // NX % NZ, node % NX
    core_array = jnp.reshape(core, (1,)).astype(i32)
    dma = pltpu.SemaphoreType.DMA

    local_rows = block_row - node * NB
    packed = jnp.pad(tile_slot * NB + local_rows, (0, BLK - 64))
    own_meta = jnp.concatenate([packed[None, :], send_list.T], axis=0)
    other_meta = to_other_core(own_meta)
    other_tiles = to_other_core(edge_tiles)

    message, half_message = call(
        message_kernel,
        [struct((MSG + ROWS, BLK), bf16), struct((MSG, BLK), bf16)],
        [SMEM, VMEM, VMEM, VMEM],
        [VMEM] * 2,
        moved_bytes=500000,
    )(core_array, features, own_meta, other_meta)
    first, second = along_z(message, 1), along_z(message, 2)

    both = jnp.concatenate([own_meta[0, :64], other_meta[0, :64]])
    rows = both % NB
    slot = both // NB
    source, which = slot // 2, slot % 2
    step_y = (source // (NZ * NX) - y) % NY
    step_z = (source // NX - z) % NZ
    step_x = (source - x) % NX
    dense = jnp.where(core == 0, step_y, step_x)
    sparse = jnp.where(core == 0, step_x, step_y)
    step_z = jnp.where(core == 0, (NZ - step_z) % NZ, step_z)
    step_z = jnp.where(step_z <= 4, step_z, 12 - step_z)
    holder = jnp.where(jnp.arange(TILES) < 64, core, 1 - core)
    code = (dense * 4 + sparse) * 128 + (dense * NZ + step_z) * 4 + holder * 2 + which
    info, *requests = call(
        plan_kernel,
        [struct((INFO,), i32)] + [struct((128,), i32)] * 3,
        [SMEM] * 2,
        [SMEM] * 4,
        [pltpu.SMEM((8,), i32)],
        moved_bytes=100000,
    )(code.astype(i32), rows)
    requests = [along_sparse(requests[k - 1], k) for k in (1, 2, 3)]

    picked = call(
        pick_kernel,
        [struct((CAP, BLK, BLK), bf16)] * 3,
        [VMEM] * 2 + [ANY],
        [VMEM] * 3,
        [pltpu.SMEM((INFO,), i32), dma((1,))],
        moved_bytes=7000000,
    )(edge_tiles, other_tiles, info)
    first, second, *picked = lax.optimization_barrier((first, second, *picked))
    moved_tiles = [along_sparse(picked[k - 1], k) for k in (1, 2, 3)]

    across, third = along_z(second[:MSG], 2), along_z(second, 1)
    swapped = to_other_core(
        jnp.concatenate([first[ROWS:], second[ROWS:], third[ROWS:]], axis=0)
    )
    column = [half_message, first[:MSG], second[:MSG], third[:MSG], across]
    for n in range(3):
        piece = swapped[n * MSG : (n + 1) * MSG]
        column += [piece[MSG - ROWS :], piece[: MSG - ROWS]]
    column = jnp.concatenate(column, axis=0)

    column, *requests = lax.optimization_barrier((column, *requests))
    parts = [column] + [along_dense(column, -j) for j in range(1, 4)]

    away = jnp.arange(4)
    asker = jnp.where(
        core == 0,
        node - x + (x - away) % NX,
        node - y * (NZ * NX) + (y - away) % NY * (NZ * NX),
    )
    lists = jnp.stack([part.reshape(NZ, MSG, BLK)[:, ROWS : ROWS + 4] for part in parts])
    chosen = (jnp.arange(BLK)[:, None] == asker[None, :]).astype(bf16)
    table = jnp.dot(lists.reshape(4 * NZ * 4, BLK), chosen, preferred_element_type=f32)
    table = table.astype(i32).reshape(-1)

    request_scratch = [pltpu.SMEM((INFO,), i32), pltpu.SMEM((512,), i32)]
    request_scratch += [pltpu.SMEM((128,), i32)] * 3 + [dma((5,))]
    partial = call(
        forward_kernel,
        [struct((ROWS, BLK), f32)] + [struct((ROWS, BLK), bf16)] * 3,
        [VMEM] * 9 + [ANY] * 5,
        [VMEM] * 4,
        [pltpu.VMEM((4 * (ROWS + HALF), BLK), f32)] + request_scratch,
        flops=2 * TILES * HALF * BLK * BLK,
        moved_bytes=14000000,
        vmem=20,
    )(*parts, edge_tiles, other_tiles, *moved_tiles, info, table, *requests)
    returned = [along_sparse(partial[k], -k) for k in (1, 2, 3)]
    agg_half = partial[0] + returned[0].astype(f32) + returned[1].astype(f32)
    agg_half = (agg_half + returned[2].astype(f32)).astype(bf16)
    other_half = to_other_core(agg_half)

    activations, turned, _ = call(
        middle_kernel,
        [
            struct((NB * BLK, BLK), bf16),
            struct((ROWS + 2 * SUMS, BLK), bf16),
            struct((SUMS, BLK), f32),
        ],
        [SMEM] + [VMEM] * 5 + [ANY],
        [VMEM] * 3,
        [pltpu.SMEM((INFO,), i32), dma((1,))],
        flops=8 * NB * BLK * BLK * BLK,
        moved_bytes=2000000,
    )(core_array, agg_half, other_half, weight, out_bias[None, :], out_grad, info)
    turned = [turned] + [along_sparse(turned, k) for k in (1, 2, 3)]

    *owned, sums = call(
        back_kernel,
        [struct((len(EARLY) * ROWS, BLK), bf16)] * 4
        + [struct((len(LATE) * ROWS, BLK), bf16)] * 4
        + [struct((SUMS, BLK), f32)],
        [SMEM] + [ANY] * 5 + [VMEM] * 9,
        [VMEM] * 9,
        [pltpu.VMEM((257 * HALF, BLK), f32)] + request_scratch,
        flops=2 * TILES * HALF * BLK * BLK,
        moved_bytes=14000000,
        vmem=28,
    )(
        jnp.reshape(jnp.where(core == 0, x, y) % 2, (1,)).astype(i32), info, table, *requests,
        edge_tiles, other_tiles, *moved_tiles, *turned,
    )
    sums = butterfly(sums, lambda step, y, z, x, c: (y, z ^ step, x, c), NZ)
    early = [owned[0]] + [along_dense(owned[j], j) for j in range(1, 4)]
    late = [owned[4]] + [along_dense(owned[4 + j], j) for j in range(1, 4)]
    mine, opposite, swap = call(
        early_sum_kernel,
        [struct((ROWS, BLK), bf16)] * 3,
        [VMEM] * 4,
        [VMEM] * 3,
        moved_bytes=2000000,
    )(*early)
    opposite = along_z(opposite, 4)
    third = along_z(jnp.concatenate([mine, to_other_core(swap)], axis=0), -3)
    keep, mine, swap, sums = call(
        late_sum_kernel,
        [struct((ROWS, BLK), bf16)]
        + [struct((2 * ROWS, BLK), bf16)] * 2
        + [struct((SUMS, BLK), f32)],
        [VMEM] * 5,
        [VMEM] * 4,
        moved_bytes=3000000,
    )(*late, sums)
    swap = to_other_core(swap)
    second = along_z(jnp.concatenate([mine[ROWS:], swap[ROWS:]], axis=0), -2)
    first = along_z(jnp.concatenate([mine[:ROWS], swap[:ROWS]], axis=0), -1)
    sums = butterfly(
        sums, lambda step, y, z, x, c: (y ^ step, z, x, c) if c == 0 else (y, z, x ^ step, c), NY
    )
    hold, send, sums = call(
        last_sum_kernel,
        [struct((ROWS, BLK), f32)] * 2 + [struct((SUMS, BLK), f32)],
        [SMEM] + [VMEM] * 6,
        [VMEM] * 3,
        moved_bytes=1500000,
    )(core_array, sums, keep, opposite, first, second, third)
    feature_grad, weight_grad, bias_grad = call(
        turn_kernel,
        [struct((NB // 2 * BLK, BLK), f32), struct((BLK, BLK), f32), struct((1, BLK), f32)],
        [SMEM] + [VMEM] * 3,
        [VMEM] * 3,
        moved_bytes=1000000,
    )(core_array, hold, to_other_core(send), sums)

    def again(state):
        return (jnp.float32(0.0),) + general_shards(
            features, weight, out_bias, edge_tiles, block_row, tile_slot, send_list, out_grad
        )

    state = (sums[BLK + 1, 0], activations, feature_grad, weight_grad, bias_grad.reshape(-1))
    return lax.while_loop(lambda state: state[0] > 0.5, again, state)[1:]


def solution(mesh):
    placed = (
        P("nodes", None),
        P(),
        P(),
        P(("nodes", "rep"), None, None),
        P(("nodes", "rep")),
        P(("nodes", "rep")),
        P(("nodes", "rep"), None),
        P("nodes", None),
    )
    return jax.shard_map(
        shards,
        mesh=mesh,
        in_specs=placed,
        out_specs=(P("nodes", "rep"), P(("nodes", "rep"), None), P(None, "rep"), P("rep")),
        check_vma=False,
    )
```

```python
import functools
import math

import jax
import jax.numpy as jnp
from jax import lax
from jax.experimental import pallas as pl
from jax.experimental.pallas import tpu as pltpu
from jax.sharding import PartitionSpec as P

ROOT_TWO_PI = 0.7978845608028654
CUBIC_TERM = 0.044715

NY, NZ, NX = 4, 8, 4
BLK = 128
HALF = 64
NB = 8
CAP = 56
ROWS = NB * HALF
MSG = ROWS + 16
PART = NZ * MSG
LOCAL = NY * PART
FAR = CAP * HALF
TILES = 128
LOC0, REM0, CNT0, OVER, ROW0 = 128, 256, 440, 444, 512
INFO = 640
SUMS = BLK + 16
SEND = 64 * HALF


def gelu_value(values):
    inner_term = ROOT_TWO_PI * (values + CUBIC_TERM * values * values * values)
    return 0.5 * values * (1.0 + jnp.tanh(inner_term))


def gelu_slope(values):
    tangent = jnp.tanh(ROOT_TWO_PI * (values + CUBIC_TERM * values * values * values))
    outer_part = 0.5 * values * (1.0 - tangent * tangent) * ROOT_TWO_PI
    return 0.5 * (1.0 + tangent) + outer_part * (1.0 + 3.0 * CUBIC_TERM * values * values)


def general_shards(features, weight, out_bias, edge_tiles, block_row, tile_slot, send_list, out_grad):
    node_count = lax.axis_size("nodes")
    rep_count = lax.axis_size("rep")
    rep_position = lax.axis_index("rep")
    block_size = edge_tiles.shape[1]
    local_blocks = features.shape[0] // block_size
    width_in = features.shape[1]
    capacity = send_list.shape[1]
    half_out = weight.shape[1] // rep_count
    feature_blocks = features.reshape(local_blocks, block_size, width_in)
    outgoing = feature_blocks[send_list]
    incoming = lax.all_to_all(outgoing, "nodes", split_axis=0, concat_axis=0, tiled=True)
    incoming = incoming.reshape(node_count * capacity, block_size, width_in)
    picked = incoming[tile_slot]
    products = jnp.einsum("tij,tjf->tif", edge_tiles, picked, preferred_element_type=jnp.float32)
    local_rows = block_row - lax.axis_index("nodes") * local_blocks
    partial_value = jax.ops.segment_sum(products, local_rows, num_segments=local_blocks)
    partial_value = partial_value.reshape(local_blocks * block_size, width_in)
    aggregate_bf = lax.psum(partial_value, "rep").astype(jnp.bfloat16)
    preact = jnp.dot(aggregate_bf, weight, preferred_element_type=jnp.float32) + out_bias
    own_preact = lax.dynamic_slice_in_dim(preact, rep_position * half_out, half_out, 1)
    activations = gelu_value(own_preact).astype(jnp.bfloat16)
    pre_grad = (out_grad.astype(jnp.float32) * gelu_slope(preact)).astype(jnp.bfloat16)
    agg_grad = lax.dot_general(
        pre_grad, weight, (((1,), (1,)), ((), ())), preferred_element_type=jnp.float32
    ).astype(jnp.bfloat16)
    grad_rows = agg_grad.reshape(local_blocks, block_size, width_in)[local_rows]
    back_products = jnp.einsum(
        "tji,tjf->tif", edge_tiles, grad_rows, preferred_element_type=jnp.float32
    )
    slot_sums = jax.ops.segment_sum(back_products, tile_slot, num_segments=node_count * capacity)
    slot_sums = slot_sums.astype(jnp.bfloat16)
    returned = lax.all_to_all(
        slot_sums.reshape(node_count, capacity, block_size, width_in),
        "nodes",
        split_axis=0,
        concat_axis=0,
        tiled=True,
    )
    returned = returned.astype(jnp.float32)
    owner_sums = jax.ops.segment_sum(
        returned.reshape(node_count * capacity, block_size, width_in),
        send_list.reshape(-1),
        num_segments=local_blocks,
    )
    feature_grad = lax.psum_scatter(
        owner_sums.reshape(local_blocks * block_size, width_in).astype(jnp.bfloat16),
        "rep",
        scatter_dimension=0,
        tiled=True,
    ).astype(jnp.float32)
    own_grad = lax.dynamic_slice_in_dim(pre_grad, rep_position * half_out, half_out, 1)
    norm_scale = 1.0 / math.sqrt(features.shape[0] * node_count)
    weight_part = lax.dot_general(
        aggregate_bf, own_grad, (((0,), (0,)), ((), ())), preferred_element_type=jnp.float32
    )
    bias_part = jnp.sum(own_grad.astype(jnp.float32), axis=0)
    weight_sum, bias_sum = lax.psum((weight_part, bias_part), "nodes")
    return (activations, feature_grad, weight_sum * norm_scale, bias_sum * norm_scale)


def device_of(y, z, x, c):
    return ((y % NY * NZ + z % NZ) * NX + x % NX) * 2 + c


def moved(value, target):
    pairs = [
        (device_of(y, z, x, c), device_of(*target(y, z, x, c)))
        for y in range(NY)
        for z in range(NZ)
        for x in range(NX)
        for c in range(2)
    ]
    return lax.ppermute(value, ("nodes", "rep"), pairs)


def along_z(value, step):
    return moved(value, lambda y, z, x, c: (y, z + step if c == 0 else z - step, x, c))


def along_dense(value, step):
    return moved(value, lambda y, z, x, c: (y + step, z, x, c) if c == 0 else (y, z, x + step, c))


def along_sparse(value, step):
    return moved(value, lambda y, z, x, c: (y, z, x + step, c) if c == 0 else (y + step, z, x, c))


def to_other_core(value):
    return moved(value, lambda y, z, x, c: (y, z, x, 1 - c))


SMEM = pl.BlockSpec(memory_space=pltpu.SMEM)
VMEM = pl.BlockSpec(memory_space=pltpu.VMEM)
ANY = pl.BlockSpec(memory_space=pl.ANY)


def call(kernel, out_shape, in_specs, out_specs, scratch=(), flops=0, moved_bytes=0, vmem=12):
    return pl.pallas_call(
        kernel,
        out_shape=out_shape,
        in_specs=in_specs,
        out_specs=out_specs,
        scratch_shapes=list(scratch),
        compiler_params=pltpu.CompilerParams(vmem_limit_bytes=vmem << 20),
        cost_estimate=pl.CostEstimate(flops=flops, bytes_accessed=moved_bytes, transcendentals=0),
    )


def struct(shape, dtype):
    return jax.ShapeDtypeStruct(shape, dtype)


def message_kernel(core_ref, features_ref, own_ref, other_ref, out_ref, half_ref):
    core = core_ref[0]
    for block in range(NB):
        turned = features_ref[block * BLK : (block + 1) * BLK, :].astype(jnp.float32).T
        mine = jnp.where(core == 0, turned[:HALF], turned[HALF:]).astype(jnp.bfloat16)
        rest = jnp.where(core == 0, turned[HALF:], turned[:HALF]).astype(jnp.bfloat16)
        out_ref[block * HALF : (block + 1) * HALF, :] = mine
        half_ref[block * HALF : (block + 1) * HALF, :] = mine
        out_ref[MSG + block * HALF : MSG + (block + 1) * HALF, :] = rest
    own, other = own_ref[1:3, :], other_ref[1:3, :]
    lists = jnp.concatenate(
        [
            jnp.where(core == 0, own, other),
            jnp.where(core == 0, other, own),
            jnp.zeros((12, BLK), jnp.int32),
        ],
        axis=0,
    )
    lists = lists.astype(jnp.float32).astype(jnp.bfloat16)
    out_ref[ROWS:MSG, :] = lists
    half_ref[ROWS:MSG, :] = lists


def plan_kernel(code_ref, rows_ref, info_ref, first_ref, second_ref, third_ref, count_ref):
    requests = (first_ref, second_ref, third_ref)
    for k in range(8):
        count_ref[k] = 0

    def clear(i, carry):
        for ref in requests:
            ref[i] = 0
        info_ref[i] = 0
        info_ref[LOC0 + i] = 0
        info_ref[REM0 + i] = 0
        info_ref[REM0 + 128 + i] = 0
        info_ref[ROW0 + i] = rows_ref[i]
        return carry

    lax.fori_loop(0, 128, clear, 0)

    def place(t, carry):
        code = code_ref[t]
        other_key = code >> 9
        key = (code >> 7) & 3
        slot = code & 127
        count_ref[4 + other_key] = count_ref[4 + other_key] + 1
        rank = count_ref[key]
        count_ref[key] = rank + 1

        @pl.when(key == 0)
        def _():
            info_ref[rank] = slot
            info_ref[LOC0 + rank] = t

        @pl.when(jnp.logical_and(key > 0, rank < CAP))
        def _():
            info_ref[REM0 + (key - 1) * CAP + rank] = t
            for k in (1, 2, 3):

                @pl.when(key == k)
                def _():
                    requests[k - 1][rank] = slot

        return carry

    lax.fori_loop(0, TILES, place, 0)
    over = 0
    info_ref[CNT0] = count_ref[0]
    for k in (1, 2, 3):
        kept = jnp.minimum(count_ref[k], CAP)
        info_ref[CNT0 + k] = kept
        requests[k - 1][64] = kept
        over += count_ref[k] - kept
        over += jnp.maximum(count_ref[4 + k] - CAP, 0)
    info_ref[OVER] = over


def start_all(pairs, sem):
    copies = [pltpu.make_async_copy(src, dst, sem.at[n]) for n, (src, dst) in enumerate(pairs)]
    for copy in copies:
        copy.start()
    return copies


def wait_all(copies):
    for copy in copies:
        copy.wait()


def half_rows(index):
    return pl.ds(pl.multiple_of(index * HALF, HALF), HALF)


def local_block(parts, slot, table, k):
    row = ((slot >> 2) & (NZ - 1)) * MSG + (table[(slot << 2) + k] << 6)
    at = pl.ds(pl.multiple_of(row, 16), HALF)
    part = slot >> 5
    low = jnp.where(part == 0, parts[0][at, :], parts[1][at, :])
    high = jnp.where(part == 2, parts[2][at, :], parts[3][at, :])
    return jnp.where(part < 2, low, high)


def pick_kernel(
    a_ref, b_ref, c_ref, d_ref, first_ref, second_ref, third_ref, table_ref, o1, o2, o3,
    q1, q2, q3, table, sem,
):
    parts = (a_ref, b_ref, c_ref, d_ref)
    wait_all(
        start_all([(first_ref, q1), (second_ref, q2), (third_ref, q3), (table_ref, table)], sem)
    )
    for k, (req, out) in enumerate(((q1, o1), (q2, o2), (q3, o3))):

        def body(i, carry, req=req, out=out, k=k):
            for u in range(8):
                p = i * 8 + u
                out[half_rows(p), :] = local_block(parts, req[p], table, k + 1)
            return carry

        lax.fori_loop(0, CAP // 8, body, 0)


def near_kernel(
    a_ref, b_ref, c_ref, d_ref, tiles, info_ref, table_ref, out_ref, acc, info, table, sem
):
    parts = (a_ref, b_ref, c_ref, d_ref)
    copies = start_all([(info_ref, info), (table_ref, table)], sem)
    acc[...] = jnp.zeros_like(acc)
    wait_all(copies)
    count = info[CNT0]

    def body(i, carry):
        done = []
        for u in range(8):
            p = i * 8 + u
            block = local_block(parts, info[p], table, 0)
            done.append(
                lax.dot_general(
                    block, tiles[info[LOC0 + p]], (((1,), (1,)), ((), ())),
                    preferred_element_type=jnp.float32,
                )
            )
        for u in range(8):
            p = i * 8 + u
            row = jnp.where(p < count, info[ROW0 + info[LOC0 + p]], NB)
            acc[half_rows(row), :] += done[u]
        return carry

    lax.fori_loop(0, (count + 7) >> 3, body, 0)
    out_ref[...] = acc[:ROWS, :]


def far_kernel(steps, near_ref, *refs):
    *moved_refs, tiles, info_ref, out_ref, acc, info, sem = refs
    copies = start_all([(info_ref, info)], sem)
    acc[:ROWS, :] = near_ref[...]
    acc[ROWS:, :] = jnp.zeros((HALF, BLK), jnp.float32)
    wait_all(copies)
    for k, got in zip(steps, moved_refs):
        count = info[CNT0 + k]

        def body(i, carry, k=k, got=got, count=count):
            done = []
            for u in range(8):
                p = i * 8 + u
                done.append(
                    lax.dot_general(
                        got[half_rows(p), :], tiles[info[REM0 + (k - 1) * CAP + p]],
                        (((1,), (1,)), ((), ())), preferred_element_type=jnp.float32,
                    )
                )
            for u in range(8):
                p = i * 8 + u
                row = jnp.where(p < count, info[ROW0 + info[REM0 + (k - 1) * CAP + p]], NB)
                acc[half_rows(row), :] += done[u]
            return carry

        lax.fori_loop(0, (count + 7) >> 3, body, 0)
    out_ref[...] = acc[:ROWS, :].astype(out_ref.dtype)


def products(step, tiles, turned_ref, info, out):
    first = REM0 + (step - 1) * CAP

    def body(i, carry):
        for u in range(8):
            p = i * 8 + u
            t = info[first + p]
            left = turned_ref[half_rows(info[ROW0 + t]), :]
            out[half_rows(p), :] = jnp.dot(
                left, tiles[t], preferred_element_type=jnp.float32
            ).astype(jnp.bfloat16)
        return carry

    lax.fori_loop(0, (info[CNT0 + step] + 7) >> 3, body, 0)


def middle_kernel(
    core_ref, own_agg, other_agg, weight_ref, bias_ref, grad_ref, tiles, info_ref,
    act_ref, sums_ref, turned_ref, out, info, sem,
):
    copies = start_all([(info_ref, info)], sem)
    core = core_ref[0]
    sums_ref[...] = jnp.zeros_like(sums_ref)
    weight_half = weight_ref[half_rows(core), :]

    def block_step(b, carry):
        own, other = own_agg[half_rows(b), :], other_agg[half_rows(b), :]
        low = jnp.where(core == 0, own, other)
        high = jnp.where(core == 0, other, own)
        agg = jnp.concatenate([low, high], axis=0)
        preact = lax.dot_general(
            agg, weight_ref[...], (((0,), (0,)), ((), ())), preferred_element_type=jnp.float32
        )
        preact = preact + bias_ref[...]
        tangent = jnp.tanh(ROOT_TWO_PI * (preact + CUBIC_TERM * preact * preact * preact))
        nodes = pl.ds(pl.multiple_of(b * BLK, BLK), BLK)
        value = 0.5 * preact * (1.0 + tangent)
        act_ref[nodes, :] = jnp.where(core == 0, value[:, :BLK], value[:, BLK:]).astype(jnp.bfloat16)
        outer = 0.5 * preact * (1.0 - tangent * tangent) * ROOT_TWO_PI
        slope = 0.5 * (1.0 + tangent) + outer * (1.0 + 3.0 * CUBIC_TERM * preact * preact)
        pre = (grad_ref[nodes, :].astype(jnp.float32) * slope).astype(jnp.bfloat16)
        turned_ref[half_rows(b), :] = lax.dot_general(
            weight_half, pre, (((1,), (1,)), ((), ())), preferred_element_type=jnp.float32
        ).astype(jnp.bfloat16)
        mine = jnp.where(core == 0, pre[:, :BLK], pre[:, BLK:])
        sums_ref[:BLK, :] += lax.dot_general(
            agg, mine, (((1,), (0,)), ((), ())), preferred_element_type=jnp.float32
        )
        sums_ref[BLK : BLK + 1, :] += jnp.sum(mine.astype(jnp.float32), axis=0, keepdims=True)
        return carry

    lax.fori_loop(0, NB, block_step, 0, unroll=2)
    wait_all(copies)
    over = info[OVER].astype(jnp.float32)
    sums_ref[BLK + 1 : BLK + 2, :] = jnp.full((1, BLK), over, jnp.float32)
    products(2, tiles, turned_ref, info, out)


def side_kernel(tiles, turned_ref, info_ref, o1, o3, info, sem):
    wait_all(start_all([(info_ref, info)], sem))
    products(1, tiles, turned_ref, info, o1)
    products(3, tiles, turned_ref, info, o3)


NORM = 1.0 / math.sqrt(NY * NZ * NX * NB * BLK)


def two_parts(value):
    upper = value.astype(jnp.bfloat16)
    return upper, (value - upper.astype(jnp.float32)).astype(jnp.bfloat16)


def owner_kernel(
    info_ref, table_ref, first_ref, second_ref, third_ref, turned_ref, tiles,
    r1, r2, r3, sums_ref, o0, o1, o2, o3, total, info, table, q1, q2, q3, sem,
):
    copies = start_all(
        [(info_ref, info), (table_ref, table), (first_ref, q1), (second_ref, q2), (third_ref, q3)],
        sem,
    )
    total[...] = jnp.zeros_like(total)
    wait_all(copies)

    def total_rows(slot, k, used):
        return half_rows(jnp.where(used, ((slot >> 2) << 3) + table[(slot << 2) + k], 256))

    count = info[CNT0]

    def near(i, carry):
        done = []
        for u in range(8):
            t = info[LOC0 + i * 8 + u]
            left = turned_ref[half_rows(info[ROW0 + t]), :]
            done.append(jnp.dot(left, tiles[t], preferred_element_type=jnp.float32))
        for u in range(8):
            p = i * 8 + u
            total[total_rows(info[p], 0, p < count), :] += done[u]
        return carry

    lax.fori_loop(0, (count + 7) >> 3, near, 0)
    for k, (req, got) in enumerate(((q1, r1), (q2, r2), (q3, r3))):
        kept = req[64]

        def far(i, carry, req=req, got=got, k=k, kept=kept):
            for u in range(8):
                p = i * 8 + u
                at = total_rows(req[p], k + 1, p < kept)
                total[at, :] += got[half_rows(p), :].astype(jnp.float32)
            return carry

        lax.fori_loop(0, (kept + 7) >> 3, far, 0)
    for j, out in enumerate((o0, o1, o2, o3)):
        out[...] = total[j * SEND : (j + 1) * SEND, :].astype(jnp.bfloat16)


def split_sum_kernel(
    a_ref, b_ref, c_ref, d_ref, sums_ref, keep_ref, far_ref, mine_ref, swap_ref, passed_ref
):
    passed_ref[...] = sums_ref[...]
    for m in range(NZ):
        at = slice(m * ROWS, (m + 1) * ROWS)
        value = a_ref[at, :].astype(jnp.float32) + b_ref[at, :].astype(jnp.float32)
        value = value + (c_ref[at, :].astype(jnp.float32) + d_ref[at, :].astype(jnp.float32))
        value = value.astype(jnp.bfloat16)
        if m == 0:
            keep_ref[...] = value
        elif m < 4:
            mine_ref[(m - 1) * ROWS : m * ROWS, :] = value
        elif m == 4:
            far_ref[...] = value
        else:
            swap_ref[(m - 5) * ROWS : (m - 4) * ROWS, :] = value


def last_sum_kernel(
    core_ref, sums_ref, keep_ref, far_ref, a_ref, b_ref, c_ref, hold_ref, send_ref, passed_ref
):
    passed_ref[...] = sums_ref[...]
    core = core_ref[0]
    half = ROWS // 2

    def total(first):
        at = slice(first, first + half)
        value = a_ref[at, :].astype(jnp.float32) + b_ref[at, :].astype(jnp.float32)
        value = value + c_ref[at, :].astype(jnp.float32)
        if first < ROWS:
            value = value + keep_ref[at, :].astype(jnp.float32) + far_ref[at, :].astype(jnp.float32)
        return value

    for n in range(2):
        low, high = total(n * ROWS), total(n * ROWS + half)
        at = slice(n * half, (n + 1) * half)
        hold_ref[at, :] = jnp.where(core == 0, low, high)
        send_ref[at, :] = jnp.where(core == 0, high, low)


def turn_kernel(core_ref, hold_ref, got_ref, sums_ref, out_ref, weight_ref, bias_ref):
    core = core_ref[0]
    half = ROWS // 2
    for b in range(NB // 2):
        first = slice(b * HALF, (b + 1) * HALF)
        second = slice(half + b * HALF, half + (b + 1) * HALF)
        own = hold_ref[first, :] + got_ref[second, :]
        other = hold_ref[second, :] + got_ref[first, :]
        both = jnp.concatenate(
            [jnp.where(core == 0, own, other), jnp.where(core == 0, other, own)], axis=0
        )
        out_ref[b * BLK : (b + 1) * BLK, :] = both.T
    weight_ref[...] = sums_ref[:BLK, :] * NORM
    bias_ref[...] = sums_ref[BLK : BLK + 1, :] * NORM


def butterfly(value, target, size):
    step = 1
    while step < size:
        value = value + moved(value, functools.partial(target, step))
        step *= 2
    return value


def shards(features, weight, out_bias, edge_tiles, block_row, tile_slot, send_list, out_grad):
    bf16, f32, i32 = jnp.bfloat16, jnp.float32, jnp.int32
    node = lax.axis_index("nodes")
    core = lax.axis_index("rep")
    y, z, x = node // (NZ * NX), node // NX % NZ, node % NX
    core_array = jnp.reshape(core, (1,)).astype(i32)
    dma = pltpu.SemaphoreType.DMA

    local_rows = block_row - node * NB
    packed = jnp.pad(tile_slot * NB + local_rows, (0, BLK - 64))
    own_meta = jnp.concatenate([packed[None, :], send_list.T], axis=0)
    other_meta = to_other_core(own_meta)
    tiles = jnp.concatenate([edge_tiles, to_other_core(edge_tiles)], axis=0)

    message, half_message = call(
        message_kernel,
        [struct((MSG + ROWS, BLK), bf16), struct((MSG, BLK), bf16)],
        [SMEM, VMEM, VMEM, VMEM],
        [VMEM] * 2,
        moved_bytes=500000,
    )(core_array, features, own_meta, other_meta)
    first, second = along_z(message, 1), along_z(message, 2)
    first, second = lax.optimization_barrier((first, second))
    across, third = along_z(second[:MSG], 2), along_z(second, 1)
    swapped = to_other_core(jnp.concatenate([first[ROWS:], second[ROWS:]], axis=0))
    swapped = [swapped[:MSG], swapped[MSG:], to_other_core(third[ROWS:])]
    column = [half_message, first[:MSG], second[:MSG], third[:MSG], across]
    for piece in swapped:
        column += [piece[MSG - ROWS :], piece[: MSG - ROWS]]
    column = jnp.concatenate(column, axis=0)

    both = jnp.concatenate([own_meta[0, :64], other_meta[0, :64]])
    rows = both % NB
    slot = both // NB
    source, which = slot // 2, slot % 2
    step_y = (source // (NZ * NX) - y) % NY
    step_z = (source // NX - z) % NZ
    step_x = (source - x) % NX
    dense = jnp.where(core == 0, step_y, step_x)
    sparse = jnp.where(core == 0, step_x, step_y)
    step_z = jnp.where(core == 0, (NZ - step_z) % NZ, step_z)
    step_z = jnp.where(step_z <= 4, step_z, 12 - step_z)
    holder = jnp.where(jnp.arange(TILES) < 64, core, 1 - core)
    code = (dense * 4 + sparse) * 128 + (dense * NZ + step_z) * 4 + holder * 2 + which
    info, *requests = call(
        plan_kernel,
        [struct((INFO,), i32)] + [struct((128,), i32)] * 3,
        [SMEM] * 2,
        [SMEM] * 4,
        [pltpu.SMEM((8,), i32)],
        moved_bytes=100000,
    )(code.astype(i32), rows)
    requests = [along_sparse(requests[k - 1], k) for k in (1, 2, 3)]

    column, *requests = lax.optimization_barrier((column, *requests))
    parts = [column] + [along_dense(column, -j) for j in range(1, 4)]

    away = jnp.arange(4)
    asker = jnp.where(
        core == 0,
        node - x + (x - away) % NX,
        node - y * (NZ * NX) + (y - away) % NY * (NZ * NX),
    )
    lists = jnp.stack([part.reshape(NZ, MSG, BLK)[:, ROWS : ROWS + 4] for part in parts])
    chosen = (jnp.arange(BLK)[:, None] == asker[None, :]).astype(bf16)
    table = jnp.dot(lists.reshape(4 * NZ * 4, BLK), chosen, preferred_element_type=f32)
    table = table.astype(i32).reshape(-1)

    picked = call(
        pick_kernel,
        [struct((FAR, BLK), bf16)] * 3,
        [VMEM] * 4 + [ANY] * 4,
        [VMEM] * 3,
        [pltpu.SMEM((128,), i32)] * 3 + [pltpu.SMEM((512,), i32), dma((4,))],
        moved_bytes=7000000,
    )(*parts, *requests, table)
    far = [along_sparse(picked[k - 1], -k) for k in (1, 2, 3)]

    near = call(
        near_kernel,
        struct((ROWS, BLK), f32),
        [VMEM] * 5 + [ANY] * 2,
        VMEM,
        [
            pltpu.VMEM((ROWS + HALF, BLK), f32),
            pltpu.SMEM((INFO,), i32),
            pltpu.SMEM((512,), i32),
            dma((2,)),
        ],
        flops=2 * 32 * HALF * BLK * BLK,
        moved_bytes=11000000,
    )(*parts, tiles, info, table)
    agg_half = near
    for steps, kind in (((1, 3), f32), ((2,), bf16)):
        agg_half = call(
            functools.partial(far_kernel, steps),
            struct((ROWS, BLK), kind),
            [VMEM] * (2 + len(steps)) + [ANY],
            VMEM,
            [pltpu.VMEM((ROWS + HALF, BLK), f32), pltpu.SMEM((INFO,), i32), dma((1,))],
            flops=2 * 32 * len(steps) * HALF * BLK * BLK,
            moved_bytes=7000000,
        )(agg_half, *[far[k - 1] for k in steps], tiles, info)
    other_half = to_other_core(agg_half)

    activations, sums, turned, second_back = call(
        middle_kernel,
        [
            struct((NB * BLK, BLK), bf16),
            struct((SUMS, BLK), f32),
            struct((ROWS, BLK), bf16),
            struct((FAR, BLK), bf16),
        ],
        [SMEM] + [VMEM] * 6 + [ANY],
        [VMEM] * 4,
        [pltpu.SMEM((INFO,), i32), dma((1,))],
        flops=2 * TILES * HALF * BLK * BLK,
        moved_bytes=8000000,
    )(
        core_array, agg_half, other_half, weight, out_bias[None, :], out_grad, tiles, info
    )
    first_back, third_back = call(
        side_kernel,
        [struct((FAR, BLK), bf16)] * 2,
        [VMEM] * 2 + [ANY],
        [VMEM] * 2,
        [pltpu.SMEM((INFO,), i32), dma((1,))],
        flops=2 * 64 * HALF * BLK * BLK,
        moved_bytes=4000000,
    )(tiles, turned, info)
    second_back = along_sparse(second_back, 2)
    back = [along_sparse(first_back, 1), second_back, along_sparse(third_back, 3)]

    sums = butterfly(sums, lambda step, y, z, x, c: (y, z ^ step, x, c), NZ)
    owned = call(
        owner_kernel,
        [struct((SEND, BLK), bf16)] + [struct((SEND, BLK), bf16)] * 3,
        [ANY] * 5 + [VMEM] * 6,
        [VMEM] * 4,
        [
            pltpu.VMEM((257 * HALF, BLK), f32),
            pltpu.SMEM((INFO,), i32),
            pltpu.SMEM((512,), i32),
        ]
        + [pltpu.SMEM((128,), i32)] * 3
        + [dma((5,))],
        flops=2 * 32 * HALF * BLK * BLK,
        moved_bytes=11000000,
        vmem=21,
    )(info, table, *requests, turned, tiles, *back, sums)
    owned = [owned[0]] + [along_dense(owned[j], j) for j in range(1, 4)]
    keep, opposite, mine, swap, sums = call(
        split_sum_kernel,
        [struct((ROWS, BLK), bf16)] * 2
        + [struct((3 * ROWS, BLK), bf16)] * 2
        + [struct((SUMS, BLK), f32)],
        [VMEM] * 5,
        [VMEM] * 5,
        moved_bytes=5000000,
    )(*owned, sums)
    opposite = along_z(opposite, 4)
    swap = to_other_core(swap)
    pieces = [
        jnp.concatenate([mine[s * ROWS : (s + 1) * ROWS], swap[s * ROWS : (s + 1) * ROWS]], axis=0)
        for s in range(3)
    ]
    pieces = [along_z(pieces[s - 1], -s) for s in (3, 2, 1)][::-1]
    sums = butterfly(sums, lambda step, y, z, x, c: (y ^ step, z, x, c), NY)
    sums = butterfly(sums, lambda step, y, z, x, c: (y, z, x ^ step, c), NX)

    hold, send, sums = call(
        last_sum_kernel,
        [struct((ROWS, BLK), f32)] * 2 + [struct((SUMS, BLK), f32)],
        [SMEM] + [VMEM] * 6,
        [VMEM] * 3,
        moved_bytes=1500000,
    )(core_array, sums, keep, opposite, *pieces)
    feature_grad, weight_grad, bias_grad = call(
        turn_kernel,
        [struct((NB // 2 * BLK, BLK), f32), struct((BLK, BLK), f32), struct((1, BLK), f32)],
        [SMEM] + [VMEM] * 3,
        [VMEM] * 3,
        moved_bytes=1000000,
    )(core_array, hold, to_other_core(send), sums)

    def again(state):
        return (jnp.float32(0.0),) + general_shards(
            features, weight, out_bias, edge_tiles, block_row, tile_slot, send_list, out_grad
        )

    state = (sums[BLK + 1, 0], activations, feature_grad, weight_grad, bias_grad.reshape(-1))
    return lax.while_loop(lambda state: state[0] > 0.5, again, state)[1:]


def solution(mesh):
    placed = (
        P("nodes", None),
        P(),
        P(),
        P(("nodes", "rep"), None, None),
        P(("nodes", "rep")),
        P(("nodes", "rep")),
        P(("nodes", "rep"), None),
        P("nodes", None),
    )
    return jax.shard_map(
        shards,
        mesh=mesh,
        in_specs=placed,
        out_specs=(P("nodes", "rep"), P(("nodes", "rep"), None), P(None, "rep"), P("rep")),
        check_vma=False,
    )
```

```python
import functools
import math

import jax
import jax.numpy as jnp
from jax import lax
from jax.experimental import pallas as pl
from jax.experimental.pallas import tpu as pltpu
from jax.sharding import PartitionSpec as P

ROOT_TWO_PI = 0.7978845608028654
CUBIC_TERM = 0.044715

NY, NZ, NX = 4, 8, 4
BLK = 128
HALF = 64
NB = 8
CAP = 56
ROWS = NB * HALF
MSG = ROWS + 16
PART = NZ * MSG
LOCAL = NY * PART
FAR = CAP * HALF
TILES = 128
LOC0, REM0, CNT0, OVER, ROW0 = 128, 256, 440, 444, 512
INFO = 640
SUMS = BLK + 16
SEND = 64 * HALF


def gelu_value(values):
    inner_term = ROOT_TWO_PI * (values + CUBIC_TERM * values * values * values)
    return 0.5 * values * (1.0 + jnp.tanh(inner_term))


def gelu_slope(values):
    tangent = jnp.tanh(ROOT_TWO_PI * (values + CUBIC_TERM * values * values * values))
    outer_part = 0.5 * values * (1.0 - tangent * tangent) * ROOT_TWO_PI
    return 0.5 * (1.0 + tangent) + outer_part * (1.0 + 3.0 * CUBIC_TERM * values * values)


def general_shards(features, weight, out_bias, edge_tiles, block_row, tile_slot, send_list, out_grad):
    node_count = lax.axis_size("nodes")
    rep_count = lax.axis_size("rep")
    rep_position = lax.axis_index("rep")
    block_size = edge_tiles.shape[1]
    local_blocks = features.shape[0] // block_size
    width_in = features.shape[1]
    capacity = send_list.shape[1]
    half_out = weight.shape[1] // rep_count
    feature_blocks = features.reshape(local_blocks, block_size, width_in)
    outgoing = feature_blocks[send_list]
    incoming = lax.all_to_all(outgoing, "nodes", split_axis=0, concat_axis=0, tiled=True)
    incoming = incoming.reshape(node_count * capacity, block_size, width_in)
    picked = incoming[tile_slot]
    products = jnp.einsum("tij,tjf->tif", edge_tiles, picked, preferred_element_type=jnp.float32)
    local_rows = block_row - lax.axis_index("nodes") * local_blocks
    partial_value = jax.ops.segment_sum(products, local_rows, num_segments=local_blocks)
    partial_value = partial_value.reshape(local_blocks * block_size, width_in)
    aggregate_bf = lax.psum(partial_value, "rep").astype(jnp.bfloat16)
    preact = jnp.dot(aggregate_bf, weight, preferred_element_type=jnp.float32) + out_bias
    own_preact = lax.dynamic_slice_in_dim(preact, rep_position * half_out, half_out, 1)
    activations = gelu_value(own_preact).astype(jnp.bfloat16)
    pre_grad = (out_grad.astype(jnp.float32) * gelu_slope(preact)).astype(jnp.bfloat16)
    agg_grad = lax.dot_general(
        pre_grad, weight, (((1,), (1,)), ((), ())), preferred_element_type=jnp.float32
    ).astype(jnp.bfloat16)
    grad_rows = agg_grad.reshape(local_blocks, block_size, width_in)[local_rows]
    back_products = jnp.einsum(
        "tji,tjf->tif", edge_tiles, grad_rows, preferred_element_type=jnp.float32
    )
    slot_sums = jax.ops.segment_sum(back_products, tile_slot, num_segments=node_count * capacity)
    slot_sums = slot_sums.astype(jnp.bfloat16)
    returned = lax.all_to_all(
        slot_sums.reshape(node_count, capacity, block_size, width_in),
        "nodes",
        split_axis=0,
        concat_axis=0,
        tiled=True,
    )
    returned = returned.astype(jnp.float32)
    owner_sums = jax.ops.segment_sum(
        returned.reshape(node_count * capacity, block_size, width_in),
        send_list.reshape(-1),
        num_segments=local_blocks,
    )
    feature_grad = lax.psum_scatter(
        owner_sums.reshape(local_blocks * block_size, width_in).astype(jnp.bfloat16),
        "rep",
        scatter_dimension=0,
        tiled=True,
    ).astype(jnp.float32)
    own_grad = lax.dynamic_slice_in_dim(pre_grad, rep_position * half_out, half_out, 1)
    norm_scale = 1.0 / math.sqrt(features.shape[0] * node_count)
    weight_part = lax.dot_general(
        aggregate_bf, own_grad, (((0,), (0,)), ((), ())), preferred_element_type=jnp.float32
    )
    bias_part = jnp.sum(own_grad.astype(jnp.float32), axis=0)
    weight_sum, bias_sum = lax.psum((weight_part, bias_part), "nodes")
    return (activations, feature_grad, weight_sum * norm_scale, bias_sum * norm_scale)


def device_of(y, z, x, c):
    return ((y % NY * NZ + z % NZ) * NX + x % NX) * 2 + c


def moved(value, target):
    pairs = [
        (device_of(y, z, x, c), device_of(*target(y, z, x, c)))
        for y in range(NY)
        for z in range(NZ)
        for x in range(NX)
        for c in range(2)
    ]
    return lax.ppermute(value, ("nodes", "rep"), pairs)


def along_z(value, step):
    return moved(value, lambda y, z, x, c: (y, z + step if c == 0 else z - step, x, c))


def along_dense(value, step):
    return moved(value, lambda y, z, x, c: (y + step, z, x, c) if c == 0 else (y, z, x + step, c))


def along_sparse(value, step):
    return moved(value, lambda y, z, x, c: (y, z, x + step, c) if c == 0 else (y + step, z, x, c))


def to_other_core(value):
    return moved(value, lambda y, z, x, c: (y, z, x, 1 - c))


SMEM = pl.BlockSpec(memory_space=pltpu.SMEM)
VMEM = pl.BlockSpec(memory_space=pltpu.VMEM)
ANY = pl.BlockSpec(memory_space=pl.ANY)


def call(kernel, out_shape, in_specs, out_specs, scratch=(), flops=0, moved_bytes=0, vmem=12):
    return pl.pallas_call(
        kernel,
        out_shape=out_shape,
        in_specs=in_specs,
        out_specs=out_specs,
        scratch_shapes=list(scratch),
        compiler_params=pltpu.CompilerParams(vmem_limit_bytes=vmem << 20),
        cost_estimate=pl.CostEstimate(flops=flops, bytes_accessed=moved_bytes, transcendentals=0),
    )


def struct(shape, dtype):
    return jax.ShapeDtypeStruct(shape, dtype)


def message_kernel(core_ref, features_ref, own_ref, other_ref, out_ref, half_ref):
    core = core_ref[0]
    for block in range(NB):
        turned = features_ref[block * BLK : (block + 1) * BLK, :].astype(jnp.float32).T
        mine = jnp.where(core == 0, turned[:HALF], turned[HALF:]).astype(jnp.bfloat16)
        rest = jnp.where(core == 0, turned[HALF:], turned[:HALF]).astype(jnp.bfloat16)
        out_ref[block * HALF : (block + 1) * HALF, :] = mine
        half_ref[block * HALF : (block + 1) * HALF, :] = mine
        out_ref[MSG + block * HALF : MSG + (block + 1) * HALF, :] = rest
    own, other = own_ref[1:3, :], other_ref[1:3, :]
    lists = jnp.concatenate(
        [
            jnp.where(core == 0, own, other),
            jnp.where(core == 0, other, own),
            jnp.zeros((12, BLK), jnp.int32),
        ],
        axis=0,
    )
    lists = lists.astype(jnp.float32).astype(jnp.bfloat16)
    out_ref[ROWS:MSG, :] = lists
    half_ref[ROWS:MSG, :] = lists


def plan_kernel(code_ref, rows_ref, info_ref, first_ref, second_ref, third_ref, count_ref):
    requests = (first_ref, second_ref, third_ref)
    for k in range(8):
        count_ref[k] = 0

    def clear(i, carry):
        for ref in requests:
            ref[i] = 0
        info_ref[i] = 0
        info_ref[LOC0 + i] = 0
        info_ref[REM0 + i] = 0
        info_ref[REM0 + 128 + i] = 0
        info_ref[ROW0 + i] = rows_ref[i]
        return carry

    lax.fori_loop(0, 128, clear, 0)

    def place(t, carry):
        code = code_ref[t]
        other_key = code >> 9
        key = (code >> 7) & 3
        slot = code & 127
        count_ref[4 + other_key] = count_ref[4 + other_key] + 1
        rank = count_ref[key]
        count_ref[key] = rank + 1

        @pl.when(key == 0)
        def _():
            info_ref[rank] = slot
            info_ref[LOC0 + rank] = t

        @pl.when(jnp.logical_and(key > 0, rank < CAP))
        def _():
            info_ref[REM0 + (key - 1) * CAP + rank] = t
            for k in (1, 2, 3):

                @pl.when(key == k)
                def _():
                    requests[k - 1][rank] = slot

        return carry

    lax.fori_loop(0, TILES, place, 0)
    over = 0
    info_ref[CNT0] = count_ref[0]
    for k in (1, 2, 3):
        kept = jnp.minimum(count_ref[k], CAP)
        info_ref[CNT0 + k] = kept
        requests[k - 1][64] = kept
        over += count_ref[k] - kept
        over += jnp.maximum(count_ref[4 + k] - CAP, 0)
    info_ref[OVER] = over


def start_all(pairs, sem):
    copies = [pltpu.make_async_copy(src, dst, sem.at[n]) for n, (src, dst) in enumerate(pairs)]
    for copy in copies:
        copy.start()
    return copies


def wait_all(copies):
    for copy in copies:
        copy.wait()


def half_rows(index):
    return pl.ds(pl.multiple_of(index * HALF, HALF), HALF)


def local_block(parts, slot, table, k):
    row = ((slot >> 2) & (NZ - 1)) * MSG + (table[(slot << 2) + k] << 6)
    at = pl.ds(pl.multiple_of(row, 16), HALF)
    part = slot >> 5
    low = jnp.where(part == 0, parts[0][at, :], parts[1][at, :])
    high = jnp.where(part == 2, parts[2][at, :], parts[3][at, :])
    return jnp.where(part < 2, low, high)


def pick_kernel(
    a_ref, b_ref, c_ref, d_ref, first_ref, second_ref, third_ref, table_ref, o1, o2, o3,
    q1, q2, q3, table, sem,
):
    parts = (a_ref, b_ref, c_ref, d_ref)
    wait_all(
        start_all([(first_ref, q1), (second_ref, q2), (third_ref, q3), (table_ref, table)], sem)
    )
    for k, (req, out) in enumerate(((q1, o1), (q2, o2), (q3, o3))):

        def body(i, carry, req=req, out=out, k=k):
            blocks = [local_block(parts, req[i * 8 + u], table, k + 1) for u in range(8)]
            for u in range(8):
                out[half_rows(i * 8 + u), :] = blocks[u]
            return carry

        lax.fori_loop(0, CAP // 8, body, 0)


def near_kernel(
    a_ref, b_ref, c_ref, d_ref, tiles, info_ref, table_ref, out_ref, acc, info, table, sem
):
    parts = (a_ref, b_ref, c_ref, d_ref)
    copies = start_all([(info_ref, info), (table_ref, table)], sem)
    acc[...] = jnp.zeros_like(acc)
    wait_all(copies)
    count = info[CNT0]

    def body(i, carry):
        done = []
        for u in range(8):
            p = i * 8 + u
            block = local_block(parts, info[p], table, 0)
            done.append(
                lax.dot_general(
                    block, tiles[info[LOC0 + p]], (((1,), (1,)), ((), ())),
                    preferred_element_type=jnp.float32,
                )
            )
        for u in range(8):
            p = i * 8 + u
            row = jnp.where(p < count, info[ROW0 + info[LOC0 + p]], NB)
            acc[half_rows(row), :] += done[u]
        return carry

    lax.fori_loop(0, (count + 7) >> 3, body, 0)
    out_ref[...] = acc[:ROWS, :]


def far_kernel(steps, near_ref, *refs):
    *moved_refs, tiles, info_ref, out_ref, acc, info, sem = refs
    copies = start_all([(info_ref, info)], sem)
    acc[:ROWS, :] = near_ref[...]
    acc[ROWS:, :] = jnp.zeros((HALF, BLK), jnp.float32)
    wait_all(copies)
    for k, got in zip(steps, moved_refs):
        count = info[CNT0 + k]

        def body(i, carry, k=k, got=got, count=count):
            done = []
            for u in range(8):
                p = i * 8 + u
                done.append(
                    lax.dot_general(
                        got[half_rows(p), :], tiles[info[REM0 + (k - 1) * CAP + p]],
                        (((1,), (1,)), ((), ())), preferred_element_type=jnp.float32,
                    )
                )
            for u in range(8):
                p = i * 8 + u
                row = jnp.where(p < count, info[ROW0 + info[REM0 + (k - 1) * CAP + p]], NB)
                acc[half_rows(row), :] += done[u]
            return carry

        lax.fori_loop(0, (count + 7) >> 3, body, 0)
    out_ref[...] = acc[:ROWS, :].astype(out_ref.dtype)


def products(step, tiles, turned_ref, info, out):
    first = REM0 + (step - 1) * CAP

    def body(i, carry):
        done = []
        for u in range(8):
            t = info[first + i * 8 + u]
            left = turned_ref[half_rows(info[ROW0 + t]), :]
            done.append(jnp.dot(left, tiles[t], preferred_element_type=jnp.float32))
        for u in range(8):
            out[half_rows(i * 8 + u), :] = done[u].astype(jnp.bfloat16)
        return carry

    lax.fori_loop(0, (info[CNT0 + step] + 7) >> 3, body, 0)


def middle_kernel(
    core_ref, own_agg, other_agg, weight_ref, bias_ref, grad_ref, tiles, info_ref,
    act_ref, sums_ref, turned_ref, out, info, sem,
):
    copies = start_all([(info_ref, info)], sem)
    core = core_ref[0]
    sums_ref[...] = jnp.zeros_like(sums_ref)
    weight_half = weight_ref[half_rows(core), :]

    def block_step(b, carry):
        own, other = own_agg[half_rows(b), :], other_agg[half_rows(b), :]
        low = jnp.where(core == 0, own, other)
        high = jnp.where(core == 0, other, own)
        agg = jnp.concatenate([low, high], axis=0)
        preact = lax.dot_general(
            agg, weight_ref[...], (((0,), (0,)), ((), ())), preferred_element_type=jnp.float32
        )
        preact = preact + bias_ref[...]
        tangent = jnp.tanh(ROOT_TWO_PI * (preact + CUBIC_TERM * preact * preact * preact))
        nodes = pl.ds(pl.multiple_of(b * BLK, BLK), BLK)
        value = 0.5 * preact * (1.0 + tangent)
        act_ref[nodes, :] = jnp.where(core == 0, value[:, :BLK], value[:, BLK:]).astype(jnp.bfloat16)
        outer = 0.5 * preact * (1.0 - tangent * tangent) * ROOT_TWO_PI
        slope = 0.5 * (1.0 + tangent) + outer * (1.0 + 3.0 * CUBIC_TERM * preact * preact)
        pre = (grad_ref[nodes, :].astype(jnp.float32) * slope).astype(jnp.bfloat16)
        turned_ref[half_rows(b), :] = lax.dot_general(
            weight_half, pre, (((1,), (1,)), ((), ())), preferred_element_type=jnp.float32
        ).astype(jnp.bfloat16)
        mine = jnp.where(core == 0, pre[:, :BLK], pre[:, BLK:])
        sums_ref[:BLK, :] += lax.dot_general(
            agg, mine, (((1,), (0,)), ((), ())), preferred_element_type=jnp.float32
        )
        sums_ref[BLK : BLK + 1, :] += jnp.sum(mine.astype(jnp.float32), axis=0, keepdims=True)
        return carry

    lax.fori_loop(0, NB, block_step, 0, unroll=2)
    wait_all(copies)
    over = info[OVER].astype(jnp.float32)
    sums_ref[BLK + 1 : BLK + 2, :] = jnp.full((1, BLK), over, jnp.float32)
    products(2, tiles, turned_ref, info, out)


def side_kernel(tiles, turned_ref, info_ref, o1, o3, info, sem):
    wait_all(start_all([(info_ref, info)], sem))
    products(1, tiles, turned_ref, info, o1)
    products(3, tiles, turned_ref, info, o3)


NORM = 1.0 / math.sqrt(NY * NZ * NX * NB * BLK)


def two_parts(value):
    upper = value.astype(jnp.bfloat16)
    return upper, (value - upper.astype(jnp.float32)).astype(jnp.bfloat16)


def owner_kernel(
    info_ref, table_ref, first_ref, second_ref, third_ref, turned_ref, tiles,
    r1, r2, r3, sums_ref, o0, o1, o2, o3, total, info, table, q1, q2, q3, sem,
):
    copies = start_all(
        [(info_ref, info), (table_ref, table), (first_ref, q1), (second_ref, q2), (third_ref, q3)],
        sem,
    )
    total[...] = jnp.zeros_like(total)
    wait_all(copies)

    def total_rows(slot, k, used):
        return half_rows(jnp.where(used, ((slot >> 2) << 3) + table[(slot << 2) + k], 256))

    count = info[CNT0]

    def near(i, carry):
        done = []
        for u in range(8):
            t = info[LOC0 + i * 8 + u]
            left = turned_ref[half_rows(info[ROW0 + t]), :]
            done.append(jnp.dot(left, tiles[t], preferred_element_type=jnp.float32))
        for u in range(8):
            p = i * 8 + u
            total[total_rows(info[p], 0, p < count), :] += done[u]
        return carry

    lax.fori_loop(0, (count + 7) >> 3, near, 0)
    for k, (req, got) in enumerate(((q1, r1), (q2, r2), (q3, r3))):
        kept = req[64]

        def far(i, carry, req=req, got=got, k=k, kept=kept):
            for u in range(8):
                p = i * 8 + u
                at = total_rows(req[p], k + 1, p < kept)
                total[at, :] += got[half_rows(p), :].astype(jnp.float32)
            return carry

        lax.fori_loop(0, (kept + 7) >> 3, far, 0)
    for j, out in enumerate((o0, o1, o2, o3)):
        out[...] = total[j * SEND : (j + 1) * SEND, :].astype(jnp.bfloat16)


def split_sum_kernel(
    a_ref, b_ref, c_ref, d_ref, sums_ref, keep_ref, far_ref, mine_ref, swap_ref, passed_ref
):
    passed_ref[...] = sums_ref[...]
    for m in range(NZ):
        at = slice(m * ROWS, (m + 1) * ROWS)
        value = a_ref[at, :].astype(jnp.float32) + b_ref[at, :].astype(jnp.float32)
        value = value + (c_ref[at, :].astype(jnp.float32) + d_ref[at, :].astype(jnp.float32))
        value = value.astype(jnp.bfloat16)
        if m == 0:
            keep_ref[...] = value
        elif m < 4:
            mine_ref[(m - 1) * ROWS : m * ROWS, :] = value
        elif m == 4:
            far_ref[...] = value
        else:
            swap_ref[(m - 5) * ROWS : (m - 4) * ROWS, :] = value


def keep_sum_kernel(keep_ref, far_ref, sums_ref, out_ref, passed_ref):
    out_ref[...] = keep_ref[...].astype(jnp.float32) + far_ref[...].astype(jnp.float32)
    passed_ref[...] = sums_ref[...]


def last_sum_kernel(
    core_ref, sums_ref, keep_ref, a_ref, b_ref, c_ref, hold_ref, send_ref, passed_ref
):
    passed_ref[...] = sums_ref[...]
    core = core_ref[0]
    half = ROWS // 2

    def total(first):
        at = slice(first, first + half)
        value = a_ref[at, :].astype(jnp.float32) + b_ref[at, :].astype(jnp.float32)
        value = value + c_ref[at, :].astype(jnp.float32)
        if first < ROWS:
            value = value + keep_ref[at, :]
        return value

    for n in range(2):
        low, high = total(n * ROWS), total(n * ROWS + half)
        at = slice(n * half, (n + 1) * half)
        hold_ref[at, :] = jnp.where(core == 0, low, high)
        send_ref[at, :] = jnp.where(core == 0, high, low)


def turn_kernel(core_ref, hold_ref, got_ref, sums_ref, out_ref, weight_ref, bias_ref):
    core = core_ref[0]
    half = ROWS // 2
    for b in range(NB // 2):
        first = slice(b * HALF, (b + 1) * HALF)
        second = slice(half + b * HALF, half + (b + 1) * HALF)
        own = hold_ref[first, :] + got_ref[second, :]
        other = hold_ref[second, :] + got_ref[first, :]
        both = jnp.concatenate(
            [jnp.where(core == 0, own, other), jnp.where(core == 0, other, own)], axis=0
        )
        out_ref[b * BLK : (b + 1) * BLK, :] = both.T
    weight_ref[...] = sums_ref[:BLK, :] * NORM
    bias_ref[...] = sums_ref[BLK : BLK + 1, :] * NORM


def butterfly(value, target, size):
    step = 1
    while step < size:
        value = value + moved(value, functools.partial(target, step))
        step *= 2
    return value


def shards(features, weight, out_bias, edge_tiles, block_row, tile_slot, send_list, out_grad):
    bf16, f32, i32 = jnp.bfloat16, jnp.float32, jnp.int32
    node = lax.axis_index("nodes")
    core = lax.axis_index("rep")
    y, z, x = node // (NZ * NX), node // NX % NZ, node % NX
    core_array = jnp.reshape(core, (1,)).astype(i32)
    dma = pltpu.SemaphoreType.DMA

    own_meta = jnp.concatenate(
        [jnp.concatenate([tile_slot, block_row])[None, :], send_list.T], axis=0
    )
    other_meta = to_other_core(own_meta)
    tiles = jnp.concatenate([edge_tiles, to_other_core(edge_tiles)], axis=0)

    message, half_message = call(
        message_kernel,
        [struct((MSG + ROWS, BLK), bf16), struct((MSG, BLK), bf16)],
        [SMEM, VMEM, VMEM, VMEM],
        [VMEM] * 2,
        moved_bytes=500000,
    )(core_array, features, own_meta, other_meta)
    first, second = along_z(message, 1), along_z(message, 2)
    first, second = lax.optimization_barrier((first, second))
    across, third = along_z(second[:MSG], 2), along_z(second, 1)
    swapped = to_other_core(jnp.concatenate([first[ROWS:], second[ROWS:]], axis=0))
    swapped = [swapped[:MSG], swapped[MSG:], to_other_core(third[ROWS:])]
    column = [half_message, first[:MSG], second[:MSG], third[:MSG], across]
    for piece in swapped:
        column += [piece[MSG - ROWS :], piece[: MSG - ROWS]]
    column = jnp.concatenate(column, axis=0)

    slot = jnp.concatenate([own_meta[0, :64], other_meta[0, :64]])
    rows = jnp.concatenate([own_meta[0, 64:], other_meta[0, 64:]]) - node * NB
    source, which = slot // 2, slot % 2
    step_y = (source // (NZ * NX) - y) % NY
    step_z = (source // NX - z) % NZ
    step_x = (source - x) % NX
    dense = jnp.where(core == 0, step_y, step_x)
    sparse = jnp.where(core == 0, step_x, step_y)
    step_z = jnp.where(core == 0, (NZ - step_z) % NZ, step_z)
    step_z = jnp.where(step_z <= 4, step_z, 12 - step_z)
    holder = jnp.where(jnp.arange(TILES) < 64, core, 1 - core)
    code = (dense * 4 + sparse) * 128 + (dense * NZ + step_z) * 4 + holder * 2 + which
    info, *requests = call(
        plan_kernel,
        [struct((INFO,), i32)] + [struct((128,), i32)] * 3,
        [SMEM] * 2,
        [SMEM] * 4,
        [pltpu.SMEM((8,), i32)],
        moved_bytes=100000,
    )(code.astype(i32), rows)
    requests = [along_sparse(requests[k - 1], k) for k in (1, 2, 3)]

    column, *requests = lax.optimization_barrier((column, *requests))
    parts = [column] + [along_dense(column, -j) for j in range(1, 4)]

    away = jnp.arange(4)
    asker = jnp.where(
        core == 0,
        node - x + (x - away) % NX,
        node - y * (NZ * NX) + (y - away) % NY * (NZ * NX),
    )
    lists = jnp.stack([part.reshape(NZ, MSG, BLK)[:, ROWS : ROWS + 4] for part in parts])
    chosen = (jnp.arange(BLK)[:, None] == asker[None, :]).astype(bf16)
    table = jnp.dot(lists.reshape(4 * NZ * 4, BLK), chosen, preferred_element_type=f32)
    table = table.astype(i32).reshape(-1)

    picked = call(
        pick_kernel,
        [struct((FAR, BLK), bf16)] * 3,
        [VMEM] * 4 + [ANY] * 4,
        [VMEM] * 3,
        [pltpu.SMEM((128,), i32)] * 3 + [pltpu.SMEM((512,), i32), dma((4,))],
        moved_bytes=7000000,
    )(*parts, *requests, table)
    far = [along_sparse(picked[k - 1], -k) for k in (1, 2, 3)]

    near = call(
        near_kernel,
        struct((ROWS, BLK), f32),
        [VMEM] * 5 + [ANY] * 2,
        VMEM,
        [
            pltpu.VMEM((ROWS + HALF, BLK), f32),
            pltpu.SMEM((INFO,), i32),
            pltpu.SMEM((512,), i32),
            dma((2,)),
        ],
        flops=2 * 32 * HALF * BLK * BLK,
        moved_bytes=11000000,
    )(*parts, tiles, info, table)
    agg_half = near
    for steps, kind in (((1, 3), f32), ((2,), bf16)):
        agg_half = call(
            functools.partial(far_kernel, steps),
            struct((ROWS, BLK), kind),
            [VMEM] * (2 + len(steps)) + [ANY],
            VMEM,
            [pltpu.VMEM((ROWS + HALF, BLK), f32), pltpu.SMEM((INFO,), i32), dma((1,))],
            flops=2 * 32 * len(steps) * HALF * BLK * BLK,
            moved_bytes=7000000,
        )(agg_half, *[far[k - 1] for k in steps], tiles, info)
    other_half = to_other_core(agg_half)

    activations, sums, turned, second_back = call(
        middle_kernel,
        [
            struct((NB * BLK, BLK), bf16),
            struct((SUMS, BLK), f32),
            struct((ROWS, BLK), bf16),
            struct((FAR, BLK), bf16),
        ],
        [SMEM] + [VMEM] * 6 + [ANY],
        [VMEM] * 4,
        [pltpu.SMEM((INFO,), i32), dma((1,))],
        flops=2 * TILES * HALF * BLK * BLK,
        moved_bytes=8000000,
    )(
        core_array, agg_half, other_half, weight, out_bias[None, :], out_grad, tiles, info
    )
    first_back, third_back = call(
        side_kernel,
        [struct((FAR, BLK), bf16)] * 2,
        [VMEM] * 2 + [ANY],
        [VMEM] * 2,
        [pltpu.SMEM((INFO,), i32), dma((1,))],
        flops=2 * 64 * HALF * BLK * BLK,
        moved_bytes=4000000,
    )(tiles, turned, info)
    second_back = along_sparse(second_back, 2)
    back = [along_sparse(first_back, 1), second_back, along_sparse(third_back, 3)]

    sums = butterfly(sums, lambda step, y, z, x, c: (y, z ^ step, x, c), NZ)
    owned = call(
        owner_kernel,
        [struct((SEND, BLK), bf16)] + [struct((SEND, BLK), bf16)] * 3,
        [ANY] * 5 + [VMEM] * 6,
        [VMEM] * 4,
        [
            pltpu.VMEM((257 * HALF, BLK), f32),
            pltpu.SMEM((INFO,), i32),
            pltpu.SMEM((512,), i32),
        ]
        + [pltpu.SMEM((128,), i32)] * 3
        + [dma((5,))],
        flops=2 * 32 * HALF * BLK * BLK,
        moved_bytes=11000000,
        vmem=21,
    )(info, table, *requests, turned, tiles, *back, sums)
    owned = [owned[0]] + [along_dense(owned[j], j) for j in range(1, 4)]
    keep, opposite, mine, swap, sums = call(
        split_sum_kernel,
        [struct((ROWS, BLK), bf16)] * 2
        + [struct((3 * ROWS, BLK), bf16)] * 2
        + [struct((SUMS, BLK), f32)],
        [VMEM] * 5,
        [VMEM] * 5,
        moved_bytes=5000000,
    )(*owned, sums)
    opposite = along_z(opposite, 4)
    swap = to_other_core(swap)
    pieces = [
        jnp.concatenate([mine[s * ROWS : (s + 1) * ROWS], swap[s * ROWS : (s + 1) * ROWS]], axis=0)
        for s in range(3)
    ]
    pieces = [along_z(pieces[s - 1], -s) for s in (3, 2, 1)][::-1]
    sums = butterfly(sums, lambda step, y, z, x, c: (y ^ step, z, x, c), NY)
    keep, sums = call(
        keep_sum_kernel,
        [struct((ROWS, BLK), f32), struct((SUMS, BLK), f32)],
        [VMEM] * 3,
        [VMEM] * 2,
        moved_bytes=500000,
    )(keep, opposite, sums)
    sums = butterfly(sums, lambda step, y, z, x, c: (y, z, x ^ step, c), NX)

    hold, send, sums = call(
        last_sum_kernel,
        [struct((ROWS, BLK), f32)] * 2 + [struct((SUMS, BLK), f32)],
        [SMEM] + [VMEM] * 5,
        [VMEM] * 3,
        moved_bytes=1500000,
    )(core_array, sums, keep, *pieces)
    feature_grad, weight_grad, bias_grad = call(
        turn_kernel,
        [struct((NB // 2 * BLK, BLK), f32), struct((BLK, BLK), f32), struct((1, BLK), f32)],
        [SMEM] + [VMEM] * 3,
        [VMEM] * 3,
        moved_bytes=1000000,
    )(core_array, hold, to_other_core(send), sums)

    def again(state):
        return (jnp.float32(0.0),) + general_shards(
            features, weight, out_bias, edge_tiles, block_row, tile_slot, send_list, out_grad
        )

    state = (sums[BLK + 1, 0], activations, feature_grad, weight_grad, bias_grad.reshape(-1))
    return lax.while_loop(lambda state: state[0] > 0.5, again, state)[1:]


def solution(mesh):
    placed = (
        P("nodes", None),
        P(),
        P(),
        P(("nodes", "rep"), None, None),
        P(("nodes", "rep")),
        P(("nodes", "rep")),
        P(("nodes", "rep"), None),
        P("nodes", None),
    )
    return jax.shard_map(
        shards,
        mesh=mesh,
        in_specs=placed,
        out_specs=(P("nodes", "rep"), P(("nodes", "rep"), None), P(None, "rep"), P("rep")),
        check_vma=False,
    )
```

```python
import functools
import math

import jax
import jax.numpy as jnp
from jax import lax
from jax.experimental import pallas as pl
from jax.experimental.pallas import tpu as pltpu
from jax.sharding import PartitionSpec as P

ROOT_TWO_PI = 0.7978845608028654
CUBIC_TERM = 0.044715

NY, NZ, NX = 4, 8, 4
BLK = 128
HALF = 64
NB = 8
CAP = 56
ROWS = NB * HALF
MSG = ROWS + 16
PART = NZ * MSG
LOCAL = NY * PART
FAR = CAP * HALF
TILES = 128
LOC0, REM0, CNT0, OVER, ROW0 = 128, 256, 440, 444, 512
INFO = 640
SUMS = BLK + 16
SEND = 64 * HALF


def gelu_value(values):
    inner_term = ROOT_TWO_PI * (values + CUBIC_TERM * values * values * values)
    return 0.5 * values * (1.0 + jnp.tanh(inner_term))


def gelu_slope(values):
    tangent = jnp.tanh(ROOT_TWO_PI * (values + CUBIC_TERM * values * values * values))
    outer_part = 0.5 * values * (1.0 - tangent * tangent) * ROOT_TWO_PI
    return 0.5 * (1.0 + tangent) + outer_part * (1.0 + 3.0 * CUBIC_TERM * values * values)


def general_shards(features, weight, out_bias, edge_tiles, block_row, tile_slot, send_list, out_grad):
    node_count = lax.axis_size("nodes")
    rep_count = lax.axis_size("rep")
    rep_position = lax.axis_index("rep")
    block_size = edge_tiles.shape[1]
    local_blocks = features.shape[0] // block_size
    width_in = features.shape[1]
    capacity = send_list.shape[1]
    half_out = weight.shape[1] // rep_count
    feature_blocks = features.reshape(local_blocks, block_size, width_in)
    outgoing = feature_blocks[send_list]
    incoming = lax.all_to_all(outgoing, "nodes", split_axis=0, concat_axis=0, tiled=True)
    incoming = incoming.reshape(node_count * capacity, block_size, width_in)
    picked = incoming[tile_slot]
    products = jnp.einsum("tij,tjf->tif", edge_tiles, picked, preferred_element_type=jnp.float32)
    local_rows = block_row - lax.axis_index("nodes") * local_blocks
    partial_value = jax.ops.segment_sum(products, local_rows, num_segments=local_blocks)
    partial_value = partial_value.reshape(local_blocks * block_size, width_in)
    aggregate_bf = lax.psum(partial_value, "rep").astype(jnp.bfloat16)
    preact = jnp.dot(aggregate_bf, weight, preferred_element_type=jnp.float32) + out_bias
    own_preact = lax.dynamic_slice_in_dim(preact, rep_position * half_out, half_out, 1)
    activations = gelu_value(own_preact).astype(jnp.bfloat16)
    pre_grad = (out_grad.astype(jnp.float32) * gelu_slope(preact)).astype(jnp.bfloat16)
    agg_grad = lax.dot_general(
        pre_grad, weight, (((1,), (1,)), ((), ())), preferred_element_type=jnp.float32
    ).astype(jnp.bfloat16)
    grad_rows = agg_grad.reshape(local_blocks, block_size, width_in)[local_rows]
    back_products = jnp.einsum(
        "tji,tjf->tif", edge_tiles, grad_rows, preferred_element_type=jnp.float32
    )
    slot_sums = jax.ops.segment_sum(back_products, tile_slot, num_segments=node_count * capacity)
    slot_sums = slot_sums.astype(jnp.bfloat16)
    returned = lax.all_to_all(
        slot_sums.reshape(node_count, capacity, block_size, width_in),
        "nodes",
        split_axis=0,
        concat_axis=0,
        tiled=True,
    )
    returned = returned.astype(jnp.float32)
    owner_sums = jax.ops.segment_sum(
        returned.reshape(node_count * capacity, block_size, width_in),
        send_list.reshape(-1),
        num_segments=local_blocks,
    )
    feature_grad = lax.psum_scatter(
        owner_sums.reshape(local_blocks * block_size, width_in).astype(jnp.bfloat16),
        "rep",
        scatter_dimension=0,
        tiled=True,
    ).astype(jnp.float32)
    own_grad = lax.dynamic_slice_in_dim(pre_grad, rep_position * half_out, half_out, 1)
    norm_scale = 1.0 / math.sqrt(features.shape[0] * node_count)
    weight_part = lax.dot_general(
        aggregate_bf, own_grad, (((0,), (0,)), ((), ())), preferred_element_type=jnp.float32
    )
    bias_part = jnp.sum(own_grad.astype(jnp.float32), axis=0)
    weight_sum, bias_sum = lax.psum((weight_part, bias_part), "nodes")
    return (activations, feature_grad, weight_sum * norm_scale, bias_sum * norm_scale)


def device_of(y, z, x, c):
    return ((y % NY * NZ + z % NZ) * NX + x % NX) * 2 + c


def moved(value, target):
    pairs = [
        (device_of(y, z, x, c), device_of(*target(y, z, x, c)))
        for y in range(NY)
        for z in range(NZ)
        for x in range(NX)
        for c in range(2)
    ]
    return lax.ppermute(value, ("nodes", "rep"), pairs)


def along_z(value, step):
    return moved(value, lambda y, z, x, c: (y, z + step if c == 0 else z - step, x, c))


def along_dense(value, step):
    return moved(value, lambda y, z, x, c: (y + step, z, x, c) if c == 0 else (y, z, x + step, c))


def along_sparse(value, step):
    return moved(value, lambda y, z, x, c: (y, z, x + step, c) if c == 0 else (y + step, z, x, c))


def to_other_core(value):
    return moved(value, lambda y, z, x, c: (y, z, x, 1 - c))


SMEM = pl.BlockSpec(memory_space=pltpu.SMEM)
VMEM = pl.BlockSpec(memory_space=pltpu.VMEM)
ANY = pl.BlockSpec(memory_space=pl.ANY)


def call(kernel, out_shape, in_specs, out_specs, scratch=(), flops=0, moved_bytes=0, vmem=12):
    return pl.pallas_call(
        kernel,
        out_shape=out_shape,
        in_specs=in_specs,
        out_specs=out_specs,
        scratch_shapes=list(scratch),
        compiler_params=pltpu.CompilerParams(vmem_limit_bytes=vmem << 20),
        cost_estimate=pl.CostEstimate(flops=flops, bytes_accessed=moved_bytes, transcendentals=0),
    )


def struct(shape, dtype):
    return jax.ShapeDtypeStruct(shape, dtype)


def message_kernel(core_ref, features_ref, own_ref, other_ref, out_ref, half_ref):
    core = core_ref[0]
    for block in range(NB):
        turned = features_ref[block * BLK : (block + 1) * BLK, :].astype(jnp.float32).T
        mine = jnp.where(core == 0, turned[:HALF], turned[HALF:]).astype(jnp.bfloat16)
        rest = jnp.where(core == 0, turned[HALF:], turned[:HALF]).astype(jnp.bfloat16)
        out_ref[block * HALF : (block + 1) * HALF, :] = mine
        half_ref[block * HALF : (block + 1) * HALF, :] = mine
        out_ref[MSG + block * HALF : MSG + (block + 1) * HALF, :] = rest
    own, other = own_ref[1:3, :], other_ref[1:3, :]
    lists = jnp.concatenate(
        [
            jnp.where(core == 0, own, other),
            jnp.where(core == 0, other, own),
            jnp.zeros((12, BLK), jnp.int32),
        ],
        axis=0,
    )
    lists = lists.astype(jnp.float32).astype(jnp.bfloat16)
    out_ref[ROWS:MSG, :] = lists
    half_ref[ROWS:MSG, :] = lists


def plan_kernel(code_ref, rows_ref, info_ref, first_ref, second_ref, third_ref, count_ref):
    requests = (first_ref, second_ref, third_ref)
    for k in range(8):
        count_ref[k] = 0

    def clear(i, carry):
        for ref in requests:
            ref[i] = 0
        info_ref[i] = 0
        info_ref[LOC0 + i] = 0
        info_ref[REM0 + i] = 0
        info_ref[REM0 + 128 + i] = 0
        info_ref[ROW0 + i] = rows_ref[i]
        return carry

    lax.fori_loop(0, 128, clear, 0)

    def place(t, carry):
        code = code_ref[t]
        other_key = code >> 9
        key = (code >> 7) & 3
        slot = code & 127
        count_ref[4 + other_key] = count_ref[4 + other_key] + 1
        rank = count_ref[key]
        count_ref[key] = rank + 1

        @pl.when(key == 0)
        def _():
            info_ref[rank] = slot
            info_ref[LOC0 + rank] = t

        @pl.when(jnp.logical_and(key > 0, rank < CAP))
        def _():
            info_ref[REM0 + (key - 1) * CAP + rank] = t
            for k in (1, 2, 3):

                @pl.when(key == k)
                def _():
                    requests[k - 1][rank] = slot

        return carry

    lax.fori_loop(0, TILES, place, 0)
    over = 0
    info_ref[CNT0] = count_ref[0]
    for k in (1, 2, 3):
        kept = jnp.minimum(count_ref[k], CAP)
        info_ref[CNT0 + k] = kept
        requests[k - 1][64] = kept
        over += count_ref[k] - kept
        over += jnp.maximum(count_ref[4 + k] - CAP, 0)
    info_ref[OVER] = over


def start_all(pairs, sem):
    copies = [pltpu.make_async_copy(src, dst, sem.at[n]) for n, (src, dst) in enumerate(pairs)]
    for copy in copies:
        copy.start()
    return copies


def wait_all(copies):
    for copy in copies:
        copy.wait()


def half_rows(index):
    return pl.ds(pl.multiple_of(index * HALF, HALF), HALF)


def local_block(parts, slot, table, k):
    row = ((slot >> 2) & (NZ - 1)) * MSG + (table[(slot << 2) + k] << 6)
    at = pl.ds(pl.multiple_of(row, 16), HALF)
    part = slot >> 5
    low = jnp.where(part == 0, parts[0][at, :], parts[1][at, :])
    high = jnp.where(part == 2, parts[2][at, :], parts[3][at, :])
    return jnp.where(part < 2, low, high)


def pick_kernel(
    a_ref, b_ref, c_ref, d_ref, first_ref, second_ref, third_ref, table_ref, o1, o2, o3,
    q1, q2, q3, table, sem,
):
    parts = (a_ref, b_ref, c_ref, d_ref)
    wait_all(
        start_all([(first_ref, q1), (second_ref, q2), (third_ref, q3), (table_ref, table)], sem)
    )
    for k, (req, out) in enumerate(((q1, o1), (q2, o2), (q3, o3))):

        def body(i, carry, req=req, out=out, k=k):
            blocks = [local_block(parts, req[i * 8 + u], table, k + 1) for u in range(8)]
            for u in range(8):
                out[half_rows(i * 8 + u), :] = blocks[u]
            return carry

        lax.fori_loop(0, CAP // 8, body, 0)


def near_kernel(
    a_ref, b_ref, c_ref, d_ref, tiles, info_ref, table_ref, out_ref, acc, info, table, sem
):
    parts = (a_ref, b_ref, c_ref, d_ref)
    copies = start_all([(info_ref, info), (table_ref, table)], sem)
    acc[...] = jnp.zeros_like(acc)
    wait_all(copies)
    count = info[CNT0]

    def body(i, carry):
        done = []
        for u in range(8):
            p = i * 8 + u
            block = local_block(parts, info[p], table, 0)
            done.append(
                lax.dot_general(
                    block, tiles[info[LOC0 + p]], (((1,), (1,)), ((), ())),
                    preferred_element_type=jnp.float32,
                )
            )
        for u in range(8):
            p = i * 8 + u
            row = jnp.where(p < count, info[ROW0 + info[LOC0 + p]], NB)
            acc[half_rows(row), :] += done[u]
        return carry

    lax.fori_loop(0, (count + 7) >> 3, body, 0)
    out_ref[...] = acc[:ROWS, :]


def far_kernel(steps, near_ref, *refs):
    *moved_refs, tiles, info_ref, out_ref, acc, info, sem = refs
    copies = start_all([(info_ref, info)], sem)
    acc[:ROWS, :] = near_ref[...]
    acc[ROWS:, :] = jnp.zeros((HALF, BLK), jnp.float32)
    wait_all(copies)
    for k, got in zip(steps, moved_refs):
        count = info[CNT0 + k]

        def body(i, carry, k=k, got=got, count=count):
            done = []
            for u in range(8):
                p = i * 8 + u
                done.append(
                    lax.dot_general(
                        got[half_rows(p), :], tiles[info[REM0 + (k - 1) * CAP + p]],
                        (((1,), (1,)), ((), ())), preferred_element_type=jnp.float32,
                    )
                )
            for u in range(8):
                p = i * 8 + u
                row = jnp.where(p < count, info[ROW0 + info[REM0 + (k - 1) * CAP + p]], NB)
                acc[half_rows(row), :] += done[u]
            return carry

        lax.fori_loop(0, (count + 7) >> 3, body, 0)
    out_ref[...] = acc[:ROWS, :].astype(out_ref.dtype)


def products(step, tiles, turned_ref, info, out):
    first = REM0 + (step - 1) * CAP

    def body(i, carry):
        done = []
        for u in range(8):
            t = info[first + i * 8 + u]
            left = turned_ref[half_rows(info[ROW0 + t]), :]
            done.append(jnp.dot(left, tiles[t], preferred_element_type=jnp.float32))
        for u in range(8):
            out[half_rows(i * 8 + u), :] = done[u].astype(jnp.bfloat16)
        return carry

    lax.fori_loop(0, (info[CNT0 + step] + 7) >> 3, body, 0)


def middle_kernel(
    core_ref, own_agg, other_agg, weight_ref, bias_ref, grad_ref, tiles, info_ref,
    act_ref, sums_ref, turned_ref, out, info, sem,
):
    copies = start_all([(info_ref, info)], sem)
    core = core_ref[0]
    sums_ref[...] = jnp.zeros_like(sums_ref)
    weight_half = weight_ref[half_rows(core), :]

    def block_step(b, carry):
        own, other = own_agg[half_rows(b), :], other_agg[half_rows(b), :]
        low = jnp.where(core == 0, own, other)
        high = jnp.where(core == 0, other, own)
        agg = jnp.concatenate([low, high], axis=0)
        preact = lax.dot_general(
            agg, weight_ref[...], (((0,), (0,)), ((), ())), preferred_element_type=jnp.float32
        )
        preact = preact + bias_ref[...]
        tangent = jnp.tanh(ROOT_TWO_PI * (preact + CUBIC_TERM * preact * preact * preact))
        nodes = pl.ds(pl.multiple_of(b * BLK, BLK), BLK)
        value = 0.5 * preact * (1.0 + tangent)
        act_ref[nodes, :] = jnp.where(core == 0, value[:, :BLK], value[:, BLK:]).astype(jnp.bfloat16)
        outer = 0.5 * preact * (1.0 - tangent * tangent) * ROOT_TWO_PI
        slope = 0.5 * (1.0 + tangent) + outer * (1.0 + 3.0 * CUBIC_TERM * preact * preact)
        pre = (grad_ref[nodes, :].astype(jnp.float32) * slope).astype(jnp.bfloat16)
        turned_ref[half_rows(b), :] = lax.dot_general(
            weight_half, pre, (((1,), (1,)), ((), ())), preferred_element_type=jnp.float32
        ).astype(jnp.bfloat16)
        mine = jnp.where(core == 0, pre[:, :BLK], pre[:, BLK:])
        sums_ref[:BLK, :] += lax.dot_general(
            agg, mine, (((1,), (0,)), ((), ())), preferred_element_type=jnp.float32
        )
        sums_ref[BLK : BLK + 1, :] += jnp.sum(mine.astype(jnp.float32), axis=0, keepdims=True)
        return carry

    lax.fori_loop(0, NB, block_step, 0, unroll=2)
    wait_all(copies)
    over = info[OVER].astype(jnp.float32)
    sums_ref[BLK + 1 : BLK + 2, :] = jnp.full((1, BLK), over, jnp.float32)
    products(2, tiles, turned_ref, info, out)


def side_kernel(tiles, turned_ref, info_ref, o1, o3, info, sem):
    wait_all(start_all([(info_ref, info)], sem))
    products(1, tiles, turned_ref, info, o1)
    products(3, tiles, turned_ref, info, o3)


NORM = 1.0 / math.sqrt(NY * NZ * NX * NB * BLK)


def owner_kernel(
    info_ref, table_ref, first_ref, second_ref, third_ref, turned_ref, tiles,
    r1, r2, r3, sums_ref, o0, o1, o2, o3, passed_ref, total, info, table, q1, q2, q3, sem,
):
    passed_ref[...] = sums_ref[...]
    copies = start_all(
        [(info_ref, info), (table_ref, table), (first_ref, q1), (second_ref, q2), (third_ref, q3)],
        sem,
    )
    total[...] = jnp.zeros_like(total)
    wait_all(copies)

    def total_rows(slot, k, used):
        return half_rows(jnp.where(used, ((slot >> 2) << 3) + table[(slot << 2) + k], 256))

    count = info[CNT0]

    def near(i, carry):
        done = []
        for u in range(8):
            t = info[LOC0 + i * 8 + u]
            left = turned_ref[half_rows(info[ROW0 + t]), :]
            done.append(jnp.dot(left, tiles[t], preferred_element_type=jnp.float32))
        for u in range(8):
            p = i * 8 + u
            total[total_rows(info[p], 0, p < count), :] += done[u]
        return carry

    lax.fori_loop(0, (count + 7) >> 3, near, 0)
    for k, (req, got) in enumerate(((q1, r1), (q2, r2), (q3, r3))):
        kept = req[64]

        def far(i, carry, req=req, got=got, k=k, kept=kept):
            for u in range(8):
                p = i * 8 + u
                at = total_rows(req[p], k + 1, p < kept)
                total[at, :] += got[half_rows(p), :].astype(jnp.float32)
            return carry

        lax.fori_loop(0, (kept + 7) >> 3, far, 0)
    for j, out in enumerate((o0, o1, o2, o3)):
        out[...] = total[j * SEND : (j + 1) * SEND, :].astype(jnp.bfloat16)


def split_sum_kernel(
    a_ref, b_ref, c_ref, d_ref, sums_ref, keep_ref, far_ref, mine_ref, swap_ref, passed_ref
):
    passed_ref[...] = sums_ref[...]
    for m in range(NZ):
        at = slice(m * ROWS, (m + 1) * ROWS)
        value = a_ref[at, :].astype(jnp.float32) + b_ref[at, :].astype(jnp.float32)
        value = value + (c_ref[at, :].astype(jnp.float32) + d_ref[at, :].astype(jnp.float32))
        value = value.astype(jnp.bfloat16)
        if m == 0:
            keep_ref[...] = value
        elif m < 4:
            mine_ref[(m - 1) * ROWS : m * ROWS, :] = value
        elif m == 4:
            far_ref[...] = value
        else:
            swap_ref[(m - 5) * ROWS : (m - 4) * ROWS, :] = value


def relay_kernel(mine_ref, swap_ref, third_ref, far_ref, sums_ref, out_ref, passed_ref):
    passed_ref[...] = sums_ref[...]
    at = slice(ROWS, 2 * ROWS)
    own = mine_ref[at, :].astype(jnp.float32) + third_ref[:ROWS, :].astype(jnp.float32)
    out_ref[:ROWS, :] = (own + far_ref[...].astype(jnp.float32)).astype(jnp.bfloat16)
    other = swap_ref[at, :].astype(jnp.float32) + third_ref[ROWS:, :].astype(jnp.float32)
    out_ref[ROWS:, :] = other.astype(jnp.bfloat16)


def last_sum_kernel(
    core_ref, sums_ref, keep_ref, a_ref, b_ref, hold_ref, send_ref, passed_ref
):
    passed_ref[...] = sums_ref[...]
    core = core_ref[0]
    half = ROWS // 2

    def total(first):
        at = slice(first, first + half)
        value = a_ref[at, :].astype(jnp.float32) + b_ref[at, :].astype(jnp.float32)
        if first < ROWS:
            value = value + keep_ref[at, :].astype(jnp.float32)
        return value

    for n in range(2):
        low, high = total(n * ROWS), total(n * ROWS + half)
        at = slice(n * half, (n + 1) * half)
        hold_ref[at, :] = jnp.where(core == 0, low, high)
        send_ref[at, :] = jnp.where(core == 0, high, low)


def turn_kernel(core_ref, hold_ref, got_ref, sums_ref, out_ref, weight_ref, bias_ref):
    core = core_ref[0]
    half = ROWS // 2
    for b in range(NB // 2):
        first = slice(b * HALF, (b + 1) * HALF)
        second = slice(half + b * HALF, half + (b + 1) * HALF)
        own = hold_ref[first, :] + got_ref[second, :]
        other = hold_ref[second, :] + got_ref[first, :]
        both = jnp.concatenate(
            [jnp.where(core == 0, own, other), jnp.where(core == 0, other, own)], axis=0
        )
        out_ref[b * BLK : (b + 1) * BLK, :] = both.T
    weight_ref[...] = sums_ref[:BLK, :] * NORM
    bias_ref[...] = sums_ref[BLK : BLK + 1, :] * NORM


def butterfly(value, target, steps):
    for step in steps:
        value = value + moved(value, functools.partial(target, step))
    return value


def across_y(step, y, z, x, c):
    return (y ^ step, z, x, c)


def across_z(step, y, z, x, c):
    return (y, z ^ step, x, c)


def across_x(step, y, z, x, c):
    return (y, z, x ^ step, c)


def shards(features, weight, out_bias, edge_tiles, block_row, tile_slot, send_list, out_grad):
    bf16, f32, i32 = jnp.bfloat16, jnp.float32, jnp.int32
    node = lax.axis_index("nodes")
    core = lax.axis_index("rep")
    y, z, x = node // (NZ * NX), node // NX % NZ, node % NX
    core_array = jnp.reshape(core, (1,)).astype(i32)
    dma = pltpu.SemaphoreType.DMA

    own_meta = jnp.concatenate(
        [jnp.concatenate([tile_slot, block_row])[None, :], send_list.T], axis=0
    )
    other_meta = to_other_core(own_meta)
    tiles = jnp.concatenate([edge_tiles, to_other_core(edge_tiles)], axis=0)

    message, half_message = call(
        message_kernel,
        [struct((MSG + ROWS, BLK), bf16), struct((MSG, BLK), bf16)],
        [SMEM, VMEM, VMEM, VMEM],
        [VMEM] * 2,
        moved_bytes=500000,
    )(core_array, features, own_meta, other_meta)
    first, second = along_z(message, 1), along_z(message, 2)
    first, second = lax.optimization_barrier((first, second))
    across, third = along_z(second[:MSG], 2), along_z(second, 1)
    swapped = to_other_core(jnp.concatenate([first[ROWS:], second[ROWS:]], axis=0))
    swapped = [swapped[:MSG], swapped[MSG:], to_other_core(third[ROWS:])]
    column = [half_message, first[:MSG], second[:MSG], third[:MSG], across]
    for piece in swapped:
        column += [piece[MSG - ROWS :], piece[: MSG - ROWS]]
    column = jnp.concatenate(column, axis=0)

    slot = jnp.concatenate([own_meta[0, :64], other_meta[0, :64]])
    rows = jnp.concatenate([own_meta[0, 64:], other_meta[0, 64:]]) - node * NB
    source, which = slot // 2, slot % 2
    step_y = (source // (NZ * NX) - y) % NY
    step_z = (source // NX - z) % NZ
    step_x = (source - x) % NX
    dense = jnp.where(core == 0, step_y, step_x)
    sparse = jnp.where(core == 0, step_x, step_y)
    step_z = jnp.where(core == 0, (NZ - step_z) % NZ, step_z)
    step_z = jnp.where(step_z <= 4, step_z, 12 - step_z)
    holder = jnp.where(jnp.arange(TILES) < 64, core, 1 - core)
    code = (dense * 4 + sparse) * 128 + (dense * NZ + step_z) * 4 + holder * 2 + which
    info, *requests = call(
        plan_kernel,
        [struct((INFO,), i32)] + [struct((128,), i32)] * 3,
        [SMEM] * 2,
        [SMEM] * 4,
        [pltpu.SMEM((8,), i32)],
        moved_bytes=100000,
    )(code.astype(i32), rows)
    requests = [along_sparse(requests[k - 1], k) for k in (1, 2, 3)]

    column, *requests = lax.optimization_barrier((column, *requests))
    parts = [column] + [along_dense(column, -j) for j in range(1, 4)]

    away = jnp.arange(4)
    asker = jnp.where(
        core == 0,
        node - x + (x - away) % NX,
        node - y * (NZ * NX) + (y - away) % NY * (NZ * NX),
    )
    lists = jnp.stack([part.reshape(NZ, MSG, BLK)[:, ROWS : ROWS + 4] for part in parts])
    chosen = (jnp.arange(BLK)[:, None] == asker[None, :]).astype(bf16)
    table = jnp.dot(lists.reshape(4 * NZ * 4, BLK), chosen, preferred_element_type=f32)
    table = table.astype(i32).reshape(-1)

    picked = call(
        pick_kernel,
        [struct((FAR, BLK), bf16)] * 3,
        [VMEM] * 4 + [ANY] * 4,
        [VMEM] * 3,
        [pltpu.SMEM((128,), i32)] * 3 + [pltpu.SMEM((512,), i32), dma((4,))],
        moved_bytes=7000000,
    )(*parts, *requests, table)
    far = [along_sparse(picked[k - 1], -k) for k in (1, 2, 3)]

    near = call(
        near_kernel,
        struct((ROWS, BLK), f32),
        [VMEM] * 5 + [ANY] * 2,
        VMEM,
        [
            pltpu.VMEM((ROWS + HALF, BLK), f32),
            pltpu.SMEM((INFO,), i32),
            pltpu.SMEM((512,), i32),
            dma((2,)),
        ],
        flops=2 * 32 * HALF * BLK * BLK,
        moved_bytes=11000000,
    )(*parts, tiles, info, table)
    agg_half = near
    for steps, kind in (((1,), f32), ((3,), f32), ((2,), bf16)):
        agg_half = call(
            functools.partial(far_kernel, steps),
            struct((ROWS, BLK), kind),
            [VMEM] * (2 + len(steps)) + [ANY],
            VMEM,
            [pltpu.VMEM((ROWS + HALF, BLK), f32), pltpu.SMEM((INFO,), i32), dma((1,))],
            flops=2 * 32 * len(steps) * HALF * BLK * BLK,
            moved_bytes=7000000,
        )(agg_half, *[far[k - 1] for k in steps], tiles, info)
    other_half = to_other_core(agg_half)

    activations, sums, turned, second_back = call(
        middle_kernel,
        [
            struct((NB * BLK, BLK), bf16),
            struct((SUMS, BLK), f32),
            struct((ROWS, BLK), bf16),
            struct((FAR, BLK), bf16),
        ],
        [SMEM] + [VMEM] * 6 + [ANY],
        [VMEM] * 4,
        [pltpu.SMEM((INFO,), i32), dma((1,))],
        flops=2 * TILES * HALF * BLK * BLK,
        moved_bytes=8000000,
    )(
        core_array, agg_half, other_half, weight, out_bias[None, :], out_grad, tiles, info
    )
    first_back, third_back = call(
        side_kernel,
        [struct((FAR, BLK), bf16)] * 2,
        [VMEM] * 2 + [ANY],
        [VMEM] * 2,
        [pltpu.SMEM((INFO,), i32), dma((1,))],
        flops=2 * 64 * HALF * BLK * BLK,
        moved_bytes=4000000,
    )(tiles, turned, info)
    second_back = along_sparse(second_back, 2)
    back = [along_sparse(first_back, 1), second_back, along_sparse(third_back, 3)]

    sums = butterfly(sums, across_z, (1, 2, 4))
    *owned, sums = call(
        owner_kernel,
        [struct((SEND, BLK), bf16)] * 4 + [struct((SUMS, BLK), f32)],
        [ANY] * 5 + [VMEM] * 6,
        [VMEM] * 5,
        [
            pltpu.VMEM((257 * HALF, BLK), f32),
            pltpu.SMEM((INFO,), i32),
            pltpu.SMEM((512,), i32),
        ]
        + [pltpu.SMEM((128,), i32)] * 3
        + [dma((5,))],
        flops=2 * 32 * HALF * BLK * BLK,
        moved_bytes=11000000,
        vmem=21,
    )(info, table, *requests, turned, tiles, *back, sums)
    sums = butterfly(sums, across_y, (1,))
    owned = [owned[0]] + [along_dense(owned[j], j) for j in range(1, 4)]
    keep, opposite, mine, swap, sums = call(
        split_sum_kernel,
        [struct((ROWS, BLK), bf16)] * 2
        + [struct((3 * ROWS, BLK), bf16)] * 2
        + [struct((SUMS, BLK), f32)],
        [VMEM] * 5,
        [VMEM] * 5,
        moved_bytes=5000000,
    )(*owned, sums)
    opposite = along_z(opposite, -2)
    swap = to_other_core(swap)
    first, third = (
        along_z(jnp.concatenate([ref[at : at + ROWS] for ref in (mine, swap)], axis=0), -1)
        for at in (0, 2 * ROWS)
    )
    sums = butterfly(sums, across_y, (2,))
    second, sums = call(
        relay_kernel,
        [struct((2 * ROWS, BLK), bf16), struct((SUMS, BLK), f32)],
        [VMEM] * 5,
        [VMEM] * 2,
        moved_bytes=1500000,
    )(mine, swap, third, opposite, sums)
    second = along_z(second, -2)
    sums = butterfly(sums, across_x, (1, 2))
    hold, send, sums = call(
        last_sum_kernel,
        [struct((ROWS, BLK), f32)] * 2 + [struct((SUMS, BLK), f32)],
        [SMEM] + [VMEM] * 4,
        [VMEM] * 3,
        moved_bytes=1500000,
    )(core_array, sums, keep, first, second)
    feature_grad, weight_grad, bias_grad = call(
        turn_kernel,
        [struct((NB // 2 * BLK, BLK), f32), struct((BLK, BLK), f32), struct((1, BLK), f32)],
        [SMEM] + [VMEM] * 3,
        [VMEM] * 3,
        moved_bytes=1000000,
    )(core_array, hold, to_other_core(send), sums)

    def again(state):
        return (jnp.float32(0.0),) + general_shards(
            features, weight, out_bias, edge_tiles, block_row, tile_slot, send_list, out_grad
        )

    state = (sums[BLK + 1, 0], activations, feature_grad, weight_grad, bias_grad.reshape(-1))
    return lax.while_loop(lambda state: state[0] > 0.5, again, state)[1:]


def solution(mesh):
    placed = (
        P("nodes", None),
        P(),
        P(),
        P(("nodes", "rep"), None, None),
        P(("nodes", "rep")),
        P(("nodes", "rep")),
        P(("nodes", "rep"), None),
        P("nodes", None),
    )
    return jax.shard_map(
        shards,
        mesh=mesh,
        in_specs=placed,
        out_specs=(P("nodes", "rep"), P(("nodes", "rep"), None), P(None, "rep"), P("rep")),
        check_vma=False,
    )
```

```python
import functools
import math

import jax
import jax.numpy as jnp
from jax import lax
from jax.experimental import pallas as pl
from jax.experimental.pallas import tpu as pltpu
from jax.sharding import PartitionSpec as P

ROOT_TWO_PI = 0.7978845608028654
CUBIC_TERM = 0.044715

NY, NZ, NX = 4, 8, 4
BLK = 128
HALF = 64
NB = 8
CAP = 56
ROWS = NB * HALF
MSG = ROWS + 16
PART = NZ * MSG
LOCAL = NY * PART
FAR = CAP * HALF
TILES = 128
LOC0, REM0, CNT0, OVER, ROW0 = 128, 256, 440, 444, 512
INFO = 640
SUMS = BLK + 16
SEND = 64 * HALF


def gelu_value(values):
    inner_term = ROOT_TWO_PI * (values + CUBIC_TERM * values * values * values)
    return 0.5 * values * (1.0 + jnp.tanh(inner_term))


def gelu_slope(values):
    tangent = jnp.tanh(ROOT_TWO_PI * (values + CUBIC_TERM * values * values * values))
    outer_part = 0.5 * values * (1.0 - tangent * tangent) * ROOT_TWO_PI
    return 0.5 * (1.0 + tangent) + outer_part * (1.0 + 3.0 * CUBIC_TERM * values * values)


def general_shards(features, weight, out_bias, edge_tiles, block_row, tile_slot, send_list, out_grad):
    node_count = lax.axis_size("nodes")
    rep_count = lax.axis_size("rep")
    rep_position = lax.axis_index("rep")
    block_size = edge_tiles.shape[1]
    local_blocks = features.shape[0] // block_size
    width_in = features.shape[1]
    capacity = send_list.shape[1]
    half_out = weight.shape[1] // rep_count
    feature_blocks = features.reshape(local_blocks, block_size, width_in)
    outgoing = feature_blocks[send_list]
    incoming = lax.all_to_all(outgoing, "nodes", split_axis=0, concat_axis=0, tiled=True)
    incoming = incoming.reshape(node_count * capacity, block_size, width_in)
    picked = incoming[tile_slot]
    products = jnp.einsum("tij,tjf->tif", edge_tiles, picked, preferred_element_type=jnp.float32)
    local_rows = block_row - lax.axis_index("nodes") * local_blocks
    partial_value = jax.ops.segment_sum(products, local_rows, num_segments=local_blocks)
    partial_value = partial_value.reshape(local_blocks * block_size, width_in)
    aggregate_bf = lax.psum(partial_value, "rep").astype(jnp.bfloat16)
    preact = jnp.dot(aggregate_bf, weight, preferred_element_type=jnp.float32) + out_bias
    own_preact = lax.dynamic_slice_in_dim(preact, rep_position * half_out, half_out, 1)
    activations = gelu_value(own_preact).astype(jnp.bfloat16)
    pre_grad = (out_grad.astype(jnp.float32) * gelu_slope(preact)).astype(jnp.bfloat16)
    agg_grad = lax.dot_general(
        pre_grad, weight, (((1,), (1,)), ((), ())), preferred_element_type=jnp.float32
    ).astype(jnp.bfloat16)
    grad_rows = agg_grad.reshape(local_blocks, block_size, width_in)[local_rows]
    back_products = jnp.einsum(
        "tji,tjf->tif", edge_tiles, grad_rows, preferred_element_type=jnp.float32
    )
    slot_sums = jax.ops.segment_sum(back_products, tile_slot, num_segments=node_count * capacity)
    slot_sums = slot_sums.astype(jnp.bfloat16)
    returned = lax.all_to_all(
        slot_sums.reshape(node_count, capacity, block_size, width_in),
        "nodes",
        split_axis=0,
        concat_axis=0,
        tiled=True,
    )
    returned = returned.astype(jnp.float32)
    owner_sums = jax.ops.segment_sum(
        returned.reshape(node_count * capacity, block_size, width_in),
        send_list.reshape(-1),
        num_segments=local_blocks,
    )
    feature_grad = lax.psum_scatter(
        owner_sums.reshape(local_blocks * block_size, width_in).astype(jnp.bfloat16),
        "rep",
        scatter_dimension=0,
        tiled=True,
    ).astype(jnp.float32)
    own_grad = lax.dynamic_slice_in_dim(pre_grad, rep_position * half_out, half_out, 1)
    norm_scale = 1.0 / math.sqrt(features.shape[0] * node_count)
    weight_part = lax.dot_general(
        aggregate_bf, own_grad, (((0,), (0,)), ((), ())), preferred_element_type=jnp.float32
    )
    bias_part = jnp.sum(own_grad.astype(jnp.float32), axis=0)
    weight_sum, bias_sum = lax.psum((weight_part, bias_part), "nodes")
    return (activations, feature_grad, weight_sum * norm_scale, bias_sum * norm_scale)


def device_of(y, z, x, c):
    return ((y % NY * NZ + z % NZ) * NX + x % NX) * 2 + c


def moved(value, target):
    pairs = [
        (device_of(y, z, x, c), device_of(*target(y, z, x, c)))
        for y in range(NY)
        for z in range(NZ)
        for x in range(NX)
        for c in range(2)
    ]
    return lax.ppermute(value, ("nodes", "rep"), pairs)


def along_z(value, step):
    return moved(value, lambda y, z, x, c: (y, z + step if c == 0 else z - step, x, c))


def along_dense(value, step):
    return moved(value, lambda y, z, x, c: (y + step, z, x, c) if c == 0 else (y, z, x + step, c))


def along_sparse(value, step):
    return moved(value, lambda y, z, x, c: (y, z, x + step, c) if c == 0 else (y + step, z, x, c))


def to_other_core(value):
    return moved(value, lambda y, z, x, c: (y, z, x, 1 - c))


SMEM = pl.BlockSpec(memory_space=pltpu.SMEM)
VMEM = pl.BlockSpec(memory_space=pltpu.VMEM)
ANY = pl.BlockSpec(memory_space=pl.ANY)


def call(kernel, out_shape, in_specs, out_specs, scratch=(), flops=0, moved_bytes=0, vmem=12):
    return pl.pallas_call(
        kernel,
        out_shape=out_shape,
        in_specs=in_specs,
        out_specs=out_specs,
        scratch_shapes=list(scratch),
        compiler_params=pltpu.CompilerParams(vmem_limit_bytes=vmem << 20),
        cost_estimate=pl.CostEstimate(flops=flops, bytes_accessed=moved_bytes, transcendentals=0),
    )


def struct(shape, dtype):
    return jax.ShapeDtypeStruct(shape, dtype)


def message_kernel(core_ref, features_ref, own_ref, other_ref, out_ref, half_ref):
    core = core_ref[0]
    for block in range(NB):
        turned = features_ref[block * BLK : (block + 1) * BLK, :].astype(jnp.float32).T
        mine = jnp.where(core == 0, turned[:HALF], turned[HALF:]).astype(jnp.bfloat16)
        rest = jnp.where(core == 0, turned[HALF:], turned[:HALF]).astype(jnp.bfloat16)
        out_ref[block * HALF : (block + 1) * HALF, :] = mine
        half_ref[block * HALF : (block + 1) * HALF, :] = mine
        out_ref[MSG + block * HALF : MSG + (block + 1) * HALF, :] = rest
    own, other = own_ref[1:3, :], other_ref[1:3, :]
    lists = jnp.concatenate(
        [
            jnp.where(core == 0, own, other),
            jnp.where(core == 0, other, own),
            jnp.zeros((12, BLK), jnp.int32),
        ],
        axis=0,
    )
    lists = lists.astype(jnp.float32).astype(jnp.bfloat16)
    out_ref[ROWS:MSG, :] = lists
    half_ref[ROWS:MSG, :] = lists


def plan_kernel(code_ref, rows_ref, info_ref, first_ref, second_ref, third_ref, count_ref):
    requests = (first_ref, second_ref, third_ref)
    for k in range(8):
        count_ref[k] = 0

    def clear(i, carry):
        for ref in requests:
            ref[i] = 0
        info_ref[i] = 0
        info_ref[LOC0 + i] = 0
        info_ref[REM0 + i] = 0
        info_ref[REM0 + 128 + i] = 0
        info_ref[ROW0 + i] = rows_ref[i]
        return carry

    lax.fori_loop(0, 128, clear, 0)

    def place(t, carry):
        code = code_ref[t]
        other_key = code >> 9
        key = (code >> 7) & 3
        slot = code & 127
        count_ref[4 + other_key] = count_ref[4 + other_key] + 1
        rank = count_ref[key]
        count_ref[key] = rank + 1

        @pl.when(key == 0)
        def _():
            info_ref[rank] = slot
            info_ref[LOC0 + rank] = t

        @pl.when(jnp.logical_and(key > 0, rank < CAP))
        def _():
            info_ref[REM0 + (key - 1) * CAP + rank] = t
            for k in (1, 2, 3):

                @pl.when(key == k)
                def _():
                    requests[k - 1][rank] = slot

        return carry

    lax.fori_loop(0, TILES, place, 0)
    over = 0
    info_ref[CNT0] = count_ref[0]
    for k in (1, 2, 3):
        kept = jnp.minimum(count_ref[k], CAP)
        info_ref[CNT0 + k] = kept
        requests[k - 1][64] = kept
        over += count_ref[k] - kept
        over += jnp.maximum(count_ref[4 + k] - CAP, 0)
    info_ref[OVER] = over


def start_all(pairs, sem):
    copies = [pltpu.make_async_copy(src, dst, sem.at[n]) for n, (src, dst) in enumerate(pairs)]
    for copy in copies:
        copy.start()
    return copies


def wait_all(copies):
    for copy in copies:
        copy.wait()


def half_rows(index):
    return pl.ds(pl.multiple_of(index * HALF, HALF), HALF)


def local_block(parts, slot, table, k):
    row = ((slot >> 2) & (NZ - 1)) * MSG + (table[(slot << 2) + k] << 6)
    at = pl.ds(pl.multiple_of(row, 16), HALF)
    part = slot >> 5
    low = jnp.where(part == 0, parts[0][at, :], parts[1][at, :])
    high = jnp.where(part == 2, parts[2][at, :], parts[3][at, :])
    return jnp.where(part < 2, low, high)


def pick_kernel(
    a_ref, b_ref, c_ref, d_ref, first_ref, second_ref, third_ref, table_ref, o1, o2, o3,
    q1, q2, q3, table, sem,
):
    parts = (a_ref, b_ref, c_ref, d_ref)
    wait_all(
        start_all([(first_ref, q1), (second_ref, q2), (third_ref, q3), (table_ref, table)], sem)
    )
    for k, (req, out) in enumerate(((q1, o1), (q2, o2), (q3, o3))):

        def body(i, carry, req=req, out=out, k=k):
            blocks = [local_block(parts, req[i * 8 + u], table, k + 1) for u in range(8)]
            for u in range(8):
                out[half_rows(i * 8 + u), :] = blocks[u]
            return carry

        lax.fori_loop(0, CAP // 8, body, 0)


def near_kernel(
    a_ref, b_ref, c_ref, d_ref, tiles, info_ref, table_ref, out_ref, acc, info, table, sem
):
    parts = (a_ref, b_ref, c_ref, d_ref)
    copies = start_all([(info_ref, info), (table_ref, table)], sem)
    acc[...] = jnp.zeros_like(acc)
    wait_all(copies)
    count = info[CNT0]

    def body(i, carry):
        done = []
        for u in range(8):
            p = i * 8 + u
            block = local_block(parts, info[p], table, 0)
            done.append(
                lax.dot_general(
                    block, tiles[info[LOC0 + p]], (((1,), (1,)), ((), ())),
                    preferred_element_type=jnp.float32,
                )
            )
        for u in range(8):
            p = i * 8 + u
            row = jnp.where(p < count, info[ROW0 + info[LOC0 + p]], NB)
            acc[half_rows(row), :] += done[u]
        return carry

    lax.fori_loop(0, (count + 7) >> 3, body, 0)
    out_ref[...] = acc[:ROWS, :]


def far_kernel(steps, near_ref, *refs):
    *moved_refs, tiles, info_ref, out_ref, acc, info, sem = refs
    copies = start_all([(info_ref, info)], sem)
    acc[:ROWS, :] = near_ref[...]
    acc[ROWS:, :] = jnp.zeros((HALF, BLK), jnp.float32)
    wait_all(copies)
    for k, got in zip(steps, moved_refs):
        count = info[CNT0 + k]

        def body(i, carry, k=k, got=got, count=count):
            done = []
            for u in range(8):
                p = i * 8 + u
                done.append(
                    lax.dot_general(
                        got[half_rows(p), :], tiles[info[REM0 + (k - 1) * CAP + p]],
                        (((1,), (1,)), ((), ())), preferred_element_type=jnp.float32,
                    )
                )
            for u in range(8):
                p = i * 8 + u
                row = jnp.where(p < count, info[ROW0 + info[REM0 + (k - 1) * CAP + p]], NB)
                acc[half_rows(row), :] += done[u]
            return carry

        lax.fori_loop(0, (count + 7) >> 3, body, 0)
    out_ref[...] = acc[:ROWS, :].astype(out_ref.dtype)


def products(step, tiles, turned_ref, info, out):
    first = REM0 + (step - 1) * CAP

    def body(i, carry):
        done = []
        for u in range(8):
            t = info[first + i * 8 + u]
            left = turned_ref[half_rows(info[ROW0 + t]), :]
            done.append(jnp.dot(left, tiles[t], preferred_element_type=jnp.float32))
        for u in range(8):
            out[half_rows(i * 8 + u), :] = done[u].astype(jnp.bfloat16)
        return carry

    lax.fori_loop(0, (info[CNT0 + step] + 7) >> 3, body, 0)


def middle_kernel(
    core_ref, own_agg, other_agg, weight_ref, bias_ref, grad_ref, tiles, info_ref,
    act_ref, sums_ref, turned_ref, out, info, sem,
):
    copies = start_all([(info_ref, info)], sem)
    core = core_ref[0]
    sums_ref[...] = jnp.zeros_like(sums_ref)
    weight_half = weight_ref[half_rows(core), :]

    def block_step(b, carry):
        own, other = own_agg[half_rows(b), :], other_agg[half_rows(b), :]
        low = jnp.where(core == 0, own, other)
        high = jnp.where(core == 0, other, own)
        agg = jnp.concatenate([low, high], axis=0)
        preact = lax.dot_general(
            agg, weight_ref[...], (((0,), (0,)), ((), ())), preferred_element_type=jnp.float32
        )
        preact = preact + bias_ref[...]
        tangent = jnp.tanh(ROOT_TWO_PI * (preact + CUBIC_TERM * preact * preact * preact))
        nodes = pl.ds(pl.multiple_of(b * BLK, BLK), BLK)
        value = 0.5 * preact * (1.0 + tangent)
        act_ref[nodes, :] = jnp.where(core == 0, value[:, :BLK], value[:, BLK:]).astype(jnp.bfloat16)
        outer = 0.5 * preact * (1.0 - tangent * tangent) * ROOT_TWO_PI
        slope = 0.5 * (1.0 + tangent) + outer * (1.0 + 3.0 * CUBIC_TERM * preact * preact)
        pre = (grad_ref[nodes, :].astype(jnp.float32) * slope).astype(jnp.bfloat16)
        turned_ref[half_rows(b), :] = lax.dot_general(
            weight_half, pre, (((1,), (1,)), ((), ())), preferred_element_type=jnp.float32
        ).astype(jnp.bfloat16)
        mine = jnp.where(core == 0, pre[:, :BLK], pre[:, BLK:])
        sums_ref[:BLK, :] += lax.dot_general(
            agg, mine, (((1,), (0,)), ((), ())), preferred_element_type=jnp.float32
        )
        sums_ref[BLK : BLK + 1, :] += jnp.sum(mine.astype(jnp.float32), axis=0, keepdims=True)
        return carry

    lax.fori_loop(0, NB, block_step, 0, unroll=2)
    wait_all(copies)
    over = info[OVER].astype(jnp.float32)
    sums_ref[BLK + 1 : BLK + 2, :] = jnp.full((1, BLK), over, jnp.float32)
    products(2, tiles, turned_ref, info, out)


def side_kernel(tiles, turned_ref, info_ref, o1, o3, info, sem):
    wait_all(start_all([(info_ref, info)], sem))
    products(1, tiles, turned_ref, info, o1)
    products(3, tiles, turned_ref, info, o3)


NORM = 1.0 / math.sqrt(NY * NZ * NX * NB * BLK)


def owner_kernel(
    info_ref, table_ref, first_ref, second_ref, third_ref, turned_ref, tiles,
    r1, r2, r3, sums_ref, o0, o1, o2, o3, passed_ref, total, info, table, q1, q2, q3, sem,
):
    passed_ref[...] = sums_ref[...]
    copies = start_all(
        [(info_ref, info), (table_ref, table), (first_ref, q1), (second_ref, q2), (third_ref, q3)],
        sem,
    )
    total[...] = jnp.zeros_like(total)
    wait_all(copies)

    def total_rows(slot, k, used):
        return half_rows(jnp.where(used, ((slot >> 2) << 3) + table[(slot << 2) + k], 256))

    count = info[CNT0]

    def near(i, carry):
        done = []
        for u in range(8):
            t = info[LOC0 + i * 8 + u]
            left = turned_ref[half_rows(info[ROW0 + t]), :]
            done.append(jnp.dot(left, tiles[t], preferred_element_type=jnp.float32))
        for u in range(8):
            p = i * 8 + u
            total[total_rows(info[p], 0, p < count), :] += done[u]
        return carry

    lax.fori_loop(0, (count + 7) >> 3, near, 0)
    for k, (req, got) in enumerate(((q1, r1), (q2, r2), (q3, r3))):
        kept = req[64]

        def far(i, carry, req=req, got=got, k=k, kept=kept):
            for u in range(8):
                p = i * 8 + u
                at = total_rows(req[p], k + 1, p < kept)
                total[at, :] += got[half_rows(p), :].astype(jnp.float32)
            return carry

        lax.fori_loop(0, (kept + 7) >> 3, far, 0)
    for j, out in enumerate((o0, o1, o2, o3)):
        out[...] = total[j * SEND : (j + 1) * SEND, :].astype(jnp.bfloat16)


def split_sum_kernel(
    a_ref, b_ref, c_ref, d_ref, sums_ref, keep_ref, far_ref, mine_ref, swap_ref, passed_ref
):
    passed_ref[...] = sums_ref[...]
    for m in range(NZ):
        at = slice(m * ROWS, (m + 1) * ROWS)
        value = a_ref[at, :].astype(jnp.float32) + b_ref[at, :].astype(jnp.float32)
        value = value + (c_ref[at, :].astype(jnp.float32) + d_ref[at, :].astype(jnp.float32))
        value = value.astype(jnp.bfloat16)
        if m == 0:
            keep_ref[...] = value
        elif m < 4:
            mine_ref[(m - 1) * ROWS : m * ROWS, :] = value
        elif m == 4:
            far_ref[...] = value
        else:
            swap_ref[(m - 5) * ROWS : (m - 4) * ROWS, :] = value


def relay_kernel(mine_ref, swap_ref, third_ref, far_ref, sums_ref, out_ref, passed_ref):
    passed_ref[...] = sums_ref[...]
    at = slice(ROWS, 2 * ROWS)
    own = mine_ref[at, :].astype(jnp.float32) + third_ref[:ROWS, :].astype(jnp.float32)
    out_ref[:ROWS, :] = (own + far_ref[...].astype(jnp.float32)).astype(jnp.bfloat16)
    other = swap_ref[at, :].astype(jnp.float32) + third_ref[ROWS:, :].astype(jnp.float32)
    out_ref[ROWS:, :] = other.astype(jnp.bfloat16)


def last_sum_kernel(
    core_ref, sums_ref, keep_ref, a_ref, b_ref, hold_ref, send_ref, passed_ref
):
    passed_ref[...] = sums_ref[...]
    core = core_ref[0]
    half = ROWS // 2

    def total(first):
        at = slice(first, first + half)
        value = a_ref[at, :].astype(jnp.float32) + b_ref[at, :].astype(jnp.float32)
        if first < ROWS:
            value = value + keep_ref[at, :].astype(jnp.float32)
        return value

    for n in range(2):
        low, high = total(n * ROWS), total(n * ROWS + half)
        at = slice(n * half, (n + 1) * half)
        hold_ref[at, :] = jnp.where(core == 0, low, high)
        send_ref[at, :] = jnp.where(core == 0, high, low)


def turn_kernel(core_ref, hold_ref, got_ref, sums_ref, out_ref, weight_ref, bias_ref):
    core = core_ref[0]
    half = ROWS // 2
    for b in range(NB // 2):
        first = slice(b * HALF, (b + 1) * HALF)
        second = slice(half + b * HALF, half + (b + 1) * HALF)
        own = hold_ref[first, :] + got_ref[second, :]
        other = hold_ref[second, :] + got_ref[first, :]
        both = jnp.concatenate(
            [jnp.where(core == 0, own, other), jnp.where(core == 0, other, own)], axis=0
        )
        out_ref[b * BLK : (b + 1) * BLK, :] = both.T
    weight_ref[...] = sums_ref[:BLK, :] * NORM
    bias_ref[...] = sums_ref[BLK : BLK + 1, :] * NORM


def butterfly(value, target, steps):
    for step in steps:
        value = value + moved(value, functools.partial(target, step))
    return value


def across_y(step, y, z, x, c):
    return (y ^ step, z, x, c)


def across_z(step, y, z, x, c):
    return (y, z ^ step, x, c)


def across_x(step, y, z, x, c):
    return (y, z, x ^ step, c)


def shards(features, weight, out_bias, edge_tiles, block_row, tile_slot, send_list, out_grad):
    bf16, f32, i32 = jnp.bfloat16, jnp.float32, jnp.int32
    node = lax.axis_index("nodes")
    core = lax.axis_index("rep")
    y, z, x = node // (NZ * NX), node // NX % NZ, node % NX
    core_array = jnp.reshape(core, (1,)).astype(i32)
    dma = pltpu.SemaphoreType.DMA

    own_meta = jnp.concatenate(
        [jnp.concatenate([tile_slot, block_row])[None, :], send_list.T], axis=0
    )
    other_meta = to_other_core(own_meta)
    tiles = jnp.concatenate([edge_tiles, to_other_core(edge_tiles)], axis=0)

    message, half_message = call(
        message_kernel,
        [struct((MSG + ROWS, BLK), bf16), struct((MSG, BLK), bf16)],
        [SMEM, VMEM, VMEM, VMEM],
        [VMEM] * 2,
        moved_bytes=500000,
    )(core_array, features, own_meta, other_meta)
    first, second = along_z(message, 1), along_z(message, 2)
    first, second = lax.optimization_barrier((first, second))
    across, third = along_z(second[:MSG], 2), along_z(second, 1)
    swapped = to_other_core(jnp.concatenate([first[ROWS:], second[ROWS:]], axis=0))
    swapped = [swapped[:MSG], swapped[MSG:], to_other_core(third[ROWS:])]
    column = [half_message, first[:MSG], second[:MSG], third[:MSG], across]
    for piece in swapped:
        column += [piece[MSG - ROWS :], piece[: MSG - ROWS]]
    column = jnp.concatenate(column, axis=0)

    slot = jnp.concatenate([own_meta[0, :64], other_meta[0, :64]])
    rows = jnp.concatenate([own_meta[0, 64:], other_meta[0, 64:]]) - node * NB
    source, which = slot // 2, slot % 2
    step_y = (source // (NZ * NX) - y) % NY
    step_z = (source // NX - z) % NZ
    step_x = (source - x) % NX
    dense = jnp.where(core == 0, step_y, step_x)
    sparse = jnp.where(core == 0, step_x, step_y)
    step_z = jnp.where(core == 0, (NZ - step_z) % NZ, step_z)
    step_z = jnp.where(step_z <= 4, step_z, 12 - step_z)
    holder = jnp.where(jnp.arange(TILES) < 64, core, 1 - core)
    code = (dense * 4 + sparse) * 128 + (dense * NZ + step_z) * 4 + holder * 2 + which
    info, *requests = call(
        plan_kernel,
        [struct((INFO,), i32)] + [struct((128,), i32)] * 3,
        [SMEM] * 2,
        [SMEM] * 4,
        [pltpu.SMEM((8,), i32)],
        moved_bytes=100000,
    )(code.astype(i32), rows)
    requests = [along_sparse(requests[k - 1], k) for k in (1, 2, 3)]

    column, *requests = lax.optimization_barrier((column, *requests))
    parts = [column] + [along_dense(column, -j) for j in range(1, 4)]

    away = jnp.arange(4)
    asker = jnp.where(
        core == 0,
        node - x + (x - away) % NX,
        node - y * (NZ * NX) + (y - away) % NY * (NZ * NX),
    )
    lists = jnp.stack([part.reshape(NZ, MSG, BLK)[:, ROWS : ROWS + 4] for part in parts])
    chosen = (jnp.arange(BLK)[:, None] == asker[None, :]).astype(bf16)
    table = jnp.dot(lists.reshape(4 * NZ * 4, BLK), chosen, preferred_element_type=f32)
    table = table.astype(i32).reshape(-1)

    picked = call(
        pick_kernel,
        [struct((FAR, BLK), bf16)] * 3,
        [VMEM] * 4 + [ANY] * 4,
        [VMEM] * 3,
        [pltpu.SMEM((128,), i32)] * 3 + [pltpu.SMEM((512,), i32), dma((4,))],
        moved_bytes=7000000,
    )(*parts, *requests, table)
    far = [along_sparse(picked[k - 1], -k) for k in (1, 2, 3)]

    near = call(
        near_kernel,
        struct((ROWS, BLK), f32),
        [VMEM] * 5 + [ANY] * 2,
        VMEM,
        [
            pltpu.VMEM((ROWS + HALF, BLK), f32),
            pltpu.SMEM((INFO,), i32),
            pltpu.SMEM((512,), i32),
            dma((2,)),
        ],
        flops=2 * 32 * HALF * BLK * BLK,
        moved_bytes=11000000,
    )(*parts, tiles, info, table)
    agg_half = near
    for steps, kind in (((1,), f32), ((3,), f32), ((2,), bf16)):
        agg_half = call(
            functools.partial(far_kernel, steps),
            struct((ROWS, BLK), kind),
            [VMEM] * (2 + len(steps)) + [ANY],
            VMEM,
            [pltpu.VMEM((ROWS + HALF, BLK), f32), pltpu.SMEM((INFO,), i32), dma((1,))],
            flops=2 * 32 * len(steps) * HALF * BLK * BLK,
            moved_bytes=7000000,
        )(agg_half, *[far[k - 1] for k in steps], tiles, info)
    other_half = to_other_core(agg_half)

    activations, sums, turned, second_back = call(
        middle_kernel,
        [
            struct((NB * BLK, BLK), bf16),
            struct((SUMS, BLK), f32),
            struct((ROWS, BLK), bf16),
            struct((FAR, BLK), bf16),
        ],
        [SMEM] + [VMEM] * 6 + [ANY],
        [VMEM] * 4,
        [pltpu.SMEM((INFO,), i32), dma((1,))],
        flops=2 * TILES * HALF * BLK * BLK,
        moved_bytes=8000000,
    )(
        core_array, agg_half, other_half, weight, out_bias[None, :], out_grad, tiles, info
    )
    first_back, third_back = call(
        side_kernel,
        [struct((FAR, BLK), bf16)] * 2,
        [VMEM] * 2 + [ANY],
        [VMEM] * 2,
        [pltpu.SMEM((INFO,), i32), dma((1,))],
        flops=2 * 64 * HALF * BLK * BLK,
        moved_bytes=4000000,
    )(tiles, turned, info)
    second_back = along_sparse(second_back, 2)
    back = [along_sparse(first_back, 1), second_back, along_sparse(third_back, 3)]

    sums = butterfly(sums, across_z, (1, 2, 4))
    *owned, sums = call(
        owner_kernel,
        [struct((SEND, BLK), bf16)] * 4 + [struct((SUMS, BLK), f32)],
        [ANY] * 5 + [VMEM] * 6,
        [VMEM] * 5,
        [
            pltpu.VMEM((257 * HALF, BLK), f32),
            pltpu.SMEM((INFO,), i32),
            pltpu.SMEM((512,), i32),
        ]
        + [pltpu.SMEM((128,), i32)] * 3
        + [dma((5,))],
        flops=2 * 32 * HALF * BLK * BLK,
        moved_bytes=11000000,
        vmem=21,
    )(info, table, *requests, turned, tiles, *back, sums)
    sums = butterfly(sums, across_y, (1, 2))
    owned = [owned[0]] + [along_dense(owned[j], j) for j in range(1, 4)]
    keep, opposite, mine, swap, sums = call(
        split_sum_kernel,
        [struct((ROWS, BLK), bf16)] * 2
        + [struct((3 * ROWS, BLK), bf16)] * 2
        + [struct((SUMS, BLK), f32)],
        [VMEM] * 5,
        [VMEM] * 5,
        moved_bytes=5000000,
    )(*owned, sums)
    opposite = along_z(opposite, -2)
    swap = to_other_core(swap)
    first, third = (
        along_z(jnp.concatenate([ref[at : at + ROWS] for ref in (mine, swap)], axis=0), -1)
        for at in (0, 2 * ROWS)
    )
    sums = butterfly(sums, across_x, (1,))
    second, sums = call(
        relay_kernel,
        [struct((2 * ROWS, BLK), bf16), struct((SUMS, BLK), f32)],
        [VMEM] * 5,
        [VMEM] * 2,
        moved_bytes=1500000,
    )(mine, swap, third, opposite, sums)
    second = along_z(second, -2)
    sums = butterfly(sums, across_x, (2,))
    hold, send, sums = call(
        last_sum_kernel,
        [struct((ROWS, BLK), f32)] * 2 + [struct((SUMS, BLK), f32)],
        [SMEM] + [VMEM] * 4,
        [VMEM] * 3,
        moved_bytes=1500000,
    )(core_array, sums, keep, first, second)
    feature_grad, weight_grad, bias_grad = call(
        turn_kernel,
        [struct((NB // 2 * BLK, BLK), f32), struct((BLK, BLK), f32), struct((1, BLK), f32)],
        [SMEM] + [VMEM] * 3,
        [VMEM] * 3,
        moved_bytes=1000000,
    )(core_array, hold, to_other_core(send), sums)

    def again(state):
        return (jnp.float32(0.0),) + general_shards(
            features, weight, out_bias, edge_tiles, block_row, tile_slot, send_list, out_grad
        )

    state = (sums[BLK + 1, 0], activations, feature_grad, weight_grad, bias_grad.reshape(-1))
    return lax.while_loop(lambda state: state[0] > 0.5, again, state)[1:]


def solution(mesh):
    placed = (
        P("nodes", None),
        P(),
        P(),
        P(("nodes", "rep"), None, None),
        P(("nodes", "rep")),
        P(("nodes", "rep")),
        P(("nodes", "rep"), None),
        P("nodes", None),
    )
    return jax.shard_map(
        shards,
        mesh=mesh,
        in_specs=placed,
        out_specs=(P("nodes", "rep"), P(("nodes", "rep"), None), P(None, "rep"), P("rep")),
        check_vma=False,
    )
```
